128 devices in a mesh: ctx: 8 (over z_lo, y), ep: 16 (over z_hi, x, core).
Axes of the slice: x: 4, y: 4, z: 4 (z_hi: 2, z_lo: 2; z = z_hi * 2 + z_lo), core: 2. Of those that a mesh axis runs over, the one named last changes fastest.
Arguments:
- hidden: bfloat16 [16, 1024, 1024], P('ep', 'ctx'), may hold values from -6 to 6
- doc_lengths: int32 [16, 4], P('ep'), may hold values from 1 to 958, as said below
- expert_ids: int32 [16, 1024, 8], P('ep', 'ctx'), may hold values from 0 to 31, all different within a row; in each aligned block of 64 rows (0 to 63, 64 to 127, ..., all dimensions but the last counted through in order) at most 24 rows name the same one
- attn_gain: bfloat16 [1024], P('ctx'), may hold values from 0.5 to 1.5
- w_query: bfloat16 [1024, 1024], P('ctx'), may hold values from -0.1875 to 0.1875
- key_projection: bfloat16 [1024, 512], P('ctx'), may hold values from -0.1875 to 0.1875
- w_value: bfloat16 [1024, 512], P('ctx'), may hold values from -0.1875 to 0.1875
- w_out: bfloat16 [1024, 1024], P('ctx'), may hold values from -2 to 2
- moe_gain: bfloat16 [1024], P('ctx'), may hold values from 0.5 to 1.5
- w_router: bfloat16 [32, 1024], P(None, 'ctx'), may hold values from -0.09375 to 0.09375
- w_gate: bfloat16 [32, 1024, 512], P('ep', 'ctx'), may hold values from -0.1875 to 0.1875
- w_up: bfloat16 [32, 1024, 512], P('ep', 'ctx'), may hold values from -0.1875 to 0.1875
- w_down: bfloat16 [32, 512, 1024], P('ep', None, 'ctx'), may hold values from -1 to 1
- out_grad: bfloat16 [16, 1024, 1024], P('ep', 'ctx'), may hold values from -6 to 6
Outputs:
- output: bfloat16 [16, 1024, 1024], P('ep', 'ctx')
- hidden_grad: float32 [16, 1024, 1024], P('ep', 'ctx')
- attn_gain_grad: float32 [1024], P('ctx')
- w_query_grad: float32 [1024, 1024], P('ctx')
- w_key_grad: float32 [1024, 512], P('ctx')
- w_value_grad: float32 [1024, 512], P('ctx')
- w_out_grad: float32 [1024, 1024], P('ctx')
- moe_gain_grad: float32 [1024], P('ctx')
- w_router_grad: float32 [32, 1024], P(None, 'ctx')
- w_gate_grad: float32 [32, 1024, 512], P('ep', 'ctx')
- w_up_grad: float32 [32, 1024, 512], P('ep', 'ctx')
- w_down_grad: float32 [32, 512, 1024], P('ep', None, 'ctx')
The draws below stay inside these ranges and needn't reach their ends.
Inputs may be any that keep to these rules, and one draw needn't show every extreme that they name: `doc_lengths`: each row's 4 lengths sum to 1024; the longest is the second, which starts in the row's first 128 positions and ends in its last 128. `expert_ids`: a token's 8 experts differ; within each micro-batch of one device (aligned blocks of 64 tokens of a row) no expert is named more than 24 times, a bound that some block reaches.
All inputs are finite; a program needn't handle non-finite values.
Results may differ from the reference program's by a relative error of at most 0.025.
Values may be sent and summed in bfloat16 or wider, within the bound.
No kernel may reach another device: no remote copies, remote signals or barrier semaphores. Data moves between devices by JAX's collectives and lax.ppermute only.
A program may use at most 128 MiB of HBM per device.

```python
import math
import jax
import jax.numpy as jnp
import numpy as np
from jax import lax

D = 1024
FF = 512
QUERY_HEADS = 16
KEY_VALUE_HEADS = 8
HEAD_SIZE = 64
TOP = 8
DOCS = 4
EXPERTS = 32
ROWS = 16
ROW_POSITIONS = 1024
SHARE = 128
TOK_MB = 64
CAP = 24
QW = 1024
KW = 512
QUERY_PER_KEY = 2


def draw_doc_lengths(key, part):
    key = jax.random.fold_in(key, 7)
    first_key, second_key = jax.random.split(key)
    half = SHARE // 2
    first = jax.random.randint(first_key, (ROWS,), 1, half + 1)
    remain = half + 2 - first
    third = jax.random.randint(second_key, (ROWS,), 1, remain)
    fourth = remain - third
    longest = jnp.full((ROWS,), ROW_POSITIONS - half - 2, jnp.int32)
    return jnp.stack([first, longest, third, fourth], axis=1).astype(jnp.int32)


def levels(stream_key, dims, cuts, low, top_value):
    def one(position, blocks):
        heights = jax.random.uniform(jax.random.fold_in(jax.random.fold_in(stream_key, 6), position), (blocks,), jnp.float32, low / len(cuts), top_value / len(cuts))
        return jnp.repeat(jnp.exp(heights), dims[position] // blocks).reshape((-1,) + (1,) * (len(dims) - position - 1))

    level = one(*cuts[0])
    for cut in cuts[1:]:
        level = level * one(*cut)
    return level


def deal_out(rng, own, number, rows, number_of, top, bound, skew):
    order = jax.random.permutation(rng, number_of)
    packed, common = load_shares(number_of, rows * top, bound, skew, True), load_shares(number_of, rows * top, bound, skew, False)
    places = jnp.arange(number_of)

    def named(sizes, rotation):
        used = int((sizes > 0).sum())
        fixed = max(1, used // 4)
        shifted = fixed + (places - fixed + rotation * (used - fixed)) % max(1, number_of - fixed)
        return jnp.zeros((number_of,), jnp.int32).at[order[jnp.where(places < fixed, places, shifted)]].set(jnp.asarray(sizes, jnp.int32))

    sizes = jnp.where(number % 4 == 0, named(packed, number // 4), named(common, number - number // 4 - 1))
    mixed = jax.random.permutation(jax.random.fold_in(own, 3), number_of)
    giver, taker = mixed[0:number_of // 2 * 2:2], mixed[1:number_of // 2 * 2:2]
    room = jnp.minimum(sizes[giver] - 1, bound - sizes[taker]) // 2
    room = jnp.where((giver == order[0]) | (taker == order[0]) | (sizes[taker] == 0), 0, jnp.maximum(room, 0))
    shifted = jax.random.randint(jax.random.fold_in(own, 4), (number_of // 2,), 0, 1 << 20) % (room + 1)
    sizes = sizes.at[giver].add(-shifted).at[taker].add(shifted)
    labels = jnp.searchsorted(jnp.cumsum(sizes), jnp.arange(rows * top), side="right").astype(jnp.int32)
    grid = labels.reshape(top, rows).T
    grid = grid[jax.random.permutation(jax.random.fold_in(own, 1), rows)]
    rotation = jax.random.randint(jax.random.fold_in(own, 2), (rows, 1), 0, top)
    return jnp.take_along_axis(grid, (jnp.arange(top)[None, :] + rotation) % top, axis=1)


def load_shares(amount, total, limit, skew, full):
    loads = [(1 << 20) // math.isqrt(grade ** skew) + 1 for grade in range(1, amount + 1)]
    largest = limit if full else min(limit, max(-(-total // amount), total * loads[0] // sum(loads)))
    least = 1 if total - largest >= amount - 1 else 0
    counts, rest = [largest] + [least] * (amount - 1), total - largest - least * (amount - 1)
    while rest > 0:
        movable = [i for i in range(1, amount) if counts[i] < largest] or [i for i in range(1, amount) if counts[i] < limit]
        whole, left = sum([loads[i] for i in movable]), rest
        for i in movable:
            more = min(limit - counts[i], max(1, left * loads[i] // whole), rest)
            counts[i] = counts[i] + more
            rest = rest - more
    return np.array(counts)


def scatter_about(stream_key, extent, scale, limit, shards=(), kind=jnp.bfloat16):
    values = jax.random.normal(stream_key, extent, jnp.float32) * scale
    if len(shards) > 0:
        values = levels(stream_key, extent, shards, -0.22, 0.18) * values
    return jnp.clip(values, min=-limit, max=limit).astype(kind)


def setup_inputs(seed: int = 0) -> dict:
    arg_keys = jax.random.split(jax.random.key(seed), 15)
    hidden = scatter_about(arg_keys[0], (ROWS, ROW_POSITIONS, D), 1.0, 6.0, ((0, 16), (1, 8)))
    doc_lengths = draw_doc_lengths(jax.random.fold_in(arg_keys[14], 71), 0)
    expert_ids_keys = jax.random.split(jax.random.fold_in(arg_keys[2], 1), ROWS * ROW_POSITIONS // TOK_MB)
    expert_ids_turns = jax.random.permutation(jax.random.fold_in(arg_keys[2], 3), ROWS * ROW_POSITIONS // TOK_MB)
    expert_ids = jax.vmap(lambda own, number: deal_out(jax.random.fold_in(arg_keys[2], 2), own, number, TOK_MB, EXPERTS, TOP, CAP, 1))(expert_ids_keys, expert_ids_turns).reshape((ROWS, ROW_POSITIONS, TOP))
    attn_gain = jnp.clip(1.0 + 0.1 * jax.random.normal(arg_keys[3], (D,), jnp.float32), 0.5, 1.5).astype(jnp.bfloat16)
    w_query = scatter_about(arg_keys[4], (D, QW), D ** -0.5, 0.1875, ((0, 8),))
    key_projection = scatter_about(arg_keys[5], (D, KW), D ** -0.5, 0.1875, ((0, 8),))
    w_value = scatter_about(arg_keys[6], (D, KW), D ** -0.5, 0.1875, ((0, 8),))
    w_out = scatter_about(arg_keys[7], (QW, D), (max(1, QW * 8 // ROW_POSITIONS)) ** -0.5, 2.0, ((0, 8),))
    moe_gain = jnp.clip(1.0 + 0.1 * jax.random.normal(arg_keys[8], (D,), jnp.float32), 0.5, 1.5).astype(jnp.bfloat16)
    w_router = scatter_about(arg_keys[9], (EXPERTS, D), (4 * D) ** -0.5, 0.09375, ((1, 8),))
    w_gate = scatter_about(arg_keys[10], (EXPERTS, D, FF), D ** -0.5, 0.1875, ((0, 16), (1, 8)))
    w_up = scatter_about(arg_keys[11], (EXPERTS, D, FF), D ** -0.5, 0.1875, ((0, 16), (1, 8)))
    w_down = scatter_about(arg_keys[12], (EXPERTS, FF, D), (FF // 16) ** -0.5, 1.0, ((0, 16), (2, 8)))
    out_grad = scatter_about(arg_keys[13], (ROWS, ROW_POSITIONS, D), 1.0, 6.0, ((0, 16), (1, 8)))
    return {"hidden": hidden, "doc_lengths": doc_lengths, "expert_ids": expert_ids, "attn_gain": attn_gain, "w_query": w_query, "key_projection": key_projection, "w_value": w_value, "w_out": w_out, "moe_gain": moe_gain, "w_router": w_router, "w_gate": w_gate, "w_up": w_up, "w_down": w_down, "out_grad": out_grad}


EPS = 1e-05
THETA = 10000.0
MASKED = -1e+30
PRECISE = lax.Precision.HIGHEST

@jax.custom_vjp
def lower_precision(v):
    return lax.optimization_barrier(v.astype(jnp.bfloat16)).astype(jnp.float32)

@jax.custom_vjp
def lower_backward(v):
    return v

def low_keep(v):
    return (lower_precision(v), None)

def low_pass(kept, grad):
    return (grad,)

def back_keep(v):
    return (v, None)

def back_low(kept, grad):
    return (lower_precision(grad),)
lower_precision.defvjp(low_keep, low_pass)
lower_backward.defvjp(back_keep, back_low)

def matrix_product(left, right):
    return jnp.dot(left, right, precision=PRECISE, preferred_element_type=jnp.float32)

def normalize(value_vectors, gain):
    return value_vectors * lax.rsqrt(lax.optimization_barrier(jnp.mean(value_vectors * value_vectors, axis=-1, keepdims=True)) + EPS) * gain

def rotate_halves(value_vectors, heads, cosine_table, sine_table):
    shaped = value_vectors.reshape(value_vectors.shape[0], heads, HEAD_SIZE)
    first = shaped[..., :HEAD_SIZE // 2]
    second = shaped[..., HEAD_SIZE // 2:]
    cos_part = cosine_table[:, None, :]
    sin_part = sine_table[:, None, :]
    turned = jnp.concatenate([first * cos_part - second * sin_part, second * cos_part + first * sin_part], axis=-1)
    return turned.reshape(value_vectors.shape[0], heads * HEAD_SIZE)

def row_layout(lengths_row, routes_row):
    ends = jnp.cumsum(lengths_row)
    starts = ends - lengths_row
    places = jnp.arange(ROW_POSITIONS, dtype=jnp.int32)
    segment = lax.optimization_barrier(jnp.sum((places[:, None] >= ends[None, :]).astype(jnp.int32), axis=1))
    picks = (segment[:, None] == jnp.arange(DOCS, dtype=jnp.int32)[None, :]).astype(jnp.int32)
    offset = places - lax.optimization_barrier(jnp.sum(picks * starts[None, :], axis=1))
    freq = THETA ** (-(jnp.arange(HEAD_SIZE // 2, dtype=jnp.float32) * 2.0 / HEAD_SIZE))
    angle = offset.astype(jnp.float32)[:, None] * freq[None, :]
    flat = routes_row.reshape(-1)
    table = (flat[:, None] == jnp.arange(EXPERTS, dtype=jnp.int32)[None, :]).astype(jnp.int32)
    table = table.reshape(ROW_POSITIONS // TOK_MB, TOK_MB * TOP, EXPERTS)
    before = jnp.cumsum(table, axis=1) - table
    ranking = lax.optimization_barrier(jnp.sum(before * table, axis=2))
    offsets = jnp.arange(ROW_POSITIONS // TOK_MB, dtype=jnp.int32)[:, None] * CAP
    slots = (ranking + offsets).reshape(ROW_POSITIONS, TOP).astype(jnp.int32)
    return (segment, jnp.cos(angle), jnp.sin(angle), slots)

def forward(hidden, weights, segment, cosine_table, sine_table, routes, slots):
    attn_gain, w_query, key_projection, w_value, w_out, moe_gain, w_router, w_gate, w_up, w_down = weights
    normalized = lower_precision(normalize(hidden, attn_gain))
    query_vectors = lower_precision(rotate_halves(lower_backward(matrix_product(normalized, w_query)), QUERY_HEADS, cosine_table, sine_table))
    key = lower_precision(rotate_halves(lower_backward(matrix_product(normalized, key_projection)), KEY_VALUE_HEADS, cosine_table, sine_table))
    value_vectors = lower_precision(lower_backward(matrix_product(normalized, w_value)))
    heads_of_queries = query_vectors.reshape(ROW_POSITIONS, KEY_VALUE_HEADS, QUERY_PER_KEY, HEAD_SIZE)
    heads_of_keys = key.reshape(ROW_POSITIONS, KEY_VALUE_HEADS, HEAD_SIZE)
    heads_of_values = value_vectors.reshape(ROW_POSITIONS, KEY_VALUE_HEADS, HEAD_SIZE)
    block_rows = min(512, ROW_POSITIONS)
    places = jnp.arange(ROW_POSITIONS, dtype=jnp.int32)
    score_scale = HEAD_SIZE ** (-0.5)

    def attend(block):
        start = block * block_rows
        query_block = lax.dynamic_slice_in_dim(heads_of_queries, start, block_rows, 0)
        query_seg = lax.dynamic_slice_in_dim(segment, start, block_rows, 0)
        query_place = start + jnp.arange(block_rows, dtype=jnp.int32)
        allowed = (query_seg[:, None] == segment[None, :]) & (query_place[:, None] >= places[None, :])
        raw = lower_backward(jnp.einsum('tgjd,sgd->gjts', query_block, heads_of_keys, precision=PRECISE))
        scores = jnp.where(allowed, raw * score_scale, MASKED)
        highest = lax.optimization_barrier(jnp.max(scores, axis=-1, keepdims=True))
        weight = jnp.where(allowed, jnp.exp(scores - highest), 0.0)
        probs = lower_precision(weight / lax.optimization_barrier(jnp.sum(weight, axis=-1, keepdims=True)))
        return jnp.einsum('gjts,sgd->tgjd', probs, heads_of_values, precision=PRECISE)
    mixed = lax.map(jax.checkpoint(attend), jnp.arange(ROW_POSITIONS // block_rows, dtype=jnp.int32))
    mixed = lower_precision(lower_backward(mixed.reshape(ROW_POSITIONS, QW)))
    branch = lower_backward(matrix_product(mixed, w_out))
    middle = hidden + branch
    routed = lower_precision(normalize(middle, moe_gain))
    logits = lower_backward(jnp.dot(routed, w_router.T, precision=PRECISE, preferred_element_type=jnp.float32))
    chosen = jnp.take_along_axis(logits, routes, axis=1)
    gates = jax.nn.softmax(chosen, axis=-1)
    spread = jnp.broadcast_to(routed[:, None, :], (ROW_POSITIONS, TOP, D))
    sent = jnp.zeros((EXPERTS, ROW_POSITIONS // TOK_MB * CAP, D), jnp.float32).at[routes, slots].set(spread)
    sent = lower_backward(sent)
    gate_part = lower_backward(jnp.einsum('esd,edf->esf', sent, w_gate, precision=PRECISE))
    up_part = lower_backward(jnp.einsum('esd,edf->esf', sent, w_up, precision=PRECISE))
    inner = lower_precision(jax.nn.silu(gate_part) * up_part)
    returned = lower_precision(lower_backward(jnp.einsum('esf,efd->esd', inner, w_down, precision=PRECISE)))
    picked = returned[routes, slots]
    return middle + lax.optimization_barrier(jnp.sum(gates[:, :, None] * picked, axis=1))

def reference(hidden, doc_lengths, expert_ids, attn_gain, w_query, key_projection, w_value, w_out, moe_gain, w_router, w_gate, w_up, w_down, out_grad):
    weights = tuple((item.astype(jnp.float32) for item in (attn_gain, w_query, key_projection, w_value, w_out, moe_gain, w_router, w_gate, w_up, w_down)))

    def one_row(totals, items):
        row_hidden, row_grad, row_lengths, row_routes = items
        segment, cosine_table, sine_table, slots = row_layout(row_lengths, row_routes)

        def apply(values, params):
            return forward(values, params, segment, cosine_table, sine_table, row_routes, slots)
        result, pullback = jax.vjp(apply, row_hidden.astype(jnp.float32), weights)
        grad_hidden, grad_weights = pullback(row_grad.astype(jnp.float32))
        totals = jax.tree.map(lambda left, right: left + right, totals, grad_weights)
        return (totals, (result.astype(jnp.bfloat16), grad_hidden))
    zeros = jax.tree.map(jnp.zeros_like, weights)
    totals, outputs = lax.scan(one_row, zeros, (hidden, out_grad, doc_lengths, expert_ids))
    return (outputs[0], outputs[1], totals[0], totals[1], totals[2], totals[3], totals[4], totals[5], totals[6], totals[7], totals[8], totals[9])
```

```python
import jax
import jax.numpy as jnp
from jax import lax
from jax.experimental import pallas as pl
from jax.experimental.pallas import tpu as pltpu
from jax.sharding import Mesh, PartitionSpec as P

EPS = 1e-05
THETA = 10000.0
MASKED = -1e30
HEAD = 64
SCALE = 0.125
TILE = 256
CHOSEN_PER_PART = 48
F32 = jnp.float32
BF16 = jnp.bfloat16
EP = ("chip", "core")
NT = (((1,), (1,)), ((), ()))
TN = (((0,), (0,)), ((), ()))


def exchange(parts, axis):
    return lax.all_to_all(parts, axis, split_axis=0, concat_axis=0, tiled=True)


def spread(block, axis, count):
    return exchange(jnp.broadcast_to(block[None], (count,) + block.shape), axis)


def swap_cores(block):
    return lax.ppermute(block, "core", [(0, 1), (1, 0)])


def dot(left, right, dims=(((1,), (0,)), ((), ()))):
    return lax.dot_general(left, right, dims, preferred_element_type=F32)


def turn(block, cosine, sine):
    lane = lax.broadcasted_iota(jnp.int32, block.shape, 1)
    other = jnp.where(lane % HEAD < HEAD // 2, pltpu.roll(block, 96, 1), pltpu.roll(block, 32, 1))
    return block * cosine + other * sine


def attend_kernel(
    hidden_ref, weight_ref, gain_ref, cos_ref, sin_ref, first_ref,
    normed_ref, query_ref, key_ref, value_ref, mixed_ref,
):
    count = hidden_ref.shape[0]
    lane = lax.broadcasted_iota(jnp.int32, (TILE, 128), 1)
    low = lane < HEAD
    for tile in range(count // TILE):
        rows = slice(tile * TILE, (tile + 1) * TILE)
        x = hidden_ref[rows, :].astype(F32)
        rho = lax.rsqrt(jnp.mean(x * x, axis=-1, keepdims=True) + EPS)
        normed = (x * rho * gain_ref[...]).astype(BF16)
        normed_ref[rows, :] = normed
        projected = dot(normed, weight_ref[...])
        cosine, sine = cos_ref[rows, :], sin_ref[rows, :]
        query = turn(projected[:, :128], cosine, sine).astype(BF16)
        pair = projected[:, 128:]
        turned = pltpu.roll(pair, HEAD, 1)
        key_ref[rows, :] = turn(jnp.where(low, pair, turned), cosine, sine).astype(BF16)
        value_ref[rows, :] = jnp.where(low, turned, pair).astype(BF16)
        query_ref[rows, :] = query
        seen = (tile + 1) * TILE
        keys, values = key_ref[:seen, :], value_ref[:seen, :]
        place = tile * TILE + lax.broadcasted_iota(jnp.int32, (TILE, seen), 0)
        source = lax.broadcasted_iota(jnp.int32, (TILE, seen), 1)
        allowed = (source <= place) & (source >= first_ref[rows, :])
        scaled = query * jnp.asarray(SCALE, BF16)
        mixed = []
        for head in range(2):
            one = jnp.where(low == (head == 0), scaled, jnp.zeros_like(scaled))
            scores = jnp.where(allowed, dot(one, keys, NT), MASKED)
            weight = jnp.exp(scores - jnp.max(scores, axis=1, keepdims=True))
            probs = weight * (1.0 / jnp.sum(weight, axis=1, keepdims=True))
            mixed.append(dot(probs.astype(BF16), values))
        mixed_ref[rows, :] = jnp.where(low, mixed[0], mixed[1]).astype(BF16)


def attend_back_kernel(
    query_ref, key_ref, value_ref, d_mixed_ref, first_ref, cos_ref, sin_ref, normed_ref, weight_ref,
    grad_ref, d_normed_ref, key_sum, value_sum, pre_ref,
):
    count = query_ref.shape[0]
    lane = lax.broadcasted_iota(jnp.int32, (TILE, 128), 1)
    low = lane < HEAD
    key_sum[...] = jnp.zeros_like(key_sum)
    value_sum[...] = jnp.zeros_like(value_sum)
    for tile in range(count // TILE):
        rows = slice(tile * TILE, (tile + 1) * TILE)
        seen = (tile + 1) * TILE
        keys, values = key_ref[:seen, :], value_ref[:seen, :]
        place = tile * TILE + lax.broadcasted_iota(jnp.int32, (seen, TILE), 1)
        source = lax.broadcasted_iota(jnp.int32, (seen, TILE), 0)
        allowed = (source <= place) & (source >= first_ref[:, rows])
        scaled = query_ref[rows, :] * jnp.asarray(SCALE, BF16)
        d_mixed = d_mixed_ref[rows, :]
        d_query = []
        for head in range(2):
            mine = low == (head == 0)
            one = jnp.where(mine, scaled, jnp.zeros_like(scaled))
            d_one = jnp.where(mine, d_mixed, jnp.zeros_like(d_mixed))
            scores = jnp.where(allowed, dot(keys, one, NT), MASKED)
            weight = jnp.exp(scores - jnp.max(scores, axis=0, keepdims=True))
            probs = weight * (1.0 / jnp.sum(weight, axis=0, keepdims=True))
            d_probs = dot(values, d_one, NT)
            delta = jnp.sum(probs * d_probs, axis=0, keepdims=True)
            d_scores = (probs * (d_probs - delta)).astype(BF16)
            key_sum[:seen, :] += dot(d_scores, one)
            value_sum[:seen, :] += dot(probs.astype(BF16), d_one)
            d_query.append(dot(d_scores, keys, TN) * SCALE)
        d_query = jnp.where(low, d_query[0], d_query[1])
        pre_ref[rows, :128] = turn(d_query, cos_ref[rows, :], -sin_ref[rows, :]).astype(BF16)
    for tile in range(count // TILE):
        rows = slice(tile * TILE, (tile + 1) * TILE)
        d_key, d_value = key_sum[rows, :], value_sum[rows, :]
        d_key = turn(d_key + pltpu.roll(d_key, HEAD, 1), cos_ref[rows, :], -sin_ref[rows, :])
        d_value = d_value + pltpu.roll(d_value, HEAD, 1)
        pre_ref[rows, 128:] = jnp.where(low, d_key, d_value).astype(BF16)
        d_normed_ref[rows, :] = dot(pre_ref[rows, :], weight_ref[...], NT).astype(BF16)
    grad_ref[...] = dot(normed_ref[...], pre_ref[...], TN).astype(BF16)


def kernel_call(kernel, outs, scratch, flops):
    return pl.pallas_call(
        kernel,
        out_shape=[jax.ShapeDtypeStruct(shape, kind) for shape, kind in outs],
        scratch_shapes=scratch,
        compiler_params=pltpu.CompilerParams(vmem_limit_bytes=40 * 1024 * 1024),
        cost_estimate=pl.CostEstimate(flops=flops, bytes_accessed=8_000_000, transcendentals=0),
    )


def split_wide(values):
    high = values.astype(BF16)
    rest = values - high.astype(F32)
    middle = rest.astype(BF16)
    return high, middle, (rest - middle.astype(F32)).astype(BF16)


def on_device(
    hidden, doc_lengths, expert_ids, attn_gain, w_query, key_projection, w_value, w_out,
    moe_gain, w_router, w_gate, w_up, w_down, out_grad,
):
    share, width = hidden.shape[1], hidden.shape[2]
    ctx, chips = lax.axis_size("ctx"), lax.axis_size("chip")
    peers = 2 * chips
    row = share * ctx
    experts = w_router.shape[0]
    local, inner_width = w_gate.shape[0], w_gate.shape[2]
    me = lax.axis_index("chip") * 2 + lax.axis_index("core")

    packed = jnp.concatenate(
        [part for e in range(local) for part in (w_gate[e], w_up[e], w_down[e].T)], axis=1
    )
    expert_weights = lax.all_gather(packed, "ctx", axis=0, tiled=True)

    everything = spread(hidden[0], "ctx", ctx).reshape(row, width)
    query_cols = w_query.reshape(share, ctx, 128).transpose(1, 0, 2)
    pair_cols = jnp.concatenate(
        [key_projection.reshape(share, ctx, HEAD), w_value.reshape(share, ctx, HEAD)], axis=2
    ).transpose(1, 0, 2)
    small = jnp.concatenate(
        [attn_gain[None], moe_gain[None], w_router, jnp.zeros((14, 128), BF16)], axis=0
    )
    sent = jnp.concatenate(
        [query_cols, pair_cols, jnp.broadcast_to(small[None], (ctx,) + small.shape)], axis=1
    )
    got = exchange(sent, "ctx")
    weight = jnp.concatenate([got[:, :128], got[:, 128:256]], axis=2).reshape(width, 256)
    gain_a = got[:, 256].reshape(1, width).astype(F32)
    gain_m = got[:, 257].reshape(1, width).astype(F32)
    router = got[:, 258 : 258 + experts].transpose(1, 0, 2).reshape(experts, width)

    routes = expert_ids[0]
    expert_index = jnp.arange(experts, dtype=jnp.int32)
    chosen = jnp.any(routes[:, :, None] == expert_index[None, None, :], axis=1)
    pad = jnp.zeros((share, 128 - experts), BF16)
    grad_rows = jnp.concatenate([out_grad[0], chosen.astype(BF16), pad], axis=1)
    grads_mine = spread(grad_rows, "chip", chips)
    grads_all = jnp.concatenate([grads_mine, swap_cores(grads_mine)], axis=0)
    out_weight = spread(w_out, "ctx", ctx).reshape(row, width)

    lengths = doc_lengths[0]
    ends = jnp.cumsum(lengths)
    places = jnp.arange(row, dtype=jnp.int32)
    segment = jnp.sum((places[:, None] >= ends[None, :]).astype(jnp.int32), axis=1)
    picks = segment[:, None] == jnp.arange(lengths.shape[0], dtype=jnp.int32)[None, :]
    first = jnp.sum(jnp.where(picks, (ends - lengths)[None, :], 0), axis=1)
    freq = THETA ** (-(jnp.arange(HEAD // 2, dtype=F32) * 2.0 / HEAD))
    angle = (places - first).astype(F32)[:, None] * freq[None, :]
    cosine, sine = jnp.cos(angle), jnp.sin(angle)
    cosine = jnp.concatenate([cosine] * 4, axis=1)
    sine = jnp.concatenate([-sine, sine, -sine, sine], axis=1)

    normed, query, key, value, mixed = kernel_call(
        attend_kernel,
        [((row, width), BF16)] + [((row, 128), BF16)] * 4,
        [],
        1_500_000_000,
    )(everything, weight, gain_a, cosine, sine, first[:, None])

    mixed_rows = exchange(mixed.reshape(ctx, share, 128), "ctx")
    mixed_rows = mixed_rows.transpose(1, 0, 2).reshape(share, row)
    residual = hidden[0].astype(F32)
    middle = residual + dot(mixed_rows, out_weight)
    rho_m = lax.rsqrt(jnp.mean(middle * middle, axis=-1, keepdims=True) + EPS)
    unit_m = middle * rho_m
    routed = (unit_m * gain_m).astype(BF16)
    logits = dot(routed, router, NT)
    logits = jnp.where(chosen, logits, MASKED)
    raised = jnp.exp(logits - jnp.max(logits, axis=1, keepdims=True))
    gates = raised / jnp.sum(raised, axis=1, keepdims=True)
    tokens = jnp.concatenate([routed, *split_wide(gates), jnp.zeros((share, 128 - 3 * experts), BF16)], axis=1)
    tokens_mine = spread(tokens, "chip", chips)
    tokens_all = jnp.concatenate([tokens_mine, swap_cores(tokens_mine)], axis=0)

    flags = grads_all[:, :, width : width + experts]
    before = (jnp.arange(share)[:, None] < jnp.arange(share)[None, :]).astype(BF16)
    route_sums, out_sums, expert_grads = [], [], []
    lane = jnp.arange(128, dtype=jnp.int32)
    slot_index = jnp.arange(CHOSEN_PER_PART, dtype=F32)
    for e in range(local):
        expert = me * local + e
        named = jnp.sum(
            jnp.where(expert_index[None, None, :] == expert, flags, jnp.zeros_like(flags)).astype(F32), axis=2
        )
        rank = dot(named.astype(BF16), before)
        pick = (
            (named[:, None, :] > 0.5) & (rank[:, None, :] == slot_index[None, :, None])
        ).astype(BF16)
        gather = (((2,), (1,)), ((0,), (0,)))
        rows = dot(pick, tokens_all, gather).astype(BF16).reshape(peers * CHOSEN_PER_PART, -1)
        cotangent = dot(pick, grads_all[:, :, :width], gather).astype(BF16).reshape(peers * CHOSEN_PER_PART, width)
        mine = (lane % experts == expert) & (lane < 3 * experts)
        gate = jnp.sum(jnp.where(mine[None, :], rows[:, width:].astype(F32), 0.0), axis=1, keepdims=True)
        rows = rows[:, :width]
        base = e * 3 * inner_width
        gate_up = expert_weights[:, base : base + 2 * inner_width]
        down = expert_weights[:, base + 2 * inner_width : base + 3 * inner_width]
        both = dot(rows, gate_up)
        a, b = both[:, :inner_width], both[:, inner_width:]
        sigma = jax.nn.sigmoid(a)
        inner = (a * sigma * b).astype(BF16)
        result = dot(inner, down, NT).astype(BF16)
        gate_grad = jnp.sum(cotangent.astype(F32) * result.astype(F32), axis=1, keepdims=True)
        d_result = (gate * cotangent.astype(F32)).astype(BF16)
        d_inner = dot(d_result, down)
        d_a = (d_inner * b * sigma * (1.0 + a * (1.0 - sigma))).astype(BF16)
        d_b = (d_inner * a * sigma).astype(BF16)
        d_both = jnp.concatenate([d_a, d_b], axis=1)
        d_rows = dot(d_both, gate_up, NT).astype(BF16)
        high, low, unused = split_wide(gate_grad)
        tail = jnp.where(lane[None, :] == expert, high, jnp.zeros_like(high)) + jnp.where(
            lane[None, :] == expert + experts, low, jnp.zeros_like(low)
        )
        back = jnp.concatenate([d_rows, tail.astype(BF16)], axis=1).reshape(peers, CHOSEN_PER_PART, -1)
        scatter = (((1,), (1,)), ((0,), (0,)))
        route_sums.append(dot(pick, back, scatter))
        gated = (gate * result.astype(F32)).astype(BF16).reshape(peers, CHOSEN_PER_PART, width)
        out_sums.append(dot(pick, gated, scatter))
        expert_grads.append(dot(rows, d_both, TN).astype(BF16))
        expert_grads.append(dot(d_result, inner, TN).astype(BF16))
    expert_grads = jnp.concatenate(expert_grads, axis=1)

    def send_home(sums):
        total = sums[0] + sums[1]
        passed = swap_cores(total[chips:].astype(BF16)).astype(F32)
        return exchange((total[:chips] + passed).astype(BF16), "chip")

    route_home = jnp.sum(send_home(route_sums).astype(F32), axis=0)
    d_routed = route_home[:, :width]
    d_gates = route_home[:, width : width + experts] + route_home[:, width + experts : width + 2 * experts]
    d_logits = (gates * (d_gates - jnp.sum(gates * d_gates, axis=1, keepdims=True))).astype(BF16)
    d_routed = d_routed + dot(d_logits, router)
    cotangent = out_grad[0].astype(F32)
    moe_gain_part = jnp.sum(d_routed * unit_m, axis=0, keepdims=True)
    c = d_routed * gain_m
    d_middle = cotangent + rho_m * (c - unit_m * jnp.mean(c * unit_m, axis=-1, keepdims=True))
    d_branch = d_middle.astype(BF16)
    router_part = dot(d_logits, routed, TN)
    d_mixed = dot(d_branch, out_weight, NT).astype(BF16)
    d_mixed = exchange(d_mixed.reshape(share, ctx, 128).transpose(1, 0, 2), "ctx").reshape(row, 128)

    expert_sums = lax.psum_scatter(expert_grads, "ctx", scatter_dimension=0, tiled=True)
    output = (middle + jnp.sum(send_home(out_sums).astype(F32), axis=0)).astype(BF16)

    branch_all = spread(d_branch, "ctx", ctx).reshape(row, width)
    out_part = dot(mixed, branch_all, TN).astype(BF16)
    out_sum = jnp.sum(exchange(out_part.reshape(peers, 128 // peers, width), EP).astype(F32), axis=0)

    projection_part, d_normed_part = kernel_call(
        attend_back_kernel,
        [((width, 256), BF16), ((row, width), BF16)],
        [pltpu.VMEM((row, 128), F32), pltpu.VMEM((row, 128), F32), pltpu.VMEM((row, 256), BF16)],
        4_000_000_000,
    )(query, key, value, d_mixed, first[None, :], cosine, sine, normed, weight)

    piece = 128 // peers
    kinds = experts // peers
    router_send = router_part.astype(BF16).reshape(peers, kinds, ctx, 128).transpose(2, 0, 1, 3)
    gain_send = jnp.broadcast_to(moe_gain_part.astype(BF16).reshape(ctx, 1, 1, 128), (ctx, peers, 1, 128))
    small_send = jnp.concatenate(
        [router_send, gain_send, jnp.zeros((ctx, peers, piece - kinds - 1, 128), BF16)], axis=2
    )
    bundle = jnp.concatenate(
        [projection_part.reshape(ctx, peers, piece, 256), small_send], axis=3
    ).reshape(ctx * peers, piece, 384)
    bundle = exchange(bundle, ("ctx",) + EP).reshape(ctx, peers, piece, 384).astype(F32)
    summed = jnp.sum(bundle, axis=1)
    d_normed = jnp.sum(exchange(d_normed_part.reshape(ctx, share, width), "ctx").astype(F32), axis=0)
    small_sum = jnp.sum(summed[:, :, 256:], axis=0)
    final = jnp.concatenate(
        [
            summed[:, :, :128].transpose(1, 0, 2).reshape(piece, width),
            summed[:, :, 128:192].transpose(1, 0, 2).reshape(piece, width // 2),
            summed[:, :, 192:256].transpose(1, 0, 2).reshape(piece, width // 2),
            out_sum,
            small_sum,
        ],
        axis=1,
    ).astype(BF16)
    final = spread(final, EP, peers).astype(F32)
    rows_of = final.reshape(peers * piece, -1)
    query_grad, key_grad = rows_of[:, :width], rows_of[:, width : width + width // 2]
    value_grad = rows_of[:, width + width // 2 : 2 * width]
    out_weight_grad = rows_of[:, 2 * width : 3 * width]
    router_grad = final[:, :kinds, 3 * width :].reshape(experts, 128)
    moe_gain_grad = small_sum[kinds]
    attn_gain_grad = (
        jnp.sum(w_query.astype(F32) * query_grad, axis=1)
        + jnp.sum(key_projection.astype(F32) * key_grad, axis=1)
        + jnp.sum(w_value.astype(F32) * value_grad, axis=1)
    ) / attn_gain.astype(F32)

    rho_a = lax.rsqrt(jnp.mean(residual * residual, axis=-1, keepdims=True) + EPS)
    unit_a = residual * rho_a
    c = d_normed * gain_a
    hidden_grad = d_middle + rho_a * (c - unit_a * jnp.mean(c * unit_a, axis=-1, keepdims=True))

    expert_sums = expert_sums.astype(F32).reshape(128, local, 3, inner_width)
    gate_sum, up_sum = (expert_sums[:, :, k].transpose(1, 0, 2) for k in range(2))
    down_sum = expert_sums[:, :, 2].transpose(1, 2, 0)
    return (
        output[None], hidden_grad[None], attn_gain_grad, query_grad, key_grad, value_grad,
        out_weight_grad, moe_gain_grad, router_grad, gate_sum, up_sum, down_sum,
    )


def solution(mesh):
    sizes = dict(mesh.shape)
    inner = Mesh(
        mesh.devices.reshape(sizes["ctx"], sizes["ep"] // 2, 2), ("ctx", "chip", "core")
    )
    in_specs = (
        P(EP, "ctx", None), P(EP, None), P(EP, "ctx", None), P("ctx"), P("ctx", None), P("ctx", None),
        P("ctx", None), P("ctx", None), P("ctx"), P(None, "ctx"), P(EP, "ctx", None), P(EP, "ctx", None),
        P(EP, None, "ctx"), P(EP, "ctx", None),
    )
    out_specs = (
        P(EP, "ctx", None), P(EP, "ctx", None), P("ctx"), P("ctx", None), P("ctx", None), P("ctx", None),
        P("ctx", None), P("ctx"), P(None, "ctx"), P(EP, "ctx", None), P(EP, "ctx", None), P(EP, None, "ctx"),
    )
    return jax.shard_map(on_device, mesh=inner, in_specs=in_specs, out_specs=out_specs, check_vma=False)
```

```python
import functools

import jax
import jax.numpy as jnp
import numpy as np
from jax import lax
from jax.experimental import pallas as pl
from jax.experimental.pallas import tpu as pltpu
from jax.sharding import Mesh, PartitionSpec as P

EPS = 1e-05
THETA = 10000.0
MASKED = -1e30
HEAD = 64
SCALE = 0.125
TILE = 256
SLOTS = 48
EXPERTS = 32
F32 = jnp.float32
BF16 = jnp.bfloat16
CTX = ("zl", "y")
CHIP = ("zh", "x")
EP = ("zh", "x", "core")
NT = (((1,), (1,)), ((), ()))
TN = (((0,), (0,)), ((), ()))
STEPS = (0, -1, 1, 2)


def exchange(parts, axis):
    return lax.all_to_all(parts, axis, split_axis=0, concat_axis=0, tiled=True)


def spread(block, axis, count):
    return exchange(jnp.broadcast_to(block[None], (count,) + block.shape), axis)


def pass_on(block, axis, steps):
    size = lax.axis_size(axis)
    return lax.ppermute(block, axis, [(i, (i + steps) % size) for i in range(size)])


def after(value, *others):
    return lax.optimization_barrier((value,) + others)[0]


def after_all(values, *others):
    return list(lax.optimization_barrier((*values, *others))[: len(values)])


def ring_blocks(block, ring):
    return [block] + [pass_on(block, ring, -steps) for steps in STEPS[1:]]


def sum_ring(blocks, ring):
    total = blocks[0].astype(F32)
    for place, steps in enumerate(STEPS[1:], 1):
        total = total + pass_on(blocks[place], ring, steps).astype(F32)
    return total


def sum_pair(blocks, pair):
    return blocks[0].astype(F32) + pass_on(blocks[1].astype(BF16), pair, 1).astype(F32)


def dot(left, right, dims=(((1,), (0,)), ((), ()))):
    return lax.dot_general(left, right, dims, preferred_element_type=F32)


def turn(block, cosine, sine):
    lane = lax.broadcasted_iota(jnp.int32, block.shape, 1)
    other = jnp.where(lane % HEAD < HEAD // 2, pltpu.roll(block, 96, 1), pltpu.roll(block, 32, 1))
    return block * cosine + other * sine


def pack_kernel(
    member_ref, query_ref, key_ref, value_ref, router_ref, gain_a_ref, gain_m_ref, hidden_ref, out_ref, sent_ref
):
    out_part = out_ref[:, pl.ds(pl.multiple_of(member_ref[0] * 128, 128), 128)]
    share = hidden_ref.shape[0]
    lane = lax.broadcasted_iota(jnp.int32, (share, 128), 1)
    row = lax.broadcasted_iota(jnp.int32, (16, 128), 0)
    gains = jnp.where(row == 0, gain_a_ref[...].astype(F32), 0.0)
    gains = jnp.where(row == 1, gain_m_ref[...].astype(F32), gains).astype(BF16)
    for peer in range(8):
        sent_ref[peer, :128, :] = query_ref[:, peer * 128 : (peer + 1) * 128]
        columns = slice(peer // 2 * 128, (peer // 2 + 1) * 128)
        key, value = key_ref[:, columns].astype(F32), value_ref[:, columns].astype(F32)
        if peer % 2 == 0:
            value = pltpu.roll(value, HEAD, 1)
        else:
            key = pltpu.roll(key, HEAD, 1)
        sent_ref[peer, 128:256, :] = jnp.where(lane < HEAD, key, value).astype(BF16)
        sent_ref[peer, 256:288, :] = router_ref[...]
        sent_ref[peer, 288:304, :] = gains
        for block in range(8):
            start = 304 + block * share
            sent_ref[peer, start : start + share, :] = hidden_ref[:, block * 128 : (block + 1) * 128]
        sent_ref[peer, 304 + 8 * share :, :] = out_part


def expert_sums_kernel(own_ref, passed_ref, gate_ref, up_ref, down_ref):
    deep = gate_ref.shape[2]
    for e in range(2):
        for place, target in enumerate((gate_ref, up_ref, down_ref)):
            columns = slice((e * 3 + place) * deep, (e * 3 + place + 1) * deep)
            sums = own_ref[:, columns].astype(F32) + passed_ref[:, columns].astype(F32)
            target[e] = sums.T if place == 2 else sums


def document_start(ends_ref, place):
    start = jnp.zeros_like(place)
    for document in range(3):
        end = ends_ref[document]
        start = jnp.where(place >= end, end, start)
    return start


def attend_kernel(
    ends_ref, got_ref, angles_ref,
    mixed_ref, small_ref, *refs,
):
    outside, kept, sent, table_ref, arrived = refs[:5], refs[5:10], refs[10], refs[11], refs[12]
    fetch = pltpu.make_async_copy(angles_ref, table_ref, arrived)
    fetch.start()
    normed_ref, query_ref, key_ref, value_ref, weight_ref = kept
    moves = [pltpu.make_async_copy(kept[n], outside[n], sent.at[n]) for n in range(5)]
    count = normed_ref.shape[0]
    share = count // 8
    for block in range(8):
        rows = slice(block * 128, (block + 1) * 128)
        weight_ref[rows, :128] = got_ref[block, :128, :]
        weight_ref[rows, 128:] = got_ref[block, 128:256, :]
        small_ref[:, rows] = got_ref[block, 256:304, :]
    moves[4].start()
    fetch.wait()
    gain = small_ref[32:33, :].astype(F32)
    lane = lax.broadcasted_iota(jnp.int32, (share, 128), 1)
    low = lane < HEAD
    for piece in range(8):
        rows = slice(piece * share, (piece + 1) * share)
        x = jnp.concatenate(
            [got_ref[piece, 304 + block * share : 304 + (block + 1) * share, :] for block in range(8)], axis=1
        ).astype(F32)
        rho = lax.rsqrt(jnp.mean(x * x, axis=-1, keepdims=True) + EPS)
        normed = (x * rho * gain).astype(BF16)
        normed_ref[rows, :] = normed
        projected = dot(normed, weight_ref[...])
        cosine, sine = table_ref[rows, :128], table_ref[rows, 128:]
        pair = projected[:, 128:]
        turned = pltpu.roll(pair, HEAD, 1)
        query_ref[rows, :] = turn(projected[:, :128], cosine, sine).astype(BF16)
        key_ref[rows, :] = turn(jnp.where(low, pair, turned), cosine, sine).astype(BF16)
        value_ref[rows, :] = jnp.where(low, turned, pair).astype(BF16)
    for move in moves[:4]:
        move.start()
    lane = lax.broadcasted_iota(jnp.int32, (TILE, 128), 1)
    low = lane < HEAD
    for tile in range(count // TILE):
        rows = slice(tile * TILE, (tile + 1) * TILE)
        seen = (tile + 1) * TILE
        keys, values = key_ref[:seen, :], value_ref[:seen, :]
        place = tile * TILE + lax.broadcasted_iota(jnp.int32, (TILE, seen), 0)
        source = lax.broadcasted_iota(jnp.int32, (TILE, seen), 1)
        start = document_start(ends_ref, tile * TILE + lax.broadcasted_iota(jnp.int32, (TILE, 1), 0))
        allowed = (source <= place) & (source >= start)
        scaled = query_ref[rows, :] * jnp.asarray(SCALE, BF16)
        mixed = []
        for head in range(2):
            one = jnp.where(low == (head == 0), scaled, jnp.zeros_like(scaled))
            scores = jnp.where(allowed, dot(one, keys, NT), MASKED)
            weight = jnp.exp(scores - jnp.max(scores, axis=1, keepdims=True))
            probs = weight * (1.0 / jnp.sum(weight, axis=1, keepdims=True))
            mixed.append(dot(probs.astype(BF16), values))
        mixed_ref[rows, :] = jnp.where(low, mixed[0], mixed[1]).astype(BF16)
    for move in moves:
        move.wait()


def attend_back_kernel(
    ends_ref, index_ref, d_mixed_ref, *refs,
):
    outside, (grad_ref, d_normed_ref, key_sum, value_sum, pre_ref) = refs[:6], refs[6:11]
    inside, arrived = refs[11:17], refs[17]
    query_ref, key_ref, value_ref, table_ref, normed_ref, weight_ref = inside
    moves = [pltpu.make_async_copy(outside[n], inside[n], arrived.at[n]) for n in range(6)]
    for move in moves:
        move.start()
    count = query_ref.shape[0]
    lane = lax.broadcasted_iota(jnp.int32, (TILE, 128), 1)
    low = lane < HEAD
    key_sum[...] = jnp.zeros_like(key_sum)
    value_sum[...] = jnp.zeros_like(value_sum)
    for move in moves[:4]:
        move.wait()
    for tile in range(count // TILE):
        rows = slice(tile * TILE, (tile + 1) * TILE)
        seen = (tile + 1) * TILE
        keys, values = key_ref[:seen, :], value_ref[:seen, :]
        place = tile * TILE + lax.broadcasted_iota(jnp.int32, (seen, TILE), 1)
        source = lax.broadcasted_iota(jnp.int32, (seen, TILE), 0)
        start = document_start(ends_ref, tile * TILE + lax.broadcasted_iota(jnp.int32, (1, TILE), 1))
        allowed = (source <= place) & (source >= start)
        scaled = query_ref[rows, :] * jnp.asarray(SCALE, BF16)
        d_mixed = d_mixed_ref[rows, :]
        d_query = []
        for head in range(2):
            mine = low == (head == 0)
            one = jnp.where(mine, scaled, jnp.zeros_like(scaled))
            d_one = jnp.where(mine, d_mixed, jnp.zeros_like(d_mixed))
            scores = jnp.where(allowed, dot(keys, one, NT), MASKED)
            weight = jnp.exp(scores - jnp.max(scores, axis=0, keepdims=True))
            probs = weight * (1.0 / jnp.sum(weight, axis=0, keepdims=True))
            d_probs = dot(values, d_one, NT)
            delta = jnp.sum(probs * d_probs, axis=0, keepdims=True)
            d_scores = (probs * (d_probs - delta)).astype(BF16)
            key_sum[:seen, :] += dot(d_scores, one)
            value_sum[:seen, :] += dot(probs.astype(BF16), d_one)
            d_query.append(dot(d_scores, keys, TN) * SCALE)
        d_query = jnp.where(low, d_query[0], d_query[1])
        pre_ref[rows, :128] = turn(d_query, table_ref[rows, :128], -table_ref[rows, 128:]).astype(BF16)
    for tile in range(count // TILE):
        rows = slice(tile * TILE, (tile + 1) * TILE)
        d_key, d_value = key_sum[rows, :], value_sum[rows, :]
        d_key = turn(d_key + pltpu.roll(d_key, HEAD, 1), table_ref[rows, :128], -table_ref[rows, 128:])
        d_value = d_value + pltpu.roll(d_value, HEAD, 1)
        pre_ref[rows, 128:] = jnp.where(low, d_key, d_value).astype(BF16)
    moves[4].wait()
    moves[5].wait()
    grad_ref[...] = dot(normed_ref[...], pre_ref[...], TN).astype(BF16)
    share = d_normed_ref.shape[2]
    for piece in range(8):
        rows = pl.ds(pl.multiple_of(index_ref[piece] * share, share), share)
        sums = dot(pre_ref[rows, :], weight_ref[...], NT).astype(BF16)
        d_normed_ref[piece // 4, piece % 4] = sums


def router_rows(small_ref):
    rows = small_ref[:EXPERTS, :]
    return jnp.concatenate([rows, jnp.zeros((128 - EXPERTS, rows.shape[1]), BF16)], axis=0)


def route_kernel(
    member_ref, mixed_ref, own_ref, other_ref, hidden_ref, small_ref, grad_ref,
    middle_ref, token_ref, gates_ref, mixed_rows, branch_ref,
):
    width = hidden_ref.shape[1]
    for block in range(8):
        mixed_rows[:, block * 128 : (block + 1) * 128] = mixed_ref[block]
    for place in range(8):
        columns = pl.ds(pl.multiple_of(member_ref[place] * 128, 128), 128)
        weight = (own_ref if place < 4 else other_ref)[place % 4].reshape(width, 128)
        branch_ref[:, columns] = dot(mixed_rows[...], weight)
    middle = hidden_ref[...].astype(F32) + branch_ref[...]
    middle_ref[...] = middle
    rho = lax.rsqrt(jnp.mean(middle * middle, axis=-1, keepdims=True) + EPS)
    routed = (middle * rho * small_ref[33:34, :].astype(F32)).astype(BF16)
    token_ref[:, :width] = routed
    logits = dot(routed, router_rows(small_ref), NT)
    logits = jnp.where(grad_ref[:, width:].astype(F32) > 0.5, logits, MASKED)
    raised = jnp.exp(logits - jnp.max(logits, axis=1, keepdims=True))
    gates = raised / jnp.sum(raised, axis=1, keepdims=True)
    gates_ref[...] = gates
    high = gates.astype(BF16).astype(F32)
    rest = gates - high
    middle_part = rest.astype(BF16).astype(F32)
    last = (rest - middle_part).astype(BF16).astype(F32)
    tail = high + pltpu.roll(middle_part, EXPERTS, 1) + pltpu.roll(last, 2 * EXPERTS, 1)
    token_ref[:, width:] = tail.astype(BF16)


def unroute_kernel(
    member_ref, home_ref, *refs,
):
    outside, (d_mixed_ref, branch_ref, d_middle_ref, router_ref, gain_part_ref) = refs[:7], refs[7:12]
    inside, arrived = refs[12:19], refs[19]
    gates_ref, middle_ref, grad_ref, small_ref, token_ref, own_ref, other_ref = inside
    moves = [pltpu.make_async_copy(outside[n], inside[n], arrived.at[n]) for n in range(7)]
    for move in moves:
        move.start()
    width = middle_ref.shape[1]
    total = home_ref[0].astype(F32)
    for source in range(1, home_ref.shape[0]):
        total += home_ref[source].astype(F32)
    for move in moves[:5]:
        move.wait()
    tail = total[:, width:]
    lane = lax.broadcasted_iota(jnp.int32, tail.shape, 1)
    d_gates = jnp.where(lane < EXPERTS, tail + pltpu.roll(tail, 128 - EXPERTS, 1), 0.0)
    gates = gates_ref[...]
    d_logits = (gates * (d_gates - jnp.sum(gates * d_gates, axis=1, keepdims=True))).astype(BF16)
    d_routed = total[:, :width] + dot(d_logits, router_rows(small_ref))
    middle = middle_ref[...]
    rho = lax.rsqrt(jnp.mean(middle * middle, axis=-1, keepdims=True) + EPS)
    unit = middle * rho
    gain_part_ref[...] = jnp.sum(d_routed * unit, axis=0, keepdims=True)
    c = d_routed * small_ref[33:34, :].astype(F32)
    d_middle = grad_ref[:, :width].astype(F32) + rho * (c - unit * jnp.mean(c * unit, axis=-1, keepdims=True))
    d_middle_ref[...] = d_middle
    branch_ref[...] = d_middle.astype(BF16)
    router_ref[...] = dot(d_logits, token_ref[:, :width], TN)[:EXPERTS].astype(BF16)
    moves[5].wait()
    moves[6].wait()
    d_mixed = jnp.zeros((branch_ref.shape[0], width), F32)
    for place in range(8):
        columns = pl.ds(pl.multiple_of(member_ref[place] * 128, 128), 128)
        weight = (own_ref if place < 4 else other_ref)[place % 4].reshape(width, 128)
        d_mixed += dot(branch_ref[:, columns], weight, NT)
    d_mixed = d_mixed.astype(BF16)
    for block in range(8):
        d_mixed_ref[block] = d_mixed[:, block * 128 : (block + 1) * 128]


def pick_kernel(expert_ref, *refs):
    grads, pick_ref = refs[:4], refs[4]
    share = grads[0].shape[1]
    width = grads[0].shape[2] - 128
    row = lax.broadcasted_iota(jnp.int32, (16, 128), 0)
    lane = lax.broadcasted_iota(jnp.int32, (16, 128), 1)
    choose = ((lane == expert_ref[0] + row) & (row < 2)).astype(F32).astype(BF16)
    ahead = lax.broadcasted_iota(jnp.int32, (share, share), 0) < lax.broadcasted_iota(jnp.int32, (share, share), 1)
    ahead = ahead.astype(F32).astype(BF16)
    slot = lax.broadcasted_iota(jnp.int32, (SLOTS, share), 0).astype(F32)
    for source in range(16):
        named = dot(choose, grads[source // 4][source % 4, :, width:], NT)
        rank = dot(named.astype(BF16), ahead)
        for e in range(2):
            hit = (named[e : e + 1, :] > 0.5) & (rank[e : e + 1, :] == slot)
            pick_ref[source, e * SLOTS : (e + 1) * SLOTS, :] = hit.astype(F32).astype(BF16)


def experts_kernel(
    number, expert_ref, zl_ref, place_ref, pick_ref, token_ref, grad_ref, grad_beside_ref, own_ref, other_ref,
    route_ref, rows_ref, d_result_ref, inner_ref, d_both_ref, gated_ref,
    gate_ref, weight_ref, arrivals, *refs,
):
    back_ref = refs[0] if number == 1 else route_ref
    width = weight_ref.shape[0]
    part = width // 2
    fetches = []
    for e in range(2):
        columns = slice(e * (weight_ref.shape[1] // 2), (e + 1) * (weight_ref.shape[1] // 2))
        for place, source in enumerate((own_ref, other_ref)):
            block = (zl_ref[0] + place) % 2
            target = weight_ref.at[pl.ds(pl.multiple_of(block * part, part), part), columns]
            fetch = pltpu.make_async_copy(source.at[:, columns], target, arrivals.at[e, place])
            fetch.start()
            fetches.append(fetch)
    deep = weight_ref.shape[1] // 6
    lane = lax.broadcasted_iota(jnp.int32, (SLOTS, 128), 1)
    for source in range(8):
        pick = pick_ref[number * 8 + source]
        rows = dot(pick, token_ref[place_ref[source]])
        grads = grad_ref if source < 4 else grad_beside_ref
        cotangent = dot(pick, grads[source % 4, :, :width])
        here = slice(source * SLOTS, (source + 1) * SLOTS)
        for e in range(2):
            part = slice(e * SLOTS, (e + 1) * SLOTS)
            rows_ref[e, here, :] = rows[part, :width].astype(BF16)
            d_result_ref[e, here, :] = cotangent[part].astype(BF16)
            mine = (lane % EXPERTS == expert_ref[0] + e) & (lane < 3 * EXPERTS)
            gate = jnp.sum(jnp.where(mine, rows[part, width:], 0.0), axis=1, keepdims=True)
            gate_ref[e, here, :] = jnp.broadcast_to(gate, (SLOTS, 128))
    lane = lax.broadcasted_iota(jnp.int32, (8 * SLOTS, 128), 1)
    for e in range(2):
        base = e * 3 * deep
        fetches[2 * e].wait()
        fetches[2 * e + 1].wait()
        both = dot(rows_ref[e], weight_ref[:, base : base + 2 * deep])
        a, b = both[:, :deep], both[:, deep:]
        sigma = 1.0 / (1.0 + jnp.exp(-a))
        inner = (a * sigma * b).astype(BF16)
        inner_ref[e] = inner
        down = weight_ref[:, base + 2 * deep : base + 3 * deep]
        result = dot(inner, down, NT).astype(BF16).astype(F32)
        gate = gate_ref[e, :, 0:1]
        cotangent = d_result_ref[e].astype(F32)
        gate_grad = jnp.sum(cotangent * result, axis=1, keepdims=True)
        gated_ref[e] = (gate * result).astype(BF16)
        d_result = (gate * cotangent).astype(BF16)
        d_result_ref[e] = d_result
        d_inner = dot(d_result, down)
        d_both_ref[e, :, :deep] = (d_inner * b * sigma * (1.0 + a * (1.0 - sigma))).astype(BF16)
        d_both_ref[e, :, deep:] = (d_inner * a * sigma).astype(BF16)
        d_rows = dot(d_both_ref[e], weight_ref[:, base : base + 2 * deep], NT).astype(BF16)
        high = gate_grad.astype(BF16).astype(F32)
        low = gate_grad - high
        expert = expert_ref[0] + e
        tail = jnp.where(lane == expert, high, 0.0) + jnp.where(lane == expert + EXPERTS, low, 0.0)
        tail = tail.astype(BF16)
        for source in range(8):
            part = slice(source * SLOTS, (source + 1) * SLOTS)
            back_ref[source, e * SLOTS : (e + 1) * SLOTS, :width] = d_rows[part]
            back_ref[source, e * SLOTS : (e + 1) * SLOTS, width:] = tail[part]
    if number == 1:
        for source in range(8):
            route_ref[place_ref[source]] = dot(pick_ref[8 + source], back_ref[source], TN).astype(BF16)


def join_kernel(place_ref, pick_ref, back_ref, passed_ref, sum_ref):
    for source in range(8):
        place = place_ref[source]
        sums = dot(pick_ref[source], back_ref[source], TN)
        sum_ref[place] = (sums + passed_ref[place].astype(F32)).astype(BF16)


def expert_grads_kernel(number, zl_ref, *refs):
    halves, grads_ref = (refs[:4], refs[4:8]), refs[8]
    deep = refs[2].shape[2]
    part = refs[0].shape[2] // 2
    columns = pl.ds(pl.multiple_of((zl_ref[0] + number) % 2 * part, part), part)
    for e in range(2):
        base = e * 3 * deep
        both = sum(dot(rows[e, :, columns], d_both[e], TN) for rows, d_result, inner, d_both in halves)
        grads_ref[:, base : base + 2 * deep] = both.astype(BF16)
        down = sum(dot(d_result[e, :, columns], inner[e], TN) for rows, d_result, inner, d_both in halves)
        grads_ref[:, base + 2 * deep : base + 3 * deep] = down.astype(BF16)


def outputs_kernel(pick_ref, gated_near_ref, gated_far_ref, near_ref, far_ref):
    for source in range(16):
        gated, target = (gated_near_ref, near_ref) if source < 8 else (gated_far_ref, far_ref)
        here = slice(source % 8 * SLOTS, (source % 8 + 1) * SLOTS)
        both = jnp.concatenate([gated[0, here, :], gated[1, here, :]], axis=0)
        target[source % 4, source % 8 // 4] = dot(pick_ref[source], both, TN).astype(BF16)


def out_grad_kernel(core_ref, ctx_ref, chip_ref, mixed_ref, branch_ref, mine_ref, others_ref, total):
    half = branch_ref.shape[1] // 2
    for number, target in enumerate((others_ref, mine_ref)):
        columns = pl.ds(pl.multiple_of((core_ref[0] + 1 - number) % 2 * half, half), half)
        total[...] = dot(mixed_ref[...], branch_ref[:, columns], TN)
        for chip in range(8):
            for block in range(8):
                start = ctx_ref[block] * 128 + chip_ref[chip] * 16
                rows = pl.ds(pl.multiple_of(start, 16), 16)
                target[chip % 4, chip // 4, block // 4, block % 4] = total[rows, :].astype(BF16)


SMEM = pl.BlockSpec(memory_space=pltpu.SMEM)
VMEM = pl.BlockSpec(memory_space=pltpu.VMEM)
HBM = pl.BlockSpec(memory_space=pltpu.HBM)


def kernel_call(kernel, scalars, arrays, outs, scratch, micros, outside=(), outs_outside=(), limit=60):
    return pl.pallas_call(
        kernel,
        in_specs=[SMEM] * len(scalars) + [VMEM] * len(arrays) + [HBM] * len(outside),
        out_specs=[VMEM] * len(outs) + [HBM] * len(outs_outside),
        out_shape=[jax.ShapeDtypeStruct(shape, kind) for shape, kind in (*outs, *outs_outside)],
        scratch_shapes=scratch,
        compiler_params=pltpu.CompilerParams(vmem_limit_bytes=limit * 1024 * 1024),
        cost_estimate=pl.CostEstimate(flops=int(micros * 1.1e9), bytes_accessed=1, transcendentals=0),
    )(*scalars, *arrays, *outside)


def experts_call(number, expert, zl_index, chip_places, pick, tokens, grads, weights_own, weights_other):
    chips, share, wide = tokens.shape
    width = wide - 128
    total = chips * SLOTS
    deep = weights_own.shape[1] // 6
    back = (chips, 2 * SLOTS, wide)
    return kernel_call(
        functools.partial(experts_kernel, number),
        [expert, zl_index, chip_places],
        [pick, tokens, *grads],
        [((chips, share, wide) if number == 1 else back, BF16)]
        + [((2, total, width), BF16), ((2, total, width), BF16), ((2, total, deep), BF16)]
        + [((2, total, 2 * deep), BF16), ((2, total, width), BF16)],
        [
            pltpu.VMEM((2, total, 128), F32),
            pltpu.VMEM((width, 2 * 3 * deep), BF16),
            pltpu.SemaphoreType.DMA((2, 2)),
        ]
        + ([pltpu.VMEM(back, BF16)] if number == 1 else []),
        13,
        [weights_own, weights_other],
        limit=60,
    )


def grads_call(number, zl_index, near, far):
    shape = (near[0].shape[2] // 2, 6 * near[2].shape[2])
    return kernel_call(
        functools.partial(expert_grads_kernel, number), [zl_index], [*near[:4], *far[:4]], [(shape, BF16)], [], 8,
    )[0]


def on_device(
    hidden, doc_lengths, expert_ids, attn_gain, w_query, key_projection, w_value, w_out,
    moe_gain, w_router, w_gate, w_up, w_down, out_grad,
):
    share, width = hidden.shape[1], hidden.shape[2]
    ctx, chips, peers = 8, 8, 16
    row = share * ctx
    half = width // 2
    local, deep = w_gate.shape[0], w_gate.shape[2]
    zl, y, zh, x, core = (lax.axis_index(name) for name in ("zl", "y", "zh", "x", "core"))
    expert = (((zh * 4 + x) * 2 + core) * local).astype(jnp.int32)[None]
    core_index = core.astype(jnp.int32)[None]
    ctx_places = jnp.stack([(zl + d) % 2 * 4 + (y + s) % 4 for d in range(2) for s in STEPS]).astype(jnp.int32)
    chip_places = jnp.stack([(zh + d) % 2 * 4 + (x + s) % 4 for d in range(2) for s in STEPS]).astype(jnp.int32)
    zl_index = zl.astype(jnp.int32)[None]

    lanes = jnp.arange(128, dtype=jnp.int32)
    chosen = jnp.any(expert_ids[0][:, :, None] == lanes[None, None, :], axis=1)
    grad_rows = jnp.concatenate([out_grad[0], chosen.astype(BF16)], axis=1)
    grad_beside = pass_on(grad_rows, "zh", 1)

    members = [((x + s) % 4 * 2 + (core + d) % 2) for d in range(2) for s in STEPS]
    members = jnp.stack(members).astype(jnp.int32)
    (sent,) = kernel_call(
        pack_kernel,
        [members],
        [w_query, key_projection, w_value, w_router, attn_gain[None], moe_gain[None], after(hidden[0], grad_rows), w_out],
        [((ctx, 304 + 9 * share, 128), BF16)],
        [],
        2,
    )
    got = exchange(sent, CTX)

    packed = jnp.concatenate(
        [part for e in range(local) for part in (w_gate[e], w_up[e], w_down[e].T)], axis=1
    )
    grads = ring_blocks(after(jnp.stack([grad_rows, grad_beside]), sent), "x")
    packed, *grads = lax.optimization_barrier((packed, *grads))
    grads = [jnp.stack([piece[d] for piece in grads]) for d in range(2)]
    got, packed, *grads = lax.optimization_barrier((got, packed, *grads))
    out_blocks = ring_blocks(got[:, 304 + 8 * share :], "x")

    ends = jnp.cumsum(doc_lengths[0]).astype(jnp.int32)
    freq = THETA ** (-(np.arange(HEAD // 2, dtype=np.float32) * 2.0 / HEAD))
    angle = np.arange(row, dtype=np.float32)[:, None] * freq[None, :].astype(np.float32)
    cosine, sine = np.cos(angle), np.sin(angle)
    table = jnp.asarray(np.concatenate([cosine] * 4 + [-sine, sine, -sine, sine], axis=1).astype(np.float32))

    weights_own = lax.all_gather(packed, "y", axis=0, tiled=True)
    weights_other = lax.all_gather(pass_on(packed, "zl", 1), "y", axis=0, tiled=True)

    mixed, small, normed, query, key, value, weight = kernel_call(
        attend_kernel,
        [ends],
        [got],
        [((row, 128), BF16), ((48, width), BF16)],
        [pltpu.VMEM((row, width), BF16)]
        + [pltpu.VMEM((row, 128), BF16)] * 3
        + [pltpu.VMEM((width, 256), BF16), pltpu.SemaphoreType.DMA((5,))]
        + [pltpu.VMEM((row, 256), F32), pltpu.SemaphoreType.DMA(())],
        8,
        [table],
        outs_outside=[((row, width), BF16)] + [((row, 128), BF16)] * 3 + [((width, 256), BF16)],
    )
    mixed, *out_blocks = lax.optimization_barrier((mixed, *out_blocks))
    grads = grads + [pass_on(after(piece, mixed), "core", 1) for piece in grads]
    (pick,) = kernel_call(pick_kernel, [expert], grads, [((peers, 2 * SLOTS, share), BF16)], [], 4)
    out_own = jnp.stack(out_blocks)
    out_other = pass_on(out_own, "core", 1)

    mixed_rows = exchange(mixed.reshape(ctx, share, 128), CTX)
    middle, tokens, gates, mixed_rows = kernel_call(
        route_kernel,
        [members],
        [mixed_rows, out_own, out_other, hidden[0], small, grad_rows],
        [((share, width), F32), ((share, width + 128), BF16), ((share, 128), F32), ((share, width), BF16)],
        [pltpu.VMEM((share, width), F32)],
        3,
    )
    tokens_near = after(spread(tokens, CHIP, chips), pick)
    tokens_far = pass_on(tokens_near, "core", 1)

    common = (expert, zl_index, chip_places, pick)
    route_far, *far = experts_call(1, *common, tokens_far, grads[2:], weights_own, weights_other)
    route_passed = pass_on(route_far, "core", 1)
    back_near, *near = experts_call(
        0, *common, after(tokens_near, *far), grads[:2], weights_own, weights_other
    )
    (route_sums,) = kernel_call(
        join_kernel, [chip_places], [pick, back_near, route_passed], [((chips, share, width + 128), BF16)], [], 3
    )
    near = after_all(near, route_sums)
    grads_other = grads_call(1, zl_index, near, far)
    grads_own = grads_call(0, zl_index, near, far)
    out_near, out_far = kernel_call(
        outputs_kernel, [], [pick, near[4], far[4]], [((4, 2, share, width), BF16)] * 2, [], 4
    )
    out_sums = (out_near.astype(F32) + pass_on(out_far, "core", 1).astype(F32)).astype(BF16)
    route_sums, grads_other, grads_own, out_sums = lax.optimization_barrier(
        (exchange(route_sums, CHIP), grads_other, grads_own, out_sums)
    )
    sums_other = lax.psum_scatter(grads_other, "y", scatter_dimension=0, tiled=True)
    sums_own = lax.psum_scatter(after(grads_own, grads_other), "y", scatter_dimension=0, tiled=True)
    d_mixed, d_branch, d_middle, router_part, moe_gain_part = kernel_call(
        unroute_kernel,
        [members],
        [route_sums],
        [((ctx, share, 128), BF16), ((share, width), BF16), ((share, width), F32)]
        + [((EXPERTS, width), BF16), ((1, width), F32)],
        [pltpu.VMEM((share, 128), F32), pltpu.VMEM((share, width), F32), pltpu.VMEM((share, width + 128), BF16)]
        + [pltpu.VMEM((48, width), BF16), pltpu.VMEM((share, width + 128), BF16)]
        + [pltpu.VMEM((4, ctx, 128, 128), BF16)] * 2
        + [pltpu.SemaphoreType.DMA((7,))],
        3,
        [gates, middle, grad_rows, small, tokens, out_own, out_other],
    )
    d_mixed = exchange(d_mixed, CTX).reshape(row, 128)

    out_mine, out_others = kernel_call(
        out_grad_kernel, [core_index, ctx_places, chip_places], [mixed_rows, d_branch],
        [((4, 2, 2, 4, 16, half), BF16)] * 2, [pltpu.VMEM((width, half), F32)], 3,
    )
    out_part = (out_mine.astype(F32) + pass_on(out_others, "core", 1).astype(F32)).astype(BF16)
    d_mixed, out_part = lax.optimization_barrier((d_mixed, out_part))
    out_part = sum_ring(out_part, "x")
    out_sums = sum_ring(out_sums, "x")

    projection_part, d_normed_part = kernel_call(
        attend_back_kernel,
        [ends, ctx_places],
        [d_mixed],
        [((width, 256), BF16), ((2, 4, share, width), BF16)],
        [pltpu.VMEM((row, 128), F32), pltpu.VMEM((row, 128), F32), pltpu.VMEM((row, 256), BF16)]
        + [pltpu.VMEM((row, 128), BF16)] * 3
        + [pltpu.VMEM((row, 256), F32), pltpu.VMEM((row, width), BF16), pltpu.VMEM((width, 256), BF16)]
        + [pltpu.SemaphoreType.DMA((6,))],
        10,
        [query, key, value, table, normed, weight],
    )

    piece = 128 // peers
    kinds = EXPERTS // peers
    router_send = router_part.reshape(peers, kinds, ctx, 128).transpose(2, 0, 1, 3)
    gain_send = jnp.broadcast_to(moe_gain_part.astype(BF16).reshape(ctx, 1, 1, 128), (ctx, peers, 1, 128))
    small_send = jnp.concatenate(
        [router_send, gain_send, jnp.zeros((ctx, peers, piece - kinds - 1, 128), BF16)], axis=2
    )
    bundle = jnp.concatenate(
        [projection_part.reshape(ctx, peers, piece, 256), small_send], axis=3
    ).reshape(ctx * peers, piece, 384)
    bundle, out_part = lax.optimization_barrier((bundle, out_part))
    out_part = sum_pair(out_part, "zh").astype(BF16)
    out_sum = sum_ring(sum_pair(out_part, "zl").astype(BF16), "y")
    out_sum = jnp.concatenate([out_sum[:8], out_sum[8:]], axis=1)
    output = middle + sum_pair(out_sums, "zh")
    d_normed_near = sum_pair(d_normed_part, "zl").astype(BF16)
    bundle = after(exchange(bundle, CTX + EP), out_sum, d_normed_near, output).reshape(ctx, peers, piece, 384)
    summed = jnp.sum(bundle.astype(F32), axis=1)
    d_normed = sum_ring(d_normed_near, "y")
    small_sum = jnp.sum(summed[:, :, 256:], axis=0)
    final = jnp.concatenate(
        [
            summed[:, :, :128].transpose(1, 0, 2).reshape(piece, width),
            summed[:, :, 128:192].transpose(1, 0, 2).reshape(piece, width // 2),
            summed[:, :, 192:256].transpose(1, 0, 2).reshape(piece, width // 2),
            out_sum,
            small_sum,
        ],
        axis=1,
    ).astype(BF16)
    passed = pass_on(after(sums_other, d_normed_near), "zl", 1)
    gate_sum, up_sum, down_sum = kernel_call(
        expert_sums_kernel, [], [sums_own, passed],
        [((local, 128, deep), F32)] * 2 + [((local, deep, 128), F32)], [], 2,
    )
    residual = hidden[0].astype(F32)
    rho_a = lax.rsqrt(jnp.mean(residual * residual, axis=-1, keepdims=True) + EPS)
    unit_a = residual * rho_a
    c = d_normed * small[32:33].astype(F32)
    hidden_grad = d_middle + rho_a * (c - unit_a * jnp.mean(c * unit_a, axis=-1, keepdims=True))
    final = after(spread(final, EP, peers), gate_sum, hidden_grad, output).astype(F32)
    rows_of = final.reshape(peers * piece, -1)
    query_grad, key_grad = rows_of[:, :width], rows_of[:, width : width + width // 2]
    value_grad = rows_of[:, width + width // 2 : 2 * width]
    out_weight_grad = final[:, :, 2 * width : 3 * width].reshape(chips, 2, piece, 2, half)
    out_weight_grad = out_weight_grad.transpose(0, 3, 2, 1, 4).reshape(128, width)
    router_grad = final[:, :kinds, 3 * width :].reshape(EXPERTS, 128)
    moe_gain_grad = small_sum[kinds]
    attn_gain_grad = (
        jnp.sum(w_query.astype(F32) * query_grad, axis=1)
        + jnp.sum(key_projection.astype(F32) * key_grad, axis=1)
        + jnp.sum(w_value.astype(F32) * value_grad, axis=1)
    ) / attn_gain.astype(F32)

    return (
        output.astype(BF16)[None], hidden_grad[None], attn_gain_grad, query_grad, key_grad, value_grad,
        out_weight_grad, moe_gain_grad, router_grad, gate_sum, up_sum, down_sum,
    )


def solution(mesh):
    axes = ("zl", "y", "zh", "x", "core")
    inner = Mesh(mesh.devices.reshape(2, 4, 2, 4, 2), axes)
    in_specs = (
        P(EP, CTX, None), P(EP, None), P(EP, CTX, None), P(CTX), P(CTX, None), P(CTX, None),
        P(CTX, None), P(CTX, None), P(CTX), P(None, CTX), P(EP, CTX, None), P(EP, CTX, None),
        P(EP, None, CTX), P(EP, CTX, None),
    )
    out_specs = (
        P(EP, CTX, None), P(EP, CTX, None), P(CTX), P(CTX, None), P(CTX, None), P(CTX, None),
        P(CTX, None), P(CTX), P(None, CTX), P(EP, CTX, None), P(EP, CTX, None), P(EP, None, CTX),
    )
    return jax.shard_map(on_device, mesh=inner, in_specs=in_specs, out_specs=out_specs, check_vma=False)
```

```python
import functools

import jax
import jax.numpy as jnp
import numpy as np
from jax import lax
from jax.experimental import pallas as pl
from jax.experimental.pallas import tpu as pltpu
from jax.sharding import Mesh, PartitionSpec as P

EPS = 1e-05
THETA = 10000.0
MASKED = -1e30
HEAD = 64
SCALE = 0.125
TILE = 256
SLOTS = 48
EXPERTS = 32
F32 = jnp.float32
BF16 = jnp.bfloat16
CTX = ("zl", "y")
CHIP = ("zh", "x")
EP = ("zh", "x", "core")
SIDE = 128
NT = (((1,), (1,)), ((), ()))
TN = (((0,), (0,)), ((), ()))
STEPS = (0, -1, 1, 2)


def exchange(parts, axis):
    return lax.all_to_all(parts, axis, split_axis=0, concat_axis=0, tiled=True)


def spread(block, axis, count):
    return exchange(jnp.broadcast_to(block[None], (count,) + block.shape), axis)


def pass_on(block, axis, steps):
    size = lax.axis_size(axis)
    return lax.ppermute(block, axis, [(i, (i + steps) % size) for i in range(size)])


def together(*values):
    return lax.optimization_barrier(values)


def ring_blocks(block, ring):
    return [block] + [pass_on(block, ring, -steps) for steps in STEPS[1:]]


def ring_blocks_out(blocks, ring):
    return [blocks[0]] + [pass_on(block, ring, steps) for block, steps in zip(blocks[1:], STEPS[1:])]


def dot(left, right, dims=(((1,), (0,)), ((), ()))):
    return lax.dot_general(left, right, dims, preferred_element_type=F32)


def turn(block, cosine, sine):
    lane = lax.broadcasted_iota(jnp.int32, block.shape, 1)
    other = jnp.where(lane % HEAD < HEAD // 2, pltpu.roll(block, 96, 1), pltpu.roll(block, 32, 1))
    return block * cosine + other * sine


def pack_kernel(
    member_ref, query_ref, key_ref, value_ref, router_ref, gain_a_ref, gain_m_ref, hidden_ref, out_ref, sent_ref
):
    out_part = out_ref[:, pl.ds(pl.multiple_of(member_ref[0] * 128, 128), 128)]
    share = hidden_ref.shape[0]
    lane = lax.broadcasted_iota(jnp.int32, (share, 128), 1)
    row = lax.broadcasted_iota(jnp.int32, (16, 128), 0)
    gains = jnp.where(row == 0, gain_a_ref[...].astype(F32), 0.0)
    gains = jnp.where(row == 1, gain_m_ref[...].astype(F32), gains).astype(BF16)
    for peer in range(8):
        sent_ref[peer, :128, :] = query_ref[:, peer * 128 : (peer + 1) * 128]
        columns = slice(peer // 2 * 128, (peer // 2 + 1) * 128)
        key, value = key_ref[:, columns].astype(F32), value_ref[:, columns].astype(F32)
        if peer % 2 == 0:
            value = pltpu.roll(value, HEAD, 1)
        else:
            key = pltpu.roll(key, HEAD, 1)
        sent_ref[peer, 128:256, :] = jnp.where(lane < HEAD, key, value).astype(BF16)
        sent_ref[peer, 256:288, :] = router_ref[...]
        sent_ref[peer, 288:304, :] = gains
        for block in range(8):
            start = 304 + block * share
            sent_ref[peer, start : start + share, :] = hidden_ref[:, block * 128 : (block + 1) * 128]
        sent_ref[peer, 304 + 8 * share :, :] = out_part


def expert_sums_kernel(own_ref, passed_ref, gate_ref, up_ref, down_ref):
    deep = gate_ref.shape[2]
    for e in range(2):
        for place, target in enumerate((gate_ref, up_ref, down_ref)):
            columns = slice((e * 3 + place) * deep, (e * 3 + place + 1) * deep)
            sums = own_ref[:, columns].astype(F32) + passed_ref[:, columns].astype(F32)
            target[e] = sums.T if place == 2 else sums


def document_start(ends_ref, place):
    start = jnp.zeros_like(place)
    for document in range(3):
        end = ends_ref[document]
        start = jnp.where(place >= end, end, start)
    return start


def attend_kernel(
    ends_ref, got_ref, angles_ref,
    mixed_ref, small_ref, *refs,
):
    outside, kept, sent, table_ref, arrived = refs[:5], refs[5:10], refs[10], refs[11], refs[12]
    fetch = pltpu.make_async_copy(angles_ref, table_ref, arrived)
    fetch.start()
    normed_ref, query_ref, key_ref, value_ref, weight_ref = kept
    moves = [pltpu.make_async_copy(kept[n], outside[n], sent.at[n]) for n in range(5)]
    count = normed_ref.shape[0]
    share = count // 8
    for block in range(8):
        rows = slice(block * 128, (block + 1) * 128)
        weight_ref[rows, :128] = got_ref[block, :128, :]
        weight_ref[rows, 128:] = got_ref[block, 128:256, :]
        small_ref[:, rows] = got_ref[block, 256:304, :]
    moves[4].start()
    fetch.wait()
    gain = small_ref[32:33, :].astype(F32)
    lane = lax.broadcasted_iota(jnp.int32, (share, 128), 1)
    low = lane < HEAD
    for piece in range(8):
        rows = slice(piece * share, (piece + 1) * share)
        x = jnp.concatenate(
            [got_ref[piece, 304 + block * share : 304 + (block + 1) * share, :] for block in range(8)], axis=1
        ).astype(F32)
        rho = lax.rsqrt(jnp.mean(x * x, axis=-1, keepdims=True) + EPS)
        normed = (x * rho * gain).astype(BF16)
        normed_ref[rows, :] = normed
        projected = dot(normed, weight_ref[...])
        cosine, sine = table_ref[rows, :128], table_ref[rows, 128:]
        pair = projected[:, 128:]
        turned = pltpu.roll(pair, HEAD, 1)
        query_ref[rows, :] = turn(projected[:, :128], cosine, sine).astype(BF16)
        key_ref[rows, :] = turn(jnp.where(low, pair, turned), cosine, sine).astype(BF16)
        value_ref[rows, :] = jnp.where(low, turned, pair).astype(BF16)
    for move in moves[:4]:
        move.start()
    lane = lax.broadcasted_iota(jnp.int32, (TILE, 128), 1)
    low = lane < HEAD
    for tile in range(count // TILE):
        rows = slice(tile * TILE, (tile + 1) * TILE)
        seen = (tile + 1) * TILE
        keys, values = key_ref[:seen, :], value_ref[:seen, :]
        place = tile * TILE + lax.broadcasted_iota(jnp.int32, (TILE, seen), 0)
        source = lax.broadcasted_iota(jnp.int32, (TILE, seen), 1)
        start = document_start(ends_ref, tile * TILE + lax.broadcasted_iota(jnp.int32, (TILE, 1), 0))
        allowed = (source <= place) & (source >= start)
        scaled = query_ref[rows, :] * jnp.asarray(SCALE, BF16)
        mixed = []
        for head in range(2):
            one = jnp.where(low == (head == 0), scaled, jnp.zeros_like(scaled))
            scores = jnp.where(allowed, dot(one, keys, NT), MASKED)
            weight = jnp.exp(scores - jnp.max(scores, axis=1, keepdims=True))
            probs = weight * (1.0 / jnp.sum(weight, axis=1, keepdims=True))
            mixed.append(dot(probs.astype(BF16), values))
        mixed_ref[rows, :] = jnp.where(low, mixed[0], mixed[1]).astype(BF16)
    for move in moves:
        move.wait()


def attend_back_kernel(
    ends_ref, index_ref, core_ref, d_mixed_ref, *refs,
):
    outside, (mine_ref, others_ref), d_normed_out = refs[:6], refs[7:9], refs[9:13]
    key_sum, value_sum, pre_ref, grad_ref, d_normed_ref, left = refs[13:19]
    inside, arrived = refs[19:25], refs[25]
    query_ref, key_ref, value_ref, table_ref, normed_ref, weight_ref = inside
    moves = [pltpu.make_async_copy(outside[n], inside[n], arrived.at[n]) for n in range(6)]
    for move in moves:
        move.start()
    count = query_ref.shape[0]
    lane = lax.broadcasted_iota(jnp.int32, (TILE, 128), 1)
    low = lane < HEAD
    key_sum[...] = jnp.zeros_like(key_sum)
    value_sum[...] = jnp.zeros_like(value_sum)
    for move in moves[:4]:
        move.wait()
    for tile in range(count // TILE):
        rows = slice(tile * TILE, (tile + 1) * TILE)
        seen = (tile + 1) * TILE
        keys, values = key_ref[:seen, :], value_ref[:seen, :]
        place = tile * TILE + lax.broadcasted_iota(jnp.int32, (seen, TILE), 1)
        source = lax.broadcasted_iota(jnp.int32, (seen, TILE), 0)
        start = document_start(ends_ref, tile * TILE + lax.broadcasted_iota(jnp.int32, (1, TILE), 1))
        allowed = (source <= place) & (source >= start)
        scaled = query_ref[rows, :] * jnp.asarray(SCALE, BF16)
        d_mixed = d_mixed_ref[rows, :]
        d_query = []
        for head in range(2):
            mine = low == (head == 0)
            one = jnp.where(mine, scaled, jnp.zeros_like(scaled))
            d_one = jnp.where(mine, d_mixed, jnp.zeros_like(d_mixed))
            scores = jnp.where(allowed, dot(keys, one, NT), MASKED)
            weight = jnp.exp(scores - jnp.max(scores, axis=0, keepdims=True))
            probs = weight * (1.0 / jnp.sum(weight, axis=0, keepdims=True))
            d_probs = dot(values, d_one, NT)
            delta = jnp.sum(probs * d_probs, axis=0, keepdims=True)
            d_scores = (probs * (d_probs - delta)).astype(BF16)
            key_sum[:seen, :] += dot(d_scores, one)
            value_sum[:seen, :] += dot(probs.astype(BF16), d_one)
            d_query.append(dot(d_scores, keys, TN) * SCALE)
        d_query = jnp.where(low, d_query[0], d_query[1])
        pre_ref[rows, :128] = turn(d_query, table_ref[rows, :128], -table_ref[rows, 128:]).astype(BF16)
    for tile in range(count // TILE):
        rows = slice(tile * TILE, (tile + 1) * TILE)
        d_key, d_value = key_sum[rows, :], value_sum[rows, :]
        d_key = turn(d_key + pltpu.roll(d_key, HEAD, 1), table_ref[rows, :128], -table_ref[rows, 128:])
        d_value = d_value + pltpu.roll(d_value, HEAD, 1)
        pre_ref[rows, 128:] = jnp.where(low, d_key, d_value).astype(BF16)
    moves[4].wait()
    moves[5].wait()
    share = d_normed_ref.shape[2]
    leaving = []
    for piece in (4, 5, 6, 7, 0, 1, 2, 3):
        rows = pl.ds(pl.multiple_of(index_ref[piece] * share, share), share)
        pair, place = piece // 4, piece % 4
        d_normed_ref[place, pair] = dot(pre_ref[rows, :], weight_ref[...], NT).astype(BF16)
        leaving.append(
            pltpu.make_async_copy(d_normed_ref.at[place, pair], d_normed_out[place].at[pair], left.at[place, pair])
        )
        leaving[-1].start()
    grad_ref[...] = dot(normed_ref[...], pre_ref[...], TN)
    for number, target in enumerate((mine_ref, others_ref)):
        member = (core_ref[0] + number) % 2
        for block in range(count // 16):
            rows = grad_ref[pl.ds(pl.multiple_of(block * 16 + member * 8, 8), 8), :]
            rows = jnp.concatenate([rows[:, :128], rows[:, 128:]], axis=0)
            target[block * 16 : (block + 1) * 16, :] = rows.astype(BF16)
    for move in leaving:
        move.wait()


def router_rows(small_ref):
    rows = small_ref[:EXPERTS, :]
    return jnp.concatenate([rows, jnp.zeros((128 - EXPERTS, rows.shape[1]), BF16)], axis=0)


def route_kernel(
    member_ref, mixed_ref, own_ref, other_ref, hidden_ref, small_ref, grad_ref,
    middle_ref, gates_ref, mixed_rows, tokens_out, token_ref, branch_ref, left,
):
    width = hidden_ref.shape[1]
    for block in range(8):
        mixed_rows[:, block * 128 : (block + 1) * 128] = mixed_ref[block]
    for place in range(8):
        columns = pl.ds(pl.multiple_of(member_ref[place] * 128, 128), 128)
        weight = (own_ref if place < 4 else other_ref)[place % 4].reshape(width, 128)
        branch_ref[:, columns] = dot(mixed_rows[...], weight)
    middle = hidden_ref[...].astype(F32) + branch_ref[...]
    middle_ref[...] = middle
    rho = lax.rsqrt(jnp.mean(middle * middle, axis=-1, keepdims=True) + EPS)
    routed = (middle * rho * small_ref[33:34, :].astype(F32)).astype(BF16)
    token_ref[:, :width] = routed
    logits = dot(routed, router_rows(small_ref), NT)
    logits = jnp.where(grad_ref[:, width:].astype(F32) > 0.5, logits, MASKED)
    raised = jnp.exp(logits - jnp.max(logits, axis=1, keepdims=True))
    gates = raised / jnp.sum(raised, axis=1, keepdims=True)
    gates_ref[...] = gates
    high = gates.astype(BF16).astype(F32)
    rest = gates - high
    middle_part = rest.astype(BF16).astype(F32)
    last = (rest - middle_part).astype(BF16).astype(F32)
    tail = high + pltpu.roll(middle_part, EXPERTS, 1) + pltpu.roll(last, 2 * EXPERTS, 1)
    token_ref[:, width:] = tail.astype(BF16)
    leaving = [pltpu.make_async_copy(token_ref, tokens_out.at[chip], left.at[chip]) for chip in range(8)]
    for move in leaving:
        move.start()
    for move in leaving:
        move.wait()


def unroute_kernel(
    member_ref, home_out, *refs,
):
    outside, (d_mixed_ref, mine_ref, others_ref, d_middle_ref) = refs[:8], refs[8:12]
    inside, arrived, home_ref, home_arrived, branch_ref = refs[12:20], *refs[20:24]
    middle_ref, gates_ref, grad_ref, token_ref, small_ref, own_ref, other_ref, mixed_ref = inside
    sources = [home_out.at[source] for source in range(8)]
    homes = [pltpu.make_async_copy(sources[n], home_ref.at[n], home_arrived.at[n]) for n in range(8)]
    moves = []
    for n in range(8):
        source = outside[n].at[0] if n == 3 else outside[n]
        moves.append(pltpu.make_async_copy(source, inside[n], arrived.at[n]))
    for move in homes + moves:
        move.start()
    width = middle_ref.shape[1]
    homes[0].wait()
    total = home_ref[0].astype(F32)
    for source in range(1, 8):
        homes[source].wait()
        total += home_ref[source].astype(F32)
    for move in moves[:5]:
        move.wait()
    tail = total[:, width:]
    lane = lax.broadcasted_iota(jnp.int32, tail.shape, 1)
    d_gates = jnp.where(lane < EXPERTS, tail + pltpu.roll(tail, 128 - EXPERTS, 1), 0.0)
    gates = gates_ref[...]
    d_logits = (gates * (d_gates - jnp.sum(gates * d_gates, axis=1, keepdims=True))).astype(BF16)
    d_routed = total[:, :width] + dot(d_logits, router_rows(small_ref))
    middle = middle_ref[...]
    rho = lax.rsqrt(jnp.mean(middle * middle, axis=-1, keepdims=True) + EPS)
    unit = middle * rho
    gain_part = jnp.sum(d_routed * unit, axis=0, keepdims=True)
    c = d_routed * small_ref[33:34, :].astype(F32)
    d_middle = grad_ref[:, :width].astype(F32) + rho * (c - unit * jnp.mean(c * unit, axis=-1, keepdims=True))
    d_middle_ref[...] = d_middle
    branch_ref[...] = d_middle.astype(BF16)
    for move in moves[5:]:
        move.wait()
    d_mixed = jnp.zeros((branch_ref.shape[0], width), F32)
    for place in range(8):
        columns = pl.ds(pl.multiple_of(member_ref[place] * 128, 128), 128)
        weight = (own_ref if place < 4 else other_ref)[place % 4].reshape(width, 128)
        d_mixed += dot(branch_ref[:, columns], weight, NT)
    d_mixed = d_mixed.astype(BF16)
    for block in range(8):
        d_mixed_ref[block] = d_mixed[:, block * 128 : (block + 1) * 128]
    router_part = dot(d_logits, token_ref[:, :width], TN)[:EXPERTS].astype(BF16)
    gain_rows = jnp.where(lax.broadcasted_iota(jnp.int32, (16, width), 0) == 0, gain_part, 0.0).astype(BF16)
    small_rows = jnp.concatenate([router_part, gain_rows], axis=0)
    row = lax.broadcasted_iota(jnp.int32, (128, 48), 0)
    column = lax.broadcasted_iota(jnp.int32, (128, 48), 1)
    for number, target in enumerate((mine_ref, others_ref)):
        member = (member_ref[0] + number) % 2
        half = pl.ds(pl.multiple_of(member * (width // 2), width // 2), width // 2)
        target[:, : width // 2] = dot(mixed_ref[...], branch_ref[:, half], TN).astype(BF16)
        place = row % 16
        wanted = jnp.where(place == 2, EXPERTS, jnp.where(place < 2, row // 16 * 4 + member * 2 + place, -1))
        choose = (wanted == column).astype(F32).astype(BF16)
        for block in range(8):
            rows = slice(block * 128, (block + 1) * 128)
            target[rows, width // 2 :] = dot(choose, small_rows[:, rows]).astype(BF16)


def add_kernel(mine_ref, passed_ref, sum_ref):
    sum_ref[...] = (mine_ref[...].astype(F32) + passed_ref[...].astype(F32)).astype(BF16)


def late_kernel(mine_ref, passed_ref, *refs):
    add_kernel(mine_ref, passed_ref, refs[-1])


def add_four_kernel(a_ref, b_ref, c_ref, part_out, sum_ref, other_ref, part_ref, arrived):
    move = pltpu.make_async_copy(part_out, part_ref, arrived)
    move.start()
    total = a_ref[...].astype(F32) + b_ref[...].astype(F32) + c_ref[...].astype(F32)
    move.wait()
    total = (total + part_ref[...].astype(F32)).astype(BF16)
    sum_ref[...] = total[0]
    other_ref[...] = total[1]


def hidden_grad_kernel(near_ref, passed_ref, d_middle_ref, hidden_ref, small_ref, grad_ref):
    x = hidden_ref[...].astype(F32)
    rho = lax.rsqrt(jnp.mean(x * x, axis=-1, keepdims=True) + EPS)
    unit = x * rho
    d_normed = near_ref[...].astype(F32) + passed_ref[...].astype(F32)
    c = d_normed * small_ref[32:33, :].astype(F32)
    grad_ref[...] = d_middle_ref[...] + rho * (c - unit * jnp.mean(c * unit, axis=-1, keepdims=True))


def output_kernel(near_ref, passed_ref, middle_ref, output_ref):
    total = middle_ref[...] + near_ref[...].astype(F32) + passed_ref[...].astype(F32)
    output_ref[...] = total.astype(BF16)


def reduce_kernel(early_ref, late_ref, before_ref, sums_ref, scratch):
    early = early_ref[0].astype(F32)
    for source in range(1, 64):
        early += early_ref[source].astype(F32)
    scratch[:, 1024:] = early.astype(BF16)
    for block in range(8):
        late = late_ref[block * 8].astype(F32)
        for source in range(1, 8):
            late += late_ref[block * 8 + source].astype(F32)
        scratch[:, block * 128 : (block + 1) * 128] = late.astype(BF16)
    for peer in range(16):
        sums_ref[peer] = scratch[...]


def finish_kernel(
    sums_ref, w_query_ref, w_key_ref, w_value_ref, gain_ref,
    query_ref, key_ref, value_ref, out_ref, gain_a_ref, gain_m_ref, router_ref,
):
    lane = lax.broadcasted_iota(jnp.int32, (8, 128), 1)
    low = lane < HEAD
    for peer in range(16):
        sums = sums_ref[peer].astype(F32)
        rows = slice(peer * 8, (peer + 1) * 8)
        query_ref[rows, :] = sums[:8, :1024]
        for pair in range(4):
            even = sums[8:, pair * 256 : pair * 256 + 128]
            odd = sums[8:, pair * 256 + 128 : (pair + 1) * 256]
            columns = slice(pair * 128, (pair + 1) * 128)
            key_ref[rows, columns] = jnp.where(low, even, pltpu.roll(odd, HEAD, 1))
            value_ref[rows, columns] = jnp.where(low, pltpu.roll(even, HEAD, 1), odd)
        columns = slice(peer % 2 * 512, (peer % 2 + 1) * 512)
        out_ref[peer // 2 * 16 : (peer // 2 + 1) * 16, columns] = sums[:, 1024:1536]
        router_ref[peer * 2 : peer * 2 + 2, :] = sums[0:2, 1536:]
        if peer == 0:
            gain_m_ref[...] = sums[2:3, 1536:]
    total = jnp.sum(w_query_ref[...].astype(F32) * query_ref[...], axis=1, keepdims=True)
    total += jnp.sum(w_key_ref[...].astype(F32) * key_ref[...], axis=1, keepdims=True)
    total += jnp.sum(w_value_ref[...].astype(F32) * value_ref[...], axis=1, keepdims=True)
    total = jnp.broadcast_to(total, (128, 128)).T
    gain_a_ref[...] = total[0:1, :] / gain_ref[...].astype(F32)


def pack_weights_kernel(gate_ref, up_ref, down_ref, before_ref, packed_ref):
    deep = gate_ref.shape[2]
    for e in range(2):
        base = e * 3 * deep
        packed_ref[:, base : base + deep] = gate_ref[e]
        packed_ref[:, base + deep : base + 2 * deep] = up_ref[e]
        packed_ref[:, base + 2 * deep : base + 3 * deep] = down_ref[e].T


def pair_kernel(mine_ref, beside_ref, before_ref, pair_ref):
    pair_ref[0] = mine_ref[...]
    pair_ref[1] = beside_ref[...]


def pick_kernel(expert_ref, place_ref, *refs):
    grads, pick_ref, flags_ref, arrived = refs[:2], *refs[2:]
    share = grads[0].shape[2]
    width = grads[0].shape[3] - 128
    fetches = []
    for piece in range(16):
        source = grads[piece // 8].at[place_ref[piece % 8] % 4, piece % 8 // 4, :, width:]
        fetches.append(pltpu.make_async_copy(source, flags_ref.at[piece], arrived.at[piece]))
        fetches[-1].start()
    row = lax.broadcasted_iota(jnp.int32, (16, 128), 0)
    lane = lax.broadcasted_iota(jnp.int32, (16, 128), 1)
    choose = ((lane == expert_ref[0] + row) & (row < 2)).astype(F32).astype(BF16)
    ahead = lax.broadcasted_iota(jnp.int32, (share, share), 0) < lax.broadcasted_iota(jnp.int32, (share, share), 1)
    ahead = ahead.astype(F32).astype(BF16)
    slot = lax.broadcasted_iota(jnp.int32, (SLOTS, share), 0).astype(F32)
    for fetch in fetches:
        fetch.wait()
    for piece in range(16):
        source = piece // 8 * 8 + place_ref[piece % 8]
        named = dot(choose, flags_ref[piece], NT)
        rank = dot(named.astype(BF16), ahead)
        for e in range(2):
            hit = (named[e : e + 1, :] > 0.5) & (rank[e : e + 1, :] == slot)
            pick_ref[source, e * SLOTS : (e + 1) * SLOTS, :] = hit.astype(F32).astype(BF16)


def experts_kernel(
    number, expert_ref, zl_ref, places_ref, pick_ref, tokens_out, grads_out, own_out, other_out,
    route_out, rows_out, d_result_out, inner_out, d_both_out, gated_out,
    route_ref, rows_ref, d_result_ref, inner_ref, d_both_ref, gated_ref,
    gate_ref, weight_ref, token_ref, grad_ref, back_ref, weight_here, token_here, grad_here, left, route_left,
):
    width = weight_ref.shape[1]
    part = width // 2
    deep = weight_ref.shape[2] // 3

    def token_move(source):
        token = tokens_out.at[places_ref[source]]
        return pltpu.make_async_copy(token, token_ref.at[source], token_here.at[source])

    def weight_move(e, place):
        block = (zl_ref[0] + place) % 2
        source = (own_out, other_out)[place].at[:, pl.ds(pl.multiple_of(e * 3 * deep, 3 * deep), 3 * deep)]
        target = weight_ref.at[e, pl.ds(pl.multiple_of(block * part, part), part), :]
        return pltpu.make_async_copy(source, target, weight_here.at[e, place])

    def leave(e, place):
        source, target = ((d_result_ref, d_result_out), (inner_ref, inner_out), (d_both_ref, d_both_out),
                          (gated_ref, gated_out), (rows_ref, rows_out))[place]
        return pltpu.make_async_copy(source.at[e], target.at[e], left.at[e, place])

    def route_leave(source):
        kept = route_ref if number == 1 else back_ref
        return pltpu.make_async_copy(kept.at[source], route_out.at[places_ref[source]], route_left.at[source])

    grads = []
    for source in range(8):
        grad = grads_out.at[places_ref[source] % 4, source // 4, :, :width]
        grads.append(pltpu.make_async_copy(grad, grad_ref.at[source], grad_here.at[source]))
    for source in range(8):
        token_move(source).start()
    for move in grads:
        move.start()
    for e in range(2):
        for place in range(2):
            weight_move(e, place).start()
    for move in grads:
        move.wait()
    lane = lax.broadcasted_iota(jnp.int32, (SLOTS, 128), 1)

    def gather(source, carry):
        token_move(source).wait()
        pick = pick_ref[number * 8 + places_ref[source]]
        rows = dot(pick, token_ref[source])
        cotangent = dot(pick, grad_ref[source])
        here = pl.ds(pl.multiple_of(source * SLOTS, SLOTS), SLOTS)
        for e in range(2):
            part = slice(e * SLOTS, (e + 1) * SLOTS)
            rows_ref[e, here, :] = rows[part, :width].astype(BF16)
            d_result_ref[e, here, :] = cotangent[part].astype(BF16)
            mine = (lane % EXPERTS == expert_ref[0] + e) & (lane < 3 * EXPERTS)
            gate = jnp.sum(jnp.where(mine, rows[part, width:], 0.0), axis=1, keepdims=True)
            gate_ref[e, here, :] = jnp.broadcast_to(gate, (SLOTS, 128))
        return carry

    lax.fori_loop(0, 8, gather, 0)
    lane = lax.broadcasted_iota(jnp.int32, (8 * SLOTS, 128), 1)

    def visit(e, carry):
        leave(e, 4).start()
        weight_move(e, 0).wait()
        weight_move(e, 1).wait()
        both = dot(rows_ref[e], weight_ref[e, :, : 2 * deep])
        a, b = both[:, :deep], both[:, deep:]
        sigma = 1.0 / (1.0 + jnp.exp(-a))
        inner = (a * sigma * b).astype(BF16)
        inner_ref[e] = inner
        down = weight_ref[e, :, 2 * deep :]
        result = dot(inner, down, NT).astype(BF16).astype(F32)
        gate = gate_ref[e, :, 0:1]
        cotangent = d_result_ref[e].astype(F32)
        gate_grad = jnp.sum(cotangent * result, axis=1, keepdims=True)
        gated_ref[e] = (gate * result).astype(BF16)
        d_result = (gate * cotangent).astype(BF16)
        d_result_ref[e] = d_result
        d_inner = dot(d_result, down)
        d_both_ref[e, :, :deep] = (d_inner * b * sigma * (1.0 + a * (1.0 - sigma))).astype(BF16)
        d_both_ref[e, :, deep:] = (d_inner * a * sigma).astype(BF16)
        for place in range(4):
            leave(e, place).start()
        d_rows = dot(d_both_ref[e], weight_ref[e, :, : 2 * deep], NT).astype(BF16)
        high = gate_grad.astype(BF16).astype(F32)
        low = gate_grad - high
        expert = expert_ref[0] + e
        tail = jnp.where(lane == expert, high, 0.0) + jnp.where(lane == expert + EXPERTS, low, 0.0)
        tail = tail.astype(BF16)
        here = pl.ds(pl.multiple_of(e * SLOTS, SLOTS), SLOTS)
        for source in range(8):
            part = slice(source * SLOTS, (source + 1) * SLOTS)
            back_ref[source, here, :width] = d_rows[part]
            back_ref[source, here, width:] = tail[part]
        return carry

    lax.fori_loop(0, 2, visit, 0)

    def scatter(source, carry):
        if number == 1:
            pick = pick_ref[8 + places_ref[source]]
            route_ref[source] = dot(pick, back_ref[source], TN).astype(BF16)
        route_leave(source).start()
        return carry

    lax.fori_loop(0, 8, scatter, 0)
    for e in range(2):
        for place in range(5):
            leave(e, place).wait()
    for source in range(8):
        route_leave(source).wait()


def join_kernel(pick_ref, back_out, passed_out, before_ref, sum_out, back_ref, passed_ref, sum_ref, arrived, left):
    moves = []
    for source in range(8):
        moves.append(pltpu.make_async_copy(back_out.at[source], back_ref.at[source], arrived.at[0, source]))
        moves.append(pltpu.make_async_copy(passed_out.at[source], passed_ref.at[source], arrived.at[1, source]))
    for move in moves:
        move.start()
    leaving = []
    for source in range(8):
        moves[2 * source].wait()
        moves[2 * source + 1].wait()
        sums = dot(pick_ref[source], back_ref[source], TN)
        sum_ref[source] = (sums + passed_ref[source].astype(F32)).astype(BF16)
        leaving.append(pltpu.make_async_copy(sum_ref.at[source], sum_out.at[source], left.at[source]))
        leaving[-1].start()
    for move in leaving:
        move.wait()


def expert_grads_kernel(number, zl_ref, *refs):
    outside, grads_out, inside, grads_ref, arrived, left = refs[:8], refs[9], refs[10:18], *refs[18:21]
    deep = inside[2].shape[2]
    part = inside[0].shape[2]
    columns = pl.ds(pl.multiple_of((zl_ref[0] + number) % 2 * part, part), part)
    moves = []
    for e in range(2):
        for n in range(8):
            source = outside[n].at[e, :, columns] if n % 4 < 2 else outside[n].at[e]
            moves.append(pltpu.make_async_copy(source, inside[n].at[e], arrived.at[e, n]))
            moves[-1].start()
    halves = (inside[:4], inside[4:])
    leaving = []
    for e in range(2):
        base = e * 3 * deep
        for move in moves[8 * e : 8 * e + 8]:
            move.wait()
        both = sum(dot(rows[e], d_both[e], TN) for rows, d_result, inner, d_both in halves)
        grads_ref[:, base : base + 2 * deep] = both.astype(BF16)
        down = sum(dot(d_result[e], inner[e], TN) for rows, d_result, inner, d_both in halves)
        grads_ref[:, base + 2 * deep : base + 3 * deep] = down.astype(BF16)
        wide = slice(base, base + 3 * deep)
        leaving.append(pltpu.make_async_copy(grads_ref.at[:, wide], grads_out.at[:, wide], left.at[e]))
        leaving[-1].start()
    for move in leaving:
        move.wait()


def outputs_kernel(number, place_ref, pick_ref, *refs):
    gated_out, (gated_ref, sum_ref, arrived, left) = refs[0], refs[-4:]
    sums_out = refs[6:10] if number == 0 else refs[2:6]
    moves = [pltpu.make_async_copy(gated_out, gated_ref, arrived.at[8])]
    if number == 0:
        passed_out, passed_ref = refs[1:5], refs[10]
        for piece in range(8):
            source = passed_out[piece % 4].at[piece // 4]
            moves.append(pltpu.make_async_copy(source, passed_ref.at[piece], arrived.at[piece]))
    for move in moves:
        move.start()
    moves[0].wait()
    leaving = []
    for piece in range(8):
        here = slice(piece * SLOTS, (piece + 1) * SLOTS)
        both = jnp.concatenate([gated_ref[0, here, :], gated_ref[1, here, :]], axis=0)
        sums = dot(pick_ref[number * 8 + place_ref[piece]], both, TN)
        if number == 0:
            moves[1 + piece].wait()
            sums += passed_ref[piece].astype(F32)
        sum_ref[piece] = sums.astype(BF16)
        target = sums_out[piece % 4].at[piece // 4]
        leaving.append(pltpu.make_async_copy(sum_ref.at[piece], target, left.at[piece]))
        leaving[-1].start()
    for move in leaving:
        move.wait()


SMEM = pl.BlockSpec(memory_space=pltpu.SMEM)
VMEM = pl.BlockSpec(memory_space=pltpu.VMEM)
HBM = pl.BlockSpec(memory_space=pltpu.HBM)


def kernel_call(kernel, micros, scalars, arrays, outside, outs, outs_outside, scratch, limit=60):
    shapes = [jax.ShapeDtypeStruct(shape, kind) for shape, kind in (*outs, *outs_outside)]
    return pl.pallas_call(
        kernel,
        in_specs=[SMEM] * len(scalars) + [VMEM] * len(arrays) + [HBM] * len(outside),
        out_specs=[VMEM] * len(outs) + [HBM] * len(outs_outside),
        out_shape=shapes,
        scratch_shapes=scratch,
        compiler_params=pltpu.CompilerParams(vmem_limit_bytes=limit * 1024 * 1024),
        cost_estimate=pl.CostEstimate(flops=int(micros * 1.1e9) + 1, bytes_accessed=1, transcendentals=0),
    )(*scalars, *arrays, *outside)


def keep(*shape, kind=BF16):
    return pltpu.VMEM(shape, kind)


def arrivals(*shape):
    return pltpu.SemaphoreType.DMA(shape)


def experts_call(number, expert, zl_index, chip_places, pick, tokens, grads, weights_own, weights_other):
    chips, share, wide = tokens.shape
    width, total, deep = wide - SIDE, chips * SLOTS, weights_own.shape[1] // 6
    route = (chips, share, wide) if number == 1 else (chips, 2 * SLOTS, wide)
    shapes = [(2, total, width), (2, total, width), (2, total, deep), (2, total, 2 * deep), (2, total, width)]
    return kernel_call(
        functools.partial(experts_kernel, number), 0, [expert, zl_index, chip_places], [pick],
        [tokens, grads, weights_own, weights_other],
        [], [(shape, BF16) for shape in [route] + shapes],
        [keep(*shape) for shape in [route] + shapes]
        + [keep(2, total, 128, kind=F32), keep(2, width, 3 * deep), keep(chips, share, wide)]
        + [keep(chips, share, width), keep(chips, 2 * SLOTS, wide)]
        + [arrivals(2, 2), arrivals(8), arrivals(8), arrivals(2, 5), arrivals(8)],
    )


def grads_call(number, zl_index, near, far, before):
    two, total, width = near[0].shape
    half, deep = width // 2, near[2].shape[2]
    columns = [(2, total, half), (2, total, half), (2, total, deep), (2, total, 2 * deep)]
    return kernel_call(
        functools.partial(expert_grads_kernel, number), 0, [zl_index], [], [*near[:4], *far[:4], before],
        [], [((half, 6 * deep), BF16)],
        [keep(*shape) for shape in columns * 2] + [keep(half, 6 * deep), arrivals(2, 8), arrivals(2)],
    )[0]


def on_device(
    hidden, doc_lengths, expert_ids, attn_gain, w_query, key_projection, w_value, w_out,
    moe_gain, w_router, w_gate, w_up, w_down, out_grad,
):
    share, width = hidden.shape[1], hidden.shape[2]
    ctx, chips, peers = 8, 8, 16
    row = share * ctx
    wide, half = width + SIDE, width // 2
    local, deep = w_gate.shape[0], w_gate.shape[2]
    zl, y, zh, x, core = (lax.axis_index(name) for name in ("zl", "y", "zh", "x", "core"))
    expert = (((zh * 4 + x) * 2 + core) * local).astype(jnp.int32)[None]
    core_index = core.astype(jnp.int32)[None]
    zl_index = zl.astype(jnp.int32)[None]
    ctx_places = jnp.stack([(zl + d) % 2 * 4 + (y + s) % 4 for d in range(2) for s in STEPS]).astype(jnp.int32)
    chip_places = jnp.stack([(zh + d) % 2 * 4 + (x + s) % 4 for d in range(2) for s in STEPS]).astype(jnp.int32)
    members = [((x + s) % 4 * 2 + (core + d) % 2) for d in range(2) for s in STEPS]
    members = jnp.stack(members).astype(jnp.int32)

    lanes = jnp.arange(128, dtype=jnp.int32)
    chosen = jnp.any(expert_ids[0][:, :, None] == lanes[None, None, :], axis=1)
    grad_rows = jnp.concatenate([out_grad[0], chosen.astype(BF16)], axis=1)
    grad_beside = pass_on(grad_rows, "zh", 1)

    (sent,) = kernel_call(
        pack_kernel, 2, [members],
        [w_query, key_projection, w_value, w_router, attn_gain[None], moe_gain[None], hidden[0], w_out], [],
        [((ctx, 304 + 9 * share, 128), BF16)], [], [],
    )
    got = exchange(sent, CTX)
    (grad_pair,) = kernel_call(
        pair_kernel, 0, [], [grad_rows, grad_beside], [sent], [((2, share, wide), BF16)], [], [],
    )
    grads = lax.all_gather(grad_pair, "x", axis=0, tiled=False)

    (packed,) = kernel_call(
        pack_weights_kernel, 0, [], [w_gate, w_up, w_down], [sent], [((share, 6 * deep), BF16)], [], [],
    )
    weights_own = lax.all_gather(packed, "y", axis=0, tiled=True)
    got, packed_other = together(got, packed)
    packed_other = pass_on(packed_other, "zl", 1)
    out_blocks = ring_blocks(got[:, 304 + 8 * share :], "x")

    ends = jnp.cumsum(doc_lengths[0]).astype(jnp.int32)
    freq = THETA ** (-(np.arange(HEAD // 2, dtype=np.float32) * 2.0 / HEAD))
    angle = np.arange(row, dtype=np.float32)[:, None] * freq[None, :].astype(np.float32)
    cosine, sine = np.cos(angle), np.sin(angle)
    table = jnp.asarray(np.concatenate([cosine] * 4 + [-sine, sine, -sine, sine], axis=1).astype(np.float32))

    mixed, small, normed, query, key, value, weight = kernel_call(
        attend_kernel, 8, [ends], [got], [table],
        [((row, 128), BF16), ((48, width), BF16)],
        [((row, width), BF16)] + [((row, 128), BF16)] * 3 + [((width, 256), BF16)],
        [keep(row, width)] + [keep(row, 128)] * 3 + [keep(width, 256), arrivals(5)]
        + [keep(row, 256, kind=F32), arrivals()],
    )
    mixed_rows, packed_other = together(exchange(mixed.reshape(ctx, share, 128), CTX), packed_other)
    weights_other = lax.all_gather(packed_other, "y", axis=0, tiled=True)
    mixed, *out_blocks = together(mixed, *out_blocks)
    out_own = jnp.stack(out_blocks)
    out_other = pass_on(out_own, "core", 1)
    middle, gates, mixed_rows, tokens = kernel_call(
        route_kernel, 4, [members], [mixed_rows, out_own, out_other, hidden[0], small, grad_rows], [],
        [((share, width), F32), ((share, 128), F32), ((share, width), BF16)], [((chips, share, wide), BF16)],
        [keep(share, wide), keep(share, width, kind=F32), arrivals(8)],
    )
    tokens, grads = together(tokens, grads)
    grads_far = pass_on(grads, "core", 1)
    (pick,) = kernel_call(
        pick_kernel, 0, [expert, chip_places], [], [grads, grads_far], [((peers, 2 * SLOTS, share), BF16)], [],
        [keep(peers, share, SIDE), arrivals(16)],
    )
    tokens_near, pick = together(exchange(tokens, CHIP), pick)
    tokens_far = pass_on(tokens_near, "core", 1)

    total = chips * SLOTS

    common = (expert, zl_index, chip_places, pick)
    back_near, *near = experts_call(0, *common, tokens_near, grads, weights_own, weights_other)
    *near, tokens_far = together(*near, tokens_far)
    route_far, *far = experts_call(1, *common, tokens_far, grads_far, weights_own, weights_other)
    route_passed = pass_on(route_far, "core", 1)
    grads_other = grads_call(1, zl_index, near, far, route_far)
    sums_other = lax.psum_scatter(grads_other, "y", scatter_dimension=0, tiled=True)
    out_far = kernel_call(
        functools.partial(outputs_kernel, 1), 0, [chip_places], [pick], [far[4], grads_other],
        [], [((2, share, width), BF16)] * 4,
        [keep(2, total, width), keep(chips, share, width), arrivals(9), arrivals(8)],
    )
    (route_sums,) = kernel_call(
        join_kernel, 0, [], [pick], [back_near, route_passed, out_far[0]], [], [((chips, share, wide), BF16)],
        [keep(chips, 2 * SLOTS, wide), keep(chips, share, wide), keep(chips, share, wide), arrivals(2, 8), arrivals(8)],
        limit=16,
    )
    grads_own = grads_call(0, zl_index, near, far, route_sums)
    out_sums = kernel_call(
        functools.partial(outputs_kernel, 0), 0, [chip_places], [pick],
        [near[4], *[pass_on(block, "core", 1) for block in out_far], route_sums], [], [((2, share, width), BF16)] * 4,
        [keep(chips, share, width), keep(2, total, width), keep(chips, share, width), arrivals(9), arrivals(8)],
    )
    route_sums, grads_own, *out_sums = together(exchange(route_sums, CHIP), grads_own, *out_sums)
    sums_own = lax.psum_scatter(grads_own, "y", scatter_dimension=0, tiled=True)

    d_mixed, early_mine, early_others, d_middle = kernel_call(
        unroute_kernel, 4, [members], [],
        [route_sums, middle, gates, grad_rows, tokens, small, out_own, out_other, mixed_rows],
        [((ctx, share, 128), BF16)] + [((row, half + 128), BF16)] * 2 + [((share, width), F32)], [],
        [keep(share, width, kind=F32), keep(share, 128, kind=F32), keep(share, wide), keep(share, wide)]
        + [keep(48, width), keep(4, ctx, 128, 128), keep(4, ctx, 128, 128), keep(share, width), arrivals(8)]
        + [keep(chips, share, wide), arrivals(8), keep(share, width)],
    )
    early_passed = pass_on(early_others, "core", 1)
    out_blocks = ring_blocks_out(out_sums, "x")
    d_mixed, early_passed = together(exchange(d_mixed, CTX), early_passed)
    (early,) = kernel_call(
        add_kernel, 0, [], [early_mine, early_passed], [], [((row, 640), BF16)], [], [], limit=16,
    )
    early, d_mixed = together(early, d_mixed)
    d_mixed = d_mixed.reshape(row, 128)
    passed = pass_on(sums_other, "zl", 1)
    late_mine, late_others, *d_normed_part = kernel_call(
        attend_back_kernel, 11, [ends, ctx_places, core_index], [d_mixed],
        [query, key, value, table, normed, weight, early],
        [((row, 128), BF16)] * 2, [((2, share, width), BF16)] * 4,
        [keep(row, 128, kind=F32), keep(row, 128, kind=F32), keep(row, 256), keep(width, 256, kind=F32)]
        + [keep(4, 2, share, width), arrivals(4, 2)]
        + [keep(row, 128)] * 3 + [keep(row, 256, kind=F32), keep(row, width), keep(width, 256), arrivals(6)],
    )

    early = exchange(early.reshape(ctx * chips, 16, 640), CTX + CHIP)
    late_passed = pass_on(late_others, "core", 1)
    (late,) = kernel_call(
        late_kernel, 0, [], [late_mine, late_passed], [early, *out_blocks[1:]], [((row, 128), BF16)], [], [], limit=16,
    )
    late = exchange(late.reshape(ctx * chips, 16, 128), CTX + CHIP)
    out_sums, out_other = kernel_call(
        add_four_kernel, 0, [], out_blocks[1:], [out_blocks[0]], [((share, width), BF16)] * 2, [],
        [keep(2, share, width), arrivals()], limit=16,
    )
    (output,) = kernel_call(
        output_kernel, 0, [], [out_sums, pass_on(out_other, "zh", 1), middle], [],
        [((share, width), BF16)], [], [], limit=16,
    )
    gate_sum, up_sum, down_sum = kernel_call(
        expert_sums_kernel, 0, [], [sums_own, passed], [],
        [((local, 128, deep), F32)] * 2 + [((local, deep, 128), F32)], [], [], limit=16,
    )
    (sums,) = kernel_call(
        reduce_kernel, 0, [], [early, late], [gate_sum], [((peers, 16, 1664), BF16)], [], [keep(16, 1664)], limit=16,
    )
    d_normed_blocks = ring_blocks_out(d_normed_part, "y")
    d_normed_near, d_normed_other = kernel_call(
        add_four_kernel, 0, [], d_normed_blocks[1:], [d_normed_part[0]], [((share, width), BF16)] * 2, [],
        [keep(2, share, width), arrivals()], limit=16,
    )
    (hidden_grad,) = kernel_call(
        hidden_grad_kernel, 0, [],
        [d_normed_near, pass_on(d_normed_other, "zl", 1), d_middle, hidden[0], small], [],
        [((share, width), F32)], [], [], limit=16,
    )
    sums, gate_sum, up_sum, down_sum, hidden_grad, output = together(
        exchange(sums, EP), gate_sum, up_sum, down_sum, hidden_grad, output
    )
    query_grad, key_grad, value_grad, out_weight_grad, attn_gain_grad, moe_gain_grad, router_grad = kernel_call(
        finish_kernel, 3, [], [sums, w_query, key_projection, w_value, attn_gain[None]], [],
        [((128, width), F32), ((128, half), F32), ((128, half), F32), ((128, width), F32)]
        + [((1, 128), F32), ((1, 128), F32), ((EXPERTS, 128), F32)], [], [], limit=16,
    )
    return (
        output[None], hidden_grad[None], attn_gain_grad[0], query_grad, key_grad, value_grad,
        out_weight_grad, moe_gain_grad[0], router_grad, gate_sum, up_sum, down_sum,
    )


def solution(mesh):
    axes = ("zl", "y", "zh", "x", "core")
    inner = Mesh(mesh.devices.reshape(2, 4, 2, 4, 2), axes)
    in_specs = (
        P(EP, CTX, None), P(EP, None), P(EP, CTX, None), P(CTX), P(CTX, None), P(CTX, None),
        P(CTX, None), P(CTX, None), P(CTX), P(None, CTX), P(EP, CTX, None), P(EP, CTX, None),
        P(EP, None, CTX), P(EP, CTX, None),
    )
    out_specs = (
        P(EP, CTX, None), P(EP, CTX, None), P(CTX), P(CTX, None), P(CTX, None), P(CTX, None),
        P(CTX, None), P(CTX), P(None, CTX), P(EP, CTX, None), P(EP, CTX, None), P(EP, None, CTX),
    )
    return jax.shard_map(on_device, mesh=inner, in_specs=in_specs, out_specs=out_specs, check_vma=False)
```

```python
import functools

import jax
import jax.numpy as jnp
import numpy as np
from jax import lax
from jax.experimental import pallas as pl
from jax.experimental.pallas import tpu as pltpu
from jax.sharding import Mesh, PartitionSpec as P

EPS = 1e-05
THETA = 10000.0
MASKED = -1e30
HEAD = 64
SCALE = 0.125
TILE = 256
SLOTS = 48
EXPERTS = 32
F32 = jnp.float32
BF16 = jnp.bfloat16
CTX = ("zl", "y")
CHIP = ("zh", "x")
EP = ("zh", "x", "core")
SIDE = 128
NT = (((1,), (1,)), ((), ()))
TN = (((0,), (0,)), ((), ()))
STEPS = (0, -1, 1, 2)


def exchange(parts, axis):
    return lax.all_to_all(parts, axis, split_axis=0, concat_axis=0, tiled=True)


def spread(block, axis, count):
    return exchange(jnp.broadcast_to(block[None], (count,) + block.shape), axis)


def pass_on(block, axis, steps):
    size = lax.axis_size(axis)
    return lax.ppermute(block, axis, [(i, (i + steps) % size) for i in range(size)])


def together(*values):
    return lax.optimization_barrier(values)


def ring_blocks(block, ring):
    return [block] + [pass_on(block, ring, -steps) for steps in STEPS[1:]]


def ring_blocks_out(blocks, ring):
    return [blocks[0]] + [pass_on(block, ring, steps) for block, steps in zip(blocks[1:], STEPS[1:])]


def dot(left, right, dims=(((1,), (0,)), ((), ()))):
    return lax.dot_general(left, right, dims, preferred_element_type=F32)


def turn(block, cosine, sine):
    lane = lax.broadcasted_iota(jnp.int32, block.shape, 1)
    other = jnp.where(lane % HEAD < HEAD // 2, pltpu.roll(block, 96, 1), pltpu.roll(block, 32, 1))
    return block * cosine + other * sine


def pack_kernel(
    member_ref, query_ref, key_ref, value_ref, router_ref, gain_a_ref, gain_m_ref, hidden_ref, out_ref, sent_ref
):
    out_part = out_ref[:, pl.ds(pl.multiple_of(member_ref[0] * 128, 128), 128)]
    share = hidden_ref.shape[0]
    lane = lax.broadcasted_iota(jnp.int32, (share, 128), 1)
    row = lax.broadcasted_iota(jnp.int32, (16, 128), 0)
    gains = jnp.where(row == 0, gain_a_ref[...].astype(F32), 0.0)
    gains = jnp.where(row == 1, gain_m_ref[...].astype(F32), gains).astype(BF16)
    for peer in range(8):
        sent_ref[peer, :128, :] = query_ref[:, peer * 128 : (peer + 1) * 128]
        columns = slice(peer // 2 * 128, (peer // 2 + 1) * 128)
        key, value = key_ref[:, columns].astype(F32), value_ref[:, columns].astype(F32)
        if peer % 2 == 0:
            value = pltpu.roll(value, HEAD, 1)
        else:
            key = pltpu.roll(key, HEAD, 1)
        sent_ref[peer, 128:256, :] = jnp.where(lane < HEAD, key, value).astype(BF16)
        sent_ref[peer, 256:288, :] = router_ref[...]
        sent_ref[peer, 288:304, :] = gains
        for block in range(8):
            start = 304 + block * share
            sent_ref[peer, start : start + share, :] = hidden_ref[:, block * 128 : (block + 1) * 128]
        sent_ref[peer, 304 + 8 * share :, :] = out_part


def expert_sums_kernel(own_ref, passed_ref, gate_ref, up_ref, down_ref):
    deep = gate_ref.shape[2]
    for e in range(2):
        for place, target in enumerate((gate_ref, up_ref, down_ref)):
            columns = slice((e * 3 + place) * deep, (e * 3 + place + 1) * deep)
            sums = own_ref[:, columns].astype(F32) + passed_ref[:, columns].astype(F32)
            target[e] = sums.T if place == 2 else sums


def document_start(ends_ref, place):
    start = jnp.zeros_like(place)
    for document in range(3):
        end = ends_ref[document]
        start = jnp.where(place >= end, end, start)
    return start


def attend_kernel(
    ends_ref, got_ref, angles_ref,
    mixed_ref, small_ref, *refs,
):
    outside, kept, sent, table_ref, arrived = refs[:5], refs[5:10], refs[10], refs[11], refs[12]
    fetch = pltpu.make_async_copy(angles_ref, table_ref, arrived)
    fetch.start()
    normed_ref, query_ref, key_ref, value_ref, weight_ref = kept
    moves = [pltpu.make_async_copy(kept[n], outside[n], sent.at[n]) for n in range(5)]
    count = normed_ref.shape[0]
    share = count // 8
    for block in range(8):
        rows = slice(block * 128, (block + 1) * 128)
        weight_ref[rows, :128] = got_ref[block, :128, :]
        weight_ref[rows, 128:] = got_ref[block, 128:256, :]
        small_ref[:, rows] = got_ref[block, 256:304, :]
    moves[4].start()
    fetch.wait()
    gain = small_ref[32:33, :].astype(F32)
    lane = lax.broadcasted_iota(jnp.int32, (share, 128), 1)
    low = lane < HEAD
    for piece in range(8):
        rows = slice(piece * share, (piece + 1) * share)
        x = jnp.concatenate(
            [got_ref[piece, 304 + block * share : 304 + (block + 1) * share, :] for block in range(8)], axis=1
        ).astype(F32)
        rho = lax.rsqrt(jnp.mean(x * x, axis=-1, keepdims=True) + EPS)
        normed = (x * rho * gain).astype(BF16)
        normed_ref[rows, :] = normed
        projected = dot(normed, weight_ref[...])
        cosine, sine = table_ref[rows, :128], table_ref[rows, 128:]
        pair = projected[:, 128:]
        turned = pltpu.roll(pair, HEAD, 1)
        query_ref[rows, :] = turn(projected[:, :128], cosine, sine).astype(BF16)
        key_ref[rows, :] = turn(jnp.where(low, pair, turned), cosine, sine).astype(BF16)
        value_ref[rows, :] = jnp.where(low, turned, pair).astype(BF16)
    for move in moves[:4]:
        move.start()
    lane = lax.broadcasted_iota(jnp.int32, (TILE, 128), 1)
    low = lane < HEAD
    for tile in range(count // TILE):
        rows = slice(tile * TILE, (tile + 1) * TILE)
        seen = (tile + 1) * TILE
        keys, values = key_ref[:seen, :], value_ref[:seen, :]
        place = tile * TILE + lax.broadcasted_iota(jnp.int32, (TILE, seen), 0)
        source = lax.broadcasted_iota(jnp.int32, (TILE, seen), 1)
        start = document_start(ends_ref, tile * TILE + lax.broadcasted_iota(jnp.int32, (TILE, 1), 0))
        allowed = (source <= place) & (source >= start)
        scaled = query_ref[rows, :] * jnp.asarray(SCALE, BF16)
        mixed = []
        for head in range(2):
            one = jnp.where(low == (head == 0), scaled, jnp.zeros_like(scaled))
            scores = jnp.where(allowed, dot(one, keys, NT), MASKED)
            weight = jnp.exp(scores - jnp.max(scores, axis=1, keepdims=True))
            probs = weight * (1.0 / jnp.sum(weight, axis=1, keepdims=True))
            mixed.append(dot(probs.astype(BF16), values))
        mixed_ref[rows, :] = jnp.where(low, mixed[0], mixed[1]).astype(BF16)
    for move in moves:
        move.wait()


def attend_back_kernel(
    ends_ref, index_ref, core_ref, d_mixed_ref, *refs,
):
    outside, (mine_ref, others_ref), d_normed_out = refs[:6], refs[7:9], refs[9:13]
    key_sum, value_sum, pre_ref, grad_ref, d_normed_ref, left = refs[13:19]
    inside, arrived = refs[19:25], refs[25]
    query_ref, key_ref, value_ref, table_ref, normed_ref, weight_ref = inside
    moves = [pltpu.make_async_copy(outside[n], inside[n], arrived.at[n]) for n in range(6)]
    for move in moves:
        move.start()
    count = query_ref.shape[0]
    lane = lax.broadcasted_iota(jnp.int32, (TILE, 128), 1)
    low = lane < HEAD
    key_sum[...] = jnp.zeros_like(key_sum)
    value_sum[...] = jnp.zeros_like(value_sum)
    for move in moves[:4]:
        move.wait()
    for tile in range(count // TILE):
        rows = slice(tile * TILE, (tile + 1) * TILE)
        seen = (tile + 1) * TILE
        keys, values = key_ref[:seen, :], value_ref[:seen, :]
        place = tile * TILE + lax.broadcasted_iota(jnp.int32, (seen, TILE), 1)
        source = lax.broadcasted_iota(jnp.int32, (seen, TILE), 0)
        start = document_start(ends_ref, tile * TILE + lax.broadcasted_iota(jnp.int32, (1, TILE), 1))
        allowed = (source <= place) & (source >= start)
        scaled = query_ref[rows, :] * jnp.asarray(SCALE, BF16)
        d_mixed = d_mixed_ref[rows, :]
        d_query = []
        for head in range(2):
            mine = low == (head == 0)
            one = jnp.where(mine, scaled, jnp.zeros_like(scaled))
            d_one = jnp.where(mine, d_mixed, jnp.zeros_like(d_mixed))
            scores = jnp.where(allowed, dot(keys, one, NT), MASKED)
            weight = jnp.exp(scores - jnp.max(scores, axis=0, keepdims=True))
            probs = weight * (1.0 / jnp.sum(weight, axis=0, keepdims=True))
            d_probs = dot(values, d_one, NT)
            delta = jnp.sum(probs * d_probs, axis=0, keepdims=True)
            d_scores = (probs * (d_probs - delta)).astype(BF16)
            key_sum[:seen, :] += dot(d_scores, one)
            value_sum[:seen, :] += dot(probs.astype(BF16), d_one)
            d_query.append(dot(d_scores, keys, TN) * SCALE)
        d_query = jnp.where(low, d_query[0], d_query[1])
        pre_ref[rows, :128] = turn(d_query, table_ref[rows, :128], -table_ref[rows, 128:]).astype(BF16)
    for tile in range(count // TILE):
        rows = slice(tile * TILE, (tile + 1) * TILE)
        d_key, d_value = key_sum[rows, :], value_sum[rows, :]
        d_key = turn(d_key + pltpu.roll(d_key, HEAD, 1), table_ref[rows, :128], -table_ref[rows, 128:])
        d_value = d_value + pltpu.roll(d_value, HEAD, 1)
        pre_ref[rows, 128:] = jnp.where(low, d_key, d_value).astype(BF16)
    moves[4].wait()
    moves[5].wait()
    share = d_normed_ref.shape[2]
    leaving = []
    for piece in (4, 5, 6, 7, 0, 1, 2, 3):
        rows = pl.ds(pl.multiple_of(index_ref[piece] * share, share), share)
        pair, place = piece // 4, piece % 4
        d_normed_ref[place, pair] = dot(pre_ref[rows, :], weight_ref[...], NT).astype(BF16)
        leaving.append(
            pltpu.make_async_copy(d_normed_ref.at[place, pair], d_normed_out[place].at[pair], left.at[place, pair])
        )
        leaving[-1].start()
    grad_ref[...] = dot(normed_ref[...], pre_ref[...], TN)
    for number, target in enumerate((mine_ref, others_ref)):
        member = (core_ref[0] + number) % 2
        for block in range(count // 16):
            rows = grad_ref[pl.ds(pl.multiple_of(block * 16 + member * 8, 8), 8), :]
            rows = jnp.concatenate([rows[:, :128], rows[:, 128:]], axis=0)
            target[block * 16 : (block + 1) * 16, :] = rows.astype(BF16)
    for move in leaving:
        move.wait()


def router_rows(small_ref):
    rows = small_ref[:EXPERTS, :]
    return jnp.concatenate([rows, jnp.zeros((128 - EXPERTS, rows.shape[1]), BF16)], axis=0)


def route_kernel(
    member_ref, mixed_ref, own_ref, other_ref, hidden_ref, small_ref, grad_ref,
    middle_ref, gates_ref, mixed_rows, tokens_out, token_ref, branch_ref, left,
):
    width = hidden_ref.shape[1]
    for block in range(8):
        mixed_rows[:, block * 128 : (block + 1) * 128] = mixed_ref[block]
    for place in range(8):
        columns = pl.ds(pl.multiple_of(member_ref[place] * 128, 128), 128)
        weight = (own_ref if place < 4 else other_ref)[place % 4].reshape(width, 128)
        branch_ref[:, columns] = dot(mixed_rows[...], weight)
    middle = hidden_ref[...].astype(F32) + branch_ref[...]
    middle_ref[...] = middle
    rho = lax.rsqrt(jnp.mean(middle * middle, axis=-1, keepdims=True) + EPS)
    routed = (middle * rho * small_ref[33:34, :].astype(F32)).astype(BF16)
    token_ref[:, :width] = routed
    logits = dot(routed, router_rows(small_ref), NT)
    logits = jnp.where(grad_ref[:, width:].astype(F32) > 0.5, logits, MASKED)
    raised = jnp.exp(logits - jnp.max(logits, axis=1, keepdims=True))
    gates = raised / jnp.sum(raised, axis=1, keepdims=True)
    gates_ref[...] = gates
    high = gates.astype(BF16).astype(F32)
    rest = gates - high
    middle_part = rest.astype(BF16).astype(F32)
    last = (rest - middle_part).astype(BF16).astype(F32)
    tail = high + pltpu.roll(middle_part, EXPERTS, 1) + pltpu.roll(last, 2 * EXPERTS, 1)
    token_ref[:, width:] = tail.astype(BF16)
    leaving = [pltpu.make_async_copy(token_ref, tokens_out.at[chip], left.at[chip]) for chip in range(8)]
    for move in leaving:
        move.start()
    for move in leaving:
        move.wait()


def unroute_kernel(
    member_ref, home_out, *refs,
):
    outside, (d_mixed_ref, mine_ref, others_ref, d_middle_ref) = refs[:8], refs[8:12]
    inside, arrived, home_ref, home_arrived, branch_ref = refs[12:20], *refs[20:24]
    middle_ref, gates_ref, grad_ref, token_ref, small_ref, own_ref, other_ref, mixed_ref = inside
    sources = [home_out.at[source] for source in range(8)]
    homes = [pltpu.make_async_copy(sources[n], home_ref.at[n], home_arrived.at[n]) for n in range(8)]
    moves = []
    for n in range(8):
        source = outside[n].at[0] if n == 3 else outside[n]
        moves.append(pltpu.make_async_copy(source, inside[n], arrived.at[n]))
    for move in homes + moves:
        move.start()
    width = middle_ref.shape[1]
    homes[0].wait()
    total = home_ref[0].astype(F32)
    for source in range(1, 8):
        homes[source].wait()
        total += home_ref[source].astype(F32)
    for move in moves[:5]:
        move.wait()
    tail = total[:, width:]
    lane = lax.broadcasted_iota(jnp.int32, tail.shape, 1)
    d_gates = jnp.where(lane < EXPERTS, tail + pltpu.roll(tail, 128 - EXPERTS, 1), 0.0)
    gates = gates_ref[...]
    d_logits = (gates * (d_gates - jnp.sum(gates * d_gates, axis=1, keepdims=True))).astype(BF16)
    d_routed = total[:, :width] + dot(d_logits, router_rows(small_ref))
    middle = middle_ref[...]
    rho = lax.rsqrt(jnp.mean(middle * middle, axis=-1, keepdims=True) + EPS)
    unit = middle * rho
    gain_part = jnp.sum(d_routed * unit, axis=0, keepdims=True)
    c = d_routed * small_ref[33:34, :].astype(F32)
    d_middle = grad_ref[:, :width].astype(F32) + rho * (c - unit * jnp.mean(c * unit, axis=-1, keepdims=True))
    d_middle_ref[...] = d_middle
    branch_ref[...] = d_middle.astype(BF16)
    for move in moves[5:]:
        move.wait()
    d_mixed = jnp.zeros((branch_ref.shape[0], width), F32)
    for place in range(8):
        columns = pl.ds(pl.multiple_of(member_ref[place] * 128, 128), 128)
        weight = (own_ref if place < 4 else other_ref)[place % 4].reshape(width, 128)
        d_mixed += dot(branch_ref[:, columns], weight, NT)
    d_mixed = d_mixed.astype(BF16)
    for block in range(8):
        d_mixed_ref[block] = d_mixed[:, block * 128 : (block + 1) * 128]
    router_part = dot(d_logits, token_ref[:, :width], TN)[:EXPERTS].astype(BF16)
    gain_rows = jnp.where(lax.broadcasted_iota(jnp.int32, (16, width), 0) == 0, gain_part, 0.0).astype(BF16)
    small_rows = jnp.concatenate([router_part, gain_rows], axis=0)
    row = lax.broadcasted_iota(jnp.int32, (128, 48), 0)
    column = lax.broadcasted_iota(jnp.int32, (128, 48), 1)
    for number, target in enumerate((mine_ref, others_ref)):
        member = (member_ref[0] + number) % 2
        half = pl.ds(pl.multiple_of(member * (width // 2), width // 2), width // 2)
        target[:, : width // 2] = dot(mixed_ref[...], branch_ref[:, half], TN).astype(BF16)
        place = row % 16
        wanted = jnp.where(place == 2, EXPERTS, jnp.where(place < 2, row // 16 * 4 + member * 2 + place, -1))
        choose = (wanted == column).astype(F32).astype(BF16)
        for block in range(8):
            rows = slice(block * 128, (block + 1) * 128)
            target[rows, width // 2 :] = dot(choose, small_rows[:, rows]).astype(BF16)


def add_kernel(mine_ref, passed_ref, sum_ref):
    sum_ref[...] = (mine_ref[...].astype(F32) + passed_ref[...].astype(F32)).astype(BF16)


def late_kernel(mine_ref, passed_ref, *refs):
    add_kernel(mine_ref, passed_ref, refs[-1])


def add_four_kernel(a_ref, b_ref, c_ref, part_out, sum_ref, other_ref, part_ref, arrived):
    move = pltpu.make_async_copy(part_out, part_ref, arrived)
    move.start()
    total = a_ref[...].astype(F32) + b_ref[...].astype(F32) + c_ref[...].astype(F32)
    move.wait()
    total = (total + part_ref[...].astype(F32)).astype(BF16)
    sum_ref[...] = total[0]
    other_ref[...] = total[1]


def hidden_grad_kernel(near_ref, passed_ref, d_middle_ref, hidden_ref, small_ref, grad_ref):
    x = hidden_ref[...].astype(F32)
    rho = lax.rsqrt(jnp.mean(x * x, axis=-1, keepdims=True) + EPS)
    unit = x * rho
    d_normed = near_ref[...].astype(F32) + passed_ref[...].astype(F32)
    c = d_normed * small_ref[32:33, :].astype(F32)
    grad_ref[...] = d_middle_ref[...] + rho * (c - unit * jnp.mean(c * unit, axis=-1, keepdims=True))


def output_kernel(near_ref, passed_ref, middle_ref, output_ref):
    total = middle_ref[...] + near_ref[...].astype(F32) + passed_ref[...].astype(F32)
    output_ref[...] = total.astype(BF16)


def reduce_kernel(early_ref, late_ref, a_ref, b_ref, c_ref, sums_ref, scratch):
    early = early_ref[0].astype(F32)
    for source in range(1, 64):
        early += early_ref[source].astype(F32)
    scratch[:, 1024:] = early.astype(BF16)
    for block in range(8):
        late = late_ref[block * 8].astype(F32)
        for source in range(1, 8):
            late += late_ref[block * 8 + source].astype(F32)
        scratch[:, block * 128 : (block + 1) * 128] = late.astype(BF16)
    for peer in range(16):
        sums_ref[peer] = scratch[...]


def finish_kernel(
    sums_ref, w_query_ref, w_key_ref, w_value_ref, gain_ref,
    query_ref, key_ref, value_ref, out_ref, gain_a_ref, gain_m_ref, router_ref,
):
    lane = lax.broadcasted_iota(jnp.int32, (8, 128), 1)
    low = lane < HEAD
    for peer in range(16):
        sums = sums_ref[peer].astype(F32)
        rows = slice(peer * 8, (peer + 1) * 8)
        query_ref[rows, :] = sums[:8, :1024]
        for pair in range(4):
            even = sums[8:, pair * 256 : pair * 256 + 128]
            odd = sums[8:, pair * 256 + 128 : (pair + 1) * 256]
            columns = slice(pair * 128, (pair + 1) * 128)
            key_ref[rows, columns] = jnp.where(low, even, pltpu.roll(odd, HEAD, 1))
            value_ref[rows, columns] = jnp.where(low, pltpu.roll(even, HEAD, 1), odd)
        columns = slice(peer % 2 * 512, (peer % 2 + 1) * 512)
        out_ref[peer // 2 * 16 : (peer // 2 + 1) * 16, columns] = sums[:, 1024:1536]
        router_ref[peer * 2 : peer * 2 + 2, :] = sums[0:2, 1536:]
        if peer == 0:
            gain_m_ref[...] = sums[2:3, 1536:]
    total = jnp.sum(w_query_ref[...].astype(F32) * query_ref[...], axis=1, keepdims=True)
    total += jnp.sum(w_key_ref[...].astype(F32) * key_ref[...], axis=1, keepdims=True)
    total += jnp.sum(w_value_ref[...].astype(F32) * value_ref[...], axis=1, keepdims=True)
    total = jnp.broadcast_to(total, (128, 128)).T
    gain_a_ref[...] = total[0:1, :] / gain_ref[...].astype(F32)


def pack_weights_kernel(gate_ref, up_ref, down_ref, before_ref, packed_ref):
    deep = gate_ref.shape[2]
    for e in range(2):
        base = e * 3 * deep
        packed_ref[:, base : base + deep] = gate_ref[e]
        packed_ref[:, base + deep : base + 2 * deep] = up_ref[e]
        packed_ref[:, base + 2 * deep : base + 3 * deep] = down_ref[e].T


def pair_kernel(mine_ref, beside_ref, before_ref, pair_ref):
    pair_ref[0] = mine_ref[...]
    pair_ref[1] = beside_ref[...]


def pick_kernel(expert_ref, place_ref, *refs):
    grads, pick_ref, flags_ref, arrived = refs[:2], *refs[2:]
    share = grads[0].shape[2]
    width = grads[0].shape[3] - 128
    fetches = []
    for piece in range(16):
        source = grads[piece // 8].at[place_ref[piece % 8] % 4, piece % 8 // 4, :, width:]
        fetches.append(pltpu.make_async_copy(source, flags_ref.at[piece], arrived.at[piece]))
        fetches[-1].start()
    row = lax.broadcasted_iota(jnp.int32, (16, 128), 0)
    lane = lax.broadcasted_iota(jnp.int32, (16, 128), 1)
    choose = ((lane == expert_ref[0] + row) & (row < 2)).astype(F32).astype(BF16)
    ahead = lax.broadcasted_iota(jnp.int32, (share, share), 0) < lax.broadcasted_iota(jnp.int32, (share, share), 1)
    ahead = ahead.astype(F32).astype(BF16)
    slot = lax.broadcasted_iota(jnp.int32, (SLOTS, share), 0).astype(F32)
    for fetch in fetches:
        fetch.wait()
    for piece in range(16):
        source = piece // 8 * 8 + place_ref[piece % 8]
        named = dot(choose, flags_ref[piece], NT)
        rank = dot(named.astype(BF16), ahead)
        for e in range(2):
            hit = (named[e : e + 1, :] > 0.5) & (rank[e : e + 1, :] == slot)
            pick_ref[source, e * SLOTS : (e + 1) * SLOTS, :] = hit.astype(F32).astype(BF16)


def experts_kernel(
    number, expert_ref, zl_ref, places_ref, pick_ref, tokens_out, grads_out, own_out, other_out,
    route_out, rows_out, d_result_out, inner_out, d_both_out, gated_out,
    route_ref, rows_ref, d_result_ref, inner_ref, d_both_ref, gated_ref,
    gate_ref, weight_ref, token_ref, grad_ref, back_ref, weight_here, token_here, grad_here, left, route_left,
):
    width = weight_ref.shape[1]
    part = width // 2
    deep = weight_ref.shape[2] // 3

    def token_move(source):
        token = tokens_out.at[places_ref[source]]
        return pltpu.make_async_copy(token, token_ref.at[source], token_here.at[source])

    def weight_move(e, place):
        block = (zl_ref[0] + place) % 2
        source = (own_out, other_out)[place].at[:, pl.ds(pl.multiple_of(e * 3 * deep, 3 * deep), 3 * deep)]
        target = weight_ref.at[e, pl.ds(pl.multiple_of(block * part, part), part), :]
        return pltpu.make_async_copy(source, target, weight_here.at[e, place])

    def leave(e, place):
        source, target = ((d_result_ref, d_result_out), (inner_ref, inner_out), (d_both_ref, d_both_out),
                          (gated_ref, gated_out), (rows_ref, rows_out))[place]
        return pltpu.make_async_copy(source.at[e], target.at[e], left.at[e, place])

    def route_leave(source):
        kept = route_ref if number == 1 else back_ref
        return pltpu.make_async_copy(kept.at[source], route_out.at[places_ref[source]], route_left.at[source])

    grads = []
    for source in range(8):
        grad = grads_out.at[places_ref[source] % 4, source // 4, :, :width]
        grads.append(pltpu.make_async_copy(grad, grad_ref.at[source], grad_here.at[source]))
    for source in range(8):
        token_move(source).start()
    for move in grads:
        move.start()
    for e in range(2):
        for place in range(2):
            weight_move(e, place).start()
    for move in grads:
        move.wait()
    lane = lax.broadcasted_iota(jnp.int32, (SLOTS, 128), 1)

    def gather(source, carry):
        token_move(source).wait()
        pick = pick_ref[number * 8 + places_ref[source]]
        rows = dot(pick, token_ref[source])
        cotangent = dot(pick, grad_ref[source])
        here = pl.ds(pl.multiple_of(source * SLOTS, SLOTS), SLOTS)
        for e in range(2):
            part = slice(e * SLOTS, (e + 1) * SLOTS)
            rows_ref[e, here, :] = rows[part, :width].astype(BF16)
            d_result_ref[e, here, :] = cotangent[part].astype(BF16)
            mine = (lane % EXPERTS == expert_ref[0] + e) & (lane < 3 * EXPERTS)
            gate = jnp.sum(jnp.where(mine, rows[part, width:], 0.0), axis=1, keepdims=True)
            gate_ref[e, here, :] = jnp.broadcast_to(gate, (SLOTS, 128))
        return carry

    lax.fori_loop(0, 8, gather, 0)
    lane = lax.broadcasted_iota(jnp.int32, (8 * SLOTS, 128), 1)

    def visit(e, carry):
        leave(e, 4).start()
        weight_move(e, 0).wait()
        weight_move(e, 1).wait()
        both = dot(rows_ref[e], weight_ref[e, :, : 2 * deep])
        a, b = both[:, :deep], both[:, deep:]
        sigma = 1.0 / (1.0 + jnp.exp(-a))
        inner = (a * sigma * b).astype(BF16)
        inner_ref[e] = inner
        down = weight_ref[e, :, 2 * deep :]
        result = dot(inner, down, NT).astype(BF16).astype(F32)
        gate = gate_ref[e, :, 0:1]
        cotangent = d_result_ref[e].astype(F32)
        gate_grad = jnp.sum(cotangent * result, axis=1, keepdims=True)
        gated_ref[e] = (gate * result).astype(BF16)
        d_result = (gate * cotangent).astype(BF16)
        d_result_ref[e] = d_result
        d_inner = dot(d_result, down)
        d_both_ref[e, :, :deep] = (d_inner * b * sigma * (1.0 + a * (1.0 - sigma))).astype(BF16)
        d_both_ref[e, :, deep:] = (d_inner * a * sigma).astype(BF16)
        for place in range(4):
            leave(e, place).start()
        d_rows = dot(d_both_ref[e], weight_ref[e, :, : 2 * deep], NT).astype(BF16)
        high = gate_grad.astype(BF16).astype(F32)
        low = gate_grad - high
        expert = expert_ref[0] + e
        tail = jnp.where(lane == expert, high, 0.0) + jnp.where(lane == expert + EXPERTS, low, 0.0)
        tail = tail.astype(BF16)
        here = pl.ds(pl.multiple_of(e * SLOTS, SLOTS), SLOTS)
        for source in range(8):
            part = slice(source * SLOTS, (source + 1) * SLOTS)
            back_ref[source, here, :width] = d_rows[part]
            back_ref[source, here, width:] = tail[part]
        return carry

    lax.fori_loop(0, 2, visit, 0)

    def scatter(source, carry):
        if number == 1:
            pick = pick_ref[8 + places_ref[source]]
            route_ref[source] = dot(pick, back_ref[source], TN).astype(BF16)
        route_leave(source).start()
        return carry

    lax.fori_loop(0, 8, scatter, 0)
    for e in range(2):
        for place in range(5):
            leave(e, place).wait()
    for source in range(8):
        route_leave(source).wait()


def join_kernel(pick_ref, back_out, passed_out, sum_out, back_ref, passed_ref, sum_ref, arrived, left):
    moves = []
    for source in range(8):
        moves.append(pltpu.make_async_copy(back_out.at[source], back_ref.at[source], arrived.at[0, source]))
        moves.append(pltpu.make_async_copy(passed_out.at[source], passed_ref.at[source], arrived.at[1, source]))
    for move in moves:
        move.start()
    leaving = []
    for source in range(8):
        moves[2 * source].wait()
        moves[2 * source + 1].wait()
        sums = dot(pick_ref[source], back_ref[source], TN)
        sum_ref[source] = (sums + passed_ref[source].astype(F32)).astype(BF16)
        leaving.append(pltpu.make_async_copy(sum_ref.at[source], sum_out.at[source], left.at[source]))
        leaving[-1].start()
    for move in leaving:
        move.wait()


def expert_grads_kernel(number, zl_ref, *refs):
    outside, grads_out, inside, grads_ref, arrived, left = refs[:8], refs[9], refs[10:18], *refs[18:21]
    deep = inside[2].shape[2]
    part = inside[0].shape[2]
    columns = pl.ds(pl.multiple_of((zl_ref[0] + number) % 2 * part, part), part)
    moves = []
    for e in range(2):
        for n in range(8):
            source = outside[n].at[e, :, columns] if n % 4 < 2 else outside[n].at[e]
            moves.append(pltpu.make_async_copy(source, inside[n].at[e], arrived.at[e, n]))
            moves[-1].start()
    halves = (inside[:4], inside[4:])
    leaving = []
    for e in range(2):
        base = e * 3 * deep
        for move in moves[8 * e : 8 * e + 8]:
            move.wait()
        both = sum(dot(rows[e], d_both[e], TN) for rows, d_result, inner, d_both in halves)
        grads_ref[:, base : base + 2 * deep] = both.astype(BF16)
        down = sum(dot(d_result[e], inner[e], TN) for rows, d_result, inner, d_both in halves)
        grads_ref[:, base + 2 * deep : base + 3 * deep] = down.astype(BF16)
        wide = slice(base, base + 3 * deep)
        leaving.append(pltpu.make_async_copy(grads_ref.at[:, wide], grads_out.at[:, wide], left.at[e]))
        leaving[-1].start()
    for move in leaving:
        move.wait()


def outputs_kernel(number, place_ref, pick_ref, *refs):
    gated_out, (gated_ref, sum_ref, arrived, left) = refs[0], refs[-4:]
    sums_out = refs[6:10] if number == 0 else refs[2:6]
    moves = [pltpu.make_async_copy(gated_out, gated_ref, arrived.at[8])]
    if number == 0:
        passed_out, passed_ref = refs[1:5], refs[10]
        for piece in range(8):
            source = passed_out[piece % 4].at[piece // 4]
            moves.append(pltpu.make_async_copy(source, passed_ref.at[piece], arrived.at[piece]))
    for move in moves:
        move.start()
    moves[0].wait()
    leaving = []
    for piece in range(8):
        here = slice(piece * SLOTS, (piece + 1) * SLOTS)
        both = jnp.concatenate([gated_ref[0, here, :], gated_ref[1, here, :]], axis=0)
        sums = dot(pick_ref[number * 8 + place_ref[piece]], both, TN)
        if number == 0:
            moves[1 + piece].wait()
            sums += passed_ref[piece].astype(F32)
        sum_ref[piece] = sums.astype(BF16)
        target = sums_out[piece % 4].at[piece // 4]
        leaving.append(pltpu.make_async_copy(sum_ref.at[piece], target, left.at[piece]))
        leaving[-1].start()
    for move in leaving:
        move.wait()


SMEM = pl.BlockSpec(memory_space=pltpu.SMEM)
VMEM = pl.BlockSpec(memory_space=pltpu.VMEM)
HBM = pl.BlockSpec(memory_space=pltpu.HBM)


def kernel_call(kernel, micros, scalars, arrays, outside, outs, outs_outside, scratch, limit=60):
    shapes = [jax.ShapeDtypeStruct(shape, kind) for shape, kind in (*outs, *outs_outside)]
    return pl.pallas_call(
        kernel,
        in_specs=[SMEM] * len(scalars) + [VMEM] * len(arrays) + [HBM] * len(outside),
        out_specs=[VMEM] * len(outs) + [HBM] * len(outs_outside),
        out_shape=shapes,
        scratch_shapes=scratch,
        compiler_params=pltpu.CompilerParams(vmem_limit_bytes=limit * 1024 * 1024),
        cost_estimate=pl.CostEstimate(flops=int(micros * 1.1e9) + 1, bytes_accessed=1, transcendentals=0),
    )(*scalars, *arrays, *outside)


def keep(*shape, kind=BF16):
    return pltpu.VMEM(shape, kind)


def arrivals(*shape):
    return pltpu.SemaphoreType.DMA(shape)


def experts_call(number, expert, zl_index, chip_places, pick, tokens, grads, weights_own, weights_other):
    chips, share, wide = tokens.shape
    width, total, deep = wide - SIDE, chips * SLOTS, weights_own.shape[1] // 6
    route = (chips, share, wide) if number == 1 else (chips, 2 * SLOTS, wide)
    shapes = [(2, total, width), (2, total, width), (2, total, deep), (2, total, 2 * deep), (2, total, width)]
    return kernel_call(
        functools.partial(experts_kernel, number), 0, [expert, zl_index, chip_places], [pick],
        [tokens, grads, weights_own, weights_other],
        [], [(shape, BF16) for shape in [route] + shapes],
        [keep(*shape) for shape in [route] + shapes]
        + [keep(2, total, 128, kind=F32), keep(2, width, 3 * deep), keep(chips, share, wide)]
        + [keep(chips, share, width), keep(chips, 2 * SLOTS, wide)]
        + [arrivals(2, 2), arrivals(8), arrivals(8), arrivals(2, 5), arrivals(8)],
    )


def grads_call(number, zl_index, near, far, before):
    two, total, width = near[0].shape
    half, deep = width // 2, near[2].shape[2]
    columns = [(2, total, half), (2, total, half), (2, total, deep), (2, total, 2 * deep)]
    return kernel_call(
        functools.partial(expert_grads_kernel, number), 0, [zl_index], [], [*near[:4], *far[:4], before],
        [], [((half, 6 * deep), BF16)],
        [keep(*shape) for shape in columns * 2] + [keep(half, 6 * deep), arrivals(2, 8), arrivals(2)],
    )[0]


def on_device(
    hidden, doc_lengths, expert_ids, attn_gain, w_query, key_projection, w_value, w_out,
    moe_gain, w_router, w_gate, w_up, w_down, out_grad,
):
    share, width = hidden.shape[1], hidden.shape[2]
    ctx, chips, peers = 8, 8, 16
    row = share * ctx
    wide, half = width + SIDE, width // 2
    local, deep = w_gate.shape[0], w_gate.shape[2]
    zl, y, zh, x, core = (lax.axis_index(name) for name in ("zl", "y", "zh", "x", "core"))
    expert = (((zh * 4 + x) * 2 + core) * local).astype(jnp.int32)[None]
    core_index = core.astype(jnp.int32)[None]
    zl_index = zl.astype(jnp.int32)[None]
    ctx_places = jnp.stack([(zl + d) % 2 * 4 + (y + s) % 4 for d in range(2) for s in STEPS]).astype(jnp.int32)
    chip_places = jnp.stack([(zh + d) % 2 * 4 + (x + s) % 4 for d in range(2) for s in STEPS]).astype(jnp.int32)
    members = [((x + s) % 4 * 2 + (core + d) % 2) for d in range(2) for s in STEPS]
    members = jnp.stack(members).astype(jnp.int32)

    lanes = jnp.arange(128, dtype=jnp.int32)
    chosen = jnp.any(expert_ids[0][:, :, None] == lanes[None, None, :], axis=1)
    grad_rows = jnp.concatenate([out_grad[0], chosen.astype(BF16)], axis=1)
    grad_beside = pass_on(grad_rows, "zh", 1)

    (sent,) = kernel_call(
        pack_kernel, 2, [members],
        [w_query, key_projection, w_value, w_router, attn_gain[None], moe_gain[None], hidden[0], w_out], [],
        [((ctx, 304 + 9 * share, 128), BF16)], [], [],
    )
    got = exchange(sent, CTX)
    (grad_pair,) = kernel_call(
        pair_kernel, 0, [], [grad_rows, grad_beside], [sent], [((2, share, wide), BF16)], [], [],
    )
    grads = lax.all_gather(grad_pair, "x", axis=0, tiled=False)

    (packed,) = kernel_call(
        pack_weights_kernel, 0, [], [w_gate, w_up, w_down], [sent], [((share, 6 * deep), BF16)], [], [],
    )
    weights_own = lax.all_gather(packed, "y", axis=0, tiled=True)
    packed_other = pass_on(packed, "zl", 1)
    out_blocks = ring_blocks(got[:, 304 + 8 * share :], "x")

    ends = jnp.cumsum(doc_lengths[0]).astype(jnp.int32)
    freq = THETA ** (-(np.arange(HEAD // 2, dtype=np.float32) * 2.0 / HEAD))
    angle = np.arange(row, dtype=np.float32)[:, None] * freq[None, :].astype(np.float32)
    cosine, sine = np.cos(angle), np.sin(angle)
    table = jnp.asarray(np.concatenate([cosine] * 4 + [-sine, sine, -sine, sine], axis=1).astype(np.float32))

    mixed, small, normed, query, key, value, weight = kernel_call(
        attend_kernel, 8, [ends], [got], [table],
        [((row, 128), BF16), ((48, width), BF16)],
        [((row, width), BF16)] + [((row, 128), BF16)] * 3 + [((width, 256), BF16)],
        [keep(row, width)] + [keep(row, 128)] * 3 + [keep(width, 256), arrivals(5)]
        + [keep(row, 256, kind=F32), arrivals()],
    )
    mixed_rows, packed_other = together(exchange(mixed.reshape(ctx, share, 128), CTX), packed_other)
    weights_other = lax.all_gather(packed_other, "y", axis=0, tiled=True)
    mixed, *out_blocks = together(mixed, *out_blocks)
    out_own = jnp.stack(out_blocks)
    out_other = pass_on(out_own, "core", 1)
    middle, gates, mixed_rows, tokens = kernel_call(
        route_kernel, 4, [members], [mixed_rows, out_own, out_other, hidden[0], small, grad_rows], [],
        [((share, width), F32), ((share, 128), F32), ((share, width), BF16)], [((chips, share, wide), BF16)],
        [keep(share, wide), keep(share, width, kind=F32), arrivals(8)],
    )
    tokens, grads = together(tokens, grads)
    grads_far = pass_on(grads, "core", 1)
    (pick,) = kernel_call(
        pick_kernel, 0, [expert, chip_places], [], [grads, grads_far], [((peers, 2 * SLOTS, share), BF16)], [],
        [keep(peers, share, SIDE), arrivals(16)],
    )
    tokens_near, pick = together(exchange(tokens, CHIP), pick)
    tokens_far = pass_on(tokens_near, "core", 1)

    total = chips * SLOTS

    common = (expert, zl_index, chip_places, pick)
    back_near, *near = experts_call(0, *common, tokens_near, grads, weights_own, weights_other)
    *near, tokens_far = together(*near, tokens_far)
    route_far, *far = experts_call(1, *common, tokens_far, grads_far, weights_own, weights_other)
    route_passed = pass_on(route_far, "core", 1)
    (route_sums,) = kernel_call(
        join_kernel, 0, [], [pick], [back_near, route_passed], [], [((chips, share, wide), BF16)],
        [keep(chips, 2 * SLOTS, wide), keep(chips, share, wide), keep(chips, share, wide), arrivals(2, 8), arrivals(8)],
        limit=16,
    )
    grads_other = grads_call(1, zl_index, near, far, route_sums)
    sums_other = lax.psum_scatter(grads_other, "y", scatter_dimension=0, tiled=True)
    out_far = kernel_call(
        functools.partial(outputs_kernel, 1), 0, [chip_places], [pick], [far[4], route_sums],
        [], [((2, share, width), BF16)] * 4,
        [keep(2, total, width), keep(chips, share, width), arrivals(9), arrivals(8)],
    )
    grads_own = grads_call(0, zl_index, near, far, route_sums)
    out_sums = kernel_call(
        functools.partial(outputs_kernel, 0), 0, [chip_places], [pick],
        [near[4], *[pass_on(block, "core", 1) for block in out_far], route_sums], [], [((2, share, width), BF16)] * 4,
        [keep(chips, share, width), keep(2, total, width), keep(chips, share, width), arrivals(9), arrivals(8)],
    )
    route_sums, grads_own, *out_sums = together(exchange(route_sums, CHIP), grads_own, *out_sums)
    sums_own = lax.psum_scatter(grads_own, "y", scatter_dimension=0, tiled=True)

    d_mixed, early_mine, early_others, d_middle = kernel_call(
        unroute_kernel, 4, [members], [],
        [route_sums, middle, gates, grad_rows, tokens, small, out_own, out_other, mixed_rows],
        [((ctx, share, 128), BF16)] + [((row, half + 128), BF16)] * 2 + [((share, width), F32)], [],
        [keep(share, width, kind=F32), keep(share, 128, kind=F32), keep(share, wide), keep(share, wide)]
        + [keep(48, width), keep(4, ctx, 128, 128), keep(4, ctx, 128, 128), keep(share, width), arrivals(8)]
        + [keep(chips, share, wide), arrivals(8), keep(share, width)],
    )
    early_passed = pass_on(early_others, "core", 1)
    out_blocks = ring_blocks_out(out_sums, "x")
    d_mixed, early_passed = together(exchange(d_mixed, CTX), early_passed)
    (early,) = kernel_call(
        add_kernel, 0, [], [early_mine, early_passed], [], [((row, 640), BF16)], [], [], limit=16,
    )
    early, d_mixed = together(early, d_mixed)
    d_mixed = d_mixed.reshape(row, 128)
    passed = pass_on(sums_other, "zl", 1)
    late_mine, late_others, *d_normed_part = kernel_call(
        attend_back_kernel, 11, [ends, ctx_places, core_index], [d_mixed],
        [query, key, value, table, normed, weight, early],
        [((row, 128), BF16)] * 2, [((2, share, width), BF16)] * 4,
        [keep(row, 128, kind=F32), keep(row, 128, kind=F32), keep(row, 256), keep(width, 256, kind=F32)]
        + [keep(4, 2, share, width), arrivals(4, 2)]
        + [keep(row, 128)] * 3 + [keep(row, 256, kind=F32), keep(row, width), keep(width, 256), arrivals(6)],
    )

    early = exchange(early.reshape(ctx * chips, 16, 640), CTX + CHIP)
    late_passed = pass_on(late_others, "core", 1)
    (late,) = kernel_call(
        late_kernel, 0, [], [late_mine, late_passed], [early, *out_blocks[1:]], [((row, 128), BF16)], [], [], limit=16,
    )
    late = exchange(late.reshape(ctx * chips, 16, 128), CTX + CHIP)
    out_sums, out_other = kernel_call(
        add_four_kernel, 0, [], out_blocks[1:], [out_blocks[0]], [((share, width), BF16)] * 2, [],
        [keep(2, share, width), arrivals()], limit=16,
    )
    (output,) = kernel_call(
        output_kernel, 0, [], [out_sums, pass_on(out_other, "zh", 1), middle], [],
        [((share, width), BF16)], [], [], limit=16,
    )
    d_normed_blocks = ring_blocks_out(d_normed_part, "y")
    d_normed_near, d_normed_other = kernel_call(
        add_four_kernel, 0, [], d_normed_blocks[1:], [d_normed_part[0]], [((share, width), BF16)] * 2, [],
        [keep(2, share, width), arrivals()], limit=16,
    )
    gate_sum, up_sum, down_sum = kernel_call(
        expert_sums_kernel, 0, [], [sums_own, passed], [],
        [((local, 128, deep), F32)] * 2 + [((local, deep, 128), F32)], [], [], limit=16,
    )
    (sums,) = kernel_call(
        reduce_kernel, 0, [], [early, late], [d_normed_near, gate_sum, output], [((peers, 16, 1664), BF16)], [], [keep(16, 1664)], limit=16,
    )
    (hidden_grad,) = kernel_call(
        hidden_grad_kernel, 0, [],
        [d_normed_near, pass_on(d_normed_other, "zl", 1), d_middle, hidden[0], small], [],
        [((share, width), F32)], [], [], limit=16,
    )
    sums, gate_sum, up_sum, down_sum, hidden_grad, output = together(
        exchange(sums, EP), gate_sum, up_sum, down_sum, hidden_grad, output
    )
    query_grad, key_grad, value_grad, out_weight_grad, attn_gain_grad, moe_gain_grad, router_grad = kernel_call(
        finish_kernel, 3, [], [sums, w_query, key_projection, w_value, attn_gain[None]], [],
        [((128, width), F32), ((128, half), F32), ((128, half), F32), ((128, width), F32)]
        + [((1, 128), F32), ((1, 128), F32), ((EXPERTS, 128), F32)], [], [], limit=16,
    )
    return (
        output[None], hidden_grad[None], attn_gain_grad[0], query_grad, key_grad, value_grad,
        out_weight_grad, moe_gain_grad[0], router_grad, gate_sum, up_sum, down_sum,
    )


def solution(mesh):
    axes = ("zl", "y", "zh", "x", "core")
    inner = Mesh(mesh.devices.reshape(2, 4, 2, 4, 2), axes)
    in_specs = (
        P(EP, CTX, None), P(EP, None), P(EP, CTX, None), P(CTX), P(CTX, None), P(CTX, None),
        P(CTX, None), P(CTX, None), P(CTX), P(None, CTX), P(EP, CTX, None), P(EP, CTX, None),
        P(EP, None, CTX), P(EP, CTX, None),
    )
    out_specs = (
        P(EP, CTX, None), P(EP, CTX, None), P(CTX), P(CTX, None), P(CTX, None), P(CTX, None),
        P(CTX, None), P(CTX), P(None, CTX), P(EP, CTX, None), P(EP, CTX, None), P(EP, None, CTX),
    )
    return jax.shard_map(on_device, mesh=inner, in_specs=in_specs, out_specs=out_specs, check_vma=False)
```

```python
import functools

import jax
import jax.numpy as jnp
import numpy as np
from jax import lax
from jax.experimental import pallas as pl
from jax.experimental.pallas import tpu as pltpu
from jax.sharding import Mesh, PartitionSpec as P

EPS = 1e-05
THETA = 10000.0
MASKED = -1e30
HEAD = 64
SCALE = 0.125
TILE = 256
SLOTS = 48
EXPERTS = 32
F32 = jnp.float32
BF16 = jnp.bfloat16
CTX = ("zl", "y")
CHIP = ("zh", "x")
EP = ("zh", "x", "core")
SIDE = 128
NT = (((1,), (1,)), ((), ()))
TN = (((0,), (0,)), ((), ()))
STEPS = (0, -1, 1, 2)


def exchange(parts, axis):
    return lax.all_to_all(parts, axis, split_axis=0, concat_axis=0, tiled=True)


def spread(block, axis, count):
    return exchange(jnp.broadcast_to(block[None], (count,) + block.shape), axis)


def pass_on(block, axis, steps):
    size = lax.axis_size(axis)
    return lax.ppermute(block, axis, [(i, (i + steps) % size) for i in range(size)])


def together(*values):
    return lax.optimization_barrier(values)


def ring_blocks(block, ring):
    return [block] + [pass_on(block, ring, -steps) for steps in STEPS[1:]]


def ring_blocks_out(blocks, ring):
    return [blocks[0]] + [pass_on(block, ring, steps) for block, steps in zip(blocks[1:], STEPS[1:])]


def dot(left, right, dims=(((1,), (0,)), ((), ()))):
    return lax.dot_general(left, right, dims, preferred_element_type=F32)


def turn(block, cosine, sine):
    lane = lax.broadcasted_iota(jnp.int32, block.shape, 1)
    other = jnp.where(lane % HEAD < HEAD // 2, pltpu.roll(block, 96, 1), pltpu.roll(block, 32, 1))
    return block * cosine + other * sine


def pack_kernel(
    member_ref, query_ref, key_ref, value_ref, router_ref, gain_a_ref, gain_m_ref, hidden_ref, out_ref, sent_ref
):
    out_part = out_ref[:, pl.ds(pl.multiple_of(member_ref[0] * 128, 128), 128)]
    share = hidden_ref.shape[0]
    lane = lax.broadcasted_iota(jnp.int32, (share, 128), 1)
    row = lax.broadcasted_iota(jnp.int32, (16, 128), 0)
    gains = jnp.where(row == 0, gain_a_ref[...].astype(F32), 0.0)
    gains = jnp.where(row == 1, gain_m_ref[...].astype(F32), gains).astype(BF16)
    for peer in range(8):
        sent_ref[peer, :128, :] = query_ref[:, peer * 128 : (peer + 1) * 128]
        columns = slice(peer // 2 * 128, (peer // 2 + 1) * 128)
        key, value = key_ref[:, columns].astype(F32), value_ref[:, columns].astype(F32)
        if peer % 2 == 0:
            value = pltpu.roll(value, HEAD, 1)
        else:
            key = pltpu.roll(key, HEAD, 1)
        sent_ref[peer, 128:256, :] = jnp.where(lane < HEAD, key, value).astype(BF16)
        sent_ref[peer, 256:288, :] = router_ref[...]
        sent_ref[peer, 288:304, :] = gains
        for block in range(8):
            start = 304 + block * share
            sent_ref[peer, start : start + share, :] = hidden_ref[:, block * 128 : (block + 1) * 128]
        sent_ref[peer, 304 + 8 * share :, :] = out_part


def expert_sums_kernel(own_ref, passed_ref, gate_ref, up_ref, down_ref):
    deep = gate_ref.shape[2]
    for e in range(2):
        for place, target in enumerate((gate_ref, up_ref, down_ref)):
            columns = slice((e * 3 + place) * deep, (e * 3 + place + 1) * deep)
            sums = own_ref[:, columns].astype(F32) + passed_ref[:, columns].astype(F32)
            target[e] = sums.T if place == 2 else sums


def document_start(ends_ref, place):
    start = jnp.zeros_like(place)
    for document in range(3):
        end = ends_ref[document]
        start = jnp.where(place >= end, end, start)
    return start


def attend_kernel(
    ends_ref, got_ref, angles_ref,
    mixed_ref, small_ref, *refs,
):
    outside, kept, sent, table_ref, arrived = refs[:5], refs[5:10], refs[10], refs[11], refs[12]
    fetch = pltpu.make_async_copy(angles_ref, table_ref, arrived)
    fetch.start()
    normed_ref, query_ref, key_ref, value_ref, weight_ref = kept
    moves = [pltpu.make_async_copy(kept[n], outside[n], sent.at[n]) for n in range(5)]
    count = normed_ref.shape[0]
    share = count // 8
    for block in range(8):
        rows = slice(block * 128, (block + 1) * 128)
        weight_ref[rows, :128] = got_ref[block, :128, :]
        weight_ref[rows, 128:] = got_ref[block, 128:256, :]
        small_ref[:, rows] = got_ref[block, 256:304, :]
    moves[4].start()
    fetch.wait()
    gain = small_ref[32:33, :].astype(F32)
    lane = lax.broadcasted_iota(jnp.int32, (share, 128), 1)
    low = lane < HEAD
    for piece in range(8):
        rows = slice(piece * share, (piece + 1) * share)
        x = jnp.concatenate(
            [got_ref[piece, 304 + block * share : 304 + (block + 1) * share, :] for block in range(8)], axis=1
        ).astype(F32)
        rho = lax.rsqrt(jnp.mean(x * x, axis=-1, keepdims=True) + EPS)
        normed = (x * rho * gain).astype(BF16)
        normed_ref[rows, :] = normed
        projected = dot(normed, weight_ref[...])
        cosine, sine = table_ref[rows, :128], table_ref[rows, 128:]
        pair = projected[:, 128:]
        turned = pltpu.roll(pair, HEAD, 1)
        query_ref[rows, :] = turn(projected[:, :128], cosine, sine).astype(BF16)
        key_ref[rows, :] = turn(jnp.where(low, pair, turned), cosine, sine).astype(BF16)
        value_ref[rows, :] = jnp.where(low, turned, pair).astype(BF16)
    for move in moves[:4]:
        move.start()
    lane = lax.broadcasted_iota(jnp.int32, (TILE, 128), 1)
    low = lane < HEAD
    for tile in range(count // TILE):
        rows = slice(tile * TILE, (tile + 1) * TILE)
        seen = (tile + 1) * TILE
        keys, values = key_ref[:seen, :], value_ref[:seen, :]
        place = tile * TILE + lax.broadcasted_iota(jnp.int32, (TILE, seen), 0)
        source = lax.broadcasted_iota(jnp.int32, (TILE, seen), 1)
        start = document_start(ends_ref, tile * TILE + lax.broadcasted_iota(jnp.int32, (TILE, 1), 0))
        allowed = (source <= place) & (source >= start)
        scaled = query_ref[rows, :] * jnp.asarray(SCALE, BF16)
        mixed = []
        for head in range(2):
            one = jnp.where(low == (head == 0), scaled, jnp.zeros_like(scaled))
            scores = jnp.where(allowed, dot(one, keys, NT), MASKED)
            weight = jnp.exp(scores - jnp.max(scores, axis=1, keepdims=True))
            probs = weight * (1.0 / jnp.sum(weight, axis=1, keepdims=True))
            mixed.append(dot(probs.astype(BF16), values))
        mixed_ref[rows, :] = jnp.where(low, mixed[0], mixed[1]).astype(BF16)
    for move in moves:
        move.wait()


def attend_back_kernel(
    ends_ref, index_ref, core_ref, d_mixed_ref, *refs,
):
    outside, (mine_ref, others_ref), d_normed_out = refs[:6], refs[7:9], refs[9:13]
    key_sum, value_sum, pre_ref, grad_ref, d_normed_ref, left = refs[13:19]
    inside, arrived = refs[19:25], refs[25]
    query_ref, key_ref, value_ref, table_ref, normed_ref, weight_ref = inside
    moves = [pltpu.make_async_copy(outside[n], inside[n], arrived.at[n]) for n in range(6)]
    for move in moves:
        move.start()
    count = query_ref.shape[0]
    lane = lax.broadcasted_iota(jnp.int32, (TILE, 128), 1)
    low = lane < HEAD
    key_sum[...] = jnp.zeros_like(key_sum)
    value_sum[...] = jnp.zeros_like(value_sum)
    for move in moves[:4]:
        move.wait()
    for tile in range(count // TILE):
        rows = slice(tile * TILE, (tile + 1) * TILE)
        seen = (tile + 1) * TILE
        keys, values = key_ref[:seen, :], value_ref[:seen, :]
        place = tile * TILE + lax.broadcasted_iota(jnp.int32, (seen, TILE), 1)
        source = lax.broadcasted_iota(jnp.int32, (seen, TILE), 0)
        start = document_start(ends_ref, tile * TILE + lax.broadcasted_iota(jnp.int32, (1, TILE), 1))
        allowed = (source <= place) & (source >= start)
        scaled = query_ref[rows, :] * jnp.asarray(SCALE, BF16)
        d_mixed = d_mixed_ref[rows, :]
        d_query = []
        for head in range(2):
            mine = low == (head == 0)
            one = jnp.where(mine, scaled, jnp.zeros_like(scaled))
            d_one = jnp.where(mine, d_mixed, jnp.zeros_like(d_mixed))
            scores = jnp.where(allowed, dot(keys, one, NT), MASKED)
            weight = jnp.exp(scores - jnp.max(scores, axis=0, keepdims=True))
            probs = weight * (1.0 / jnp.sum(weight, axis=0, keepdims=True))
            d_probs = dot(values, d_one, NT)
            delta = jnp.sum(probs * d_probs, axis=0, keepdims=True)
            d_scores = (probs * (d_probs - delta)).astype(BF16)
            key_sum[:seen, :] += dot(d_scores, one)
            value_sum[:seen, :] += dot(probs.astype(BF16), d_one)
            d_query.append(dot(d_scores, keys, TN) * SCALE)
        d_query = jnp.where(low, d_query[0], d_query[1])
        pre_ref[rows, :128] = turn(d_query, table_ref[rows, :128], -table_ref[rows, 128:]).astype(BF16)
    for tile in range(count // TILE):
        rows = slice(tile * TILE, (tile + 1) * TILE)
        d_key, d_value = key_sum[rows, :], value_sum[rows, :]
        d_key = turn(d_key + pltpu.roll(d_key, HEAD, 1), table_ref[rows, :128], -table_ref[rows, 128:])
        d_value = d_value + pltpu.roll(d_value, HEAD, 1)
        pre_ref[rows, 128:] = jnp.where(low, d_key, d_value).astype(BF16)
    moves[4].wait()
    moves[5].wait()
    share = d_normed_ref.shape[2]
    leaving = []
    for piece in (4, 5, 6, 7, 0, 1, 2, 3):
        rows = pl.ds(pl.multiple_of(index_ref[piece] * share, share), share)
        pair, place = piece // 4, piece % 4
        d_normed_ref[place, pair] = dot(pre_ref[rows, :], weight_ref[...], NT).astype(BF16)
        leaving.append(
            pltpu.make_async_copy(d_normed_ref.at[place, pair], d_normed_out[place].at[pair], left.at[place, pair])
        )
        leaving[-1].start()
    grad_ref[...] = dot(normed_ref[...], pre_ref[...], TN)
    for number, target in enumerate((mine_ref, others_ref)):
        member = (core_ref[0] + number) % 2
        for block in range(count // 16):
            rows = grad_ref[pl.ds(pl.multiple_of(block * 16 + member * 8, 8), 8), :]
            rows = jnp.concatenate([rows[:, :128], rows[:, 128:]], axis=0)
            target[block * 16 : (block + 1) * 16, :] = rows.astype(BF16)
    for move in leaving:
        move.wait()


def router_rows(small_ref):
    rows = small_ref[:EXPERTS, :]
    return jnp.concatenate([rows, jnp.zeros((128 - EXPERTS, rows.shape[1]), BF16)], axis=0)


def route_kernel(
    member_ref, mixed_ref, own_ref, other_ref, hidden_ref, small_ref, grad_ref,
    middle_ref, gates_ref, mixed_rows, tokens_out, token_ref, branch_ref, left,
):
    width = hidden_ref.shape[1]
    for block in range(8):
        mixed_rows[:, block * 128 : (block + 1) * 128] = mixed_ref[block]
    for place in range(8):
        columns = pl.ds(pl.multiple_of(member_ref[place] * 128, 128), 128)
        weight = (own_ref if place < 4 else other_ref)[place % 4].reshape(width, 128)
        branch_ref[:, columns] = dot(mixed_rows[...], weight)
    middle = hidden_ref[...].astype(F32) + branch_ref[...]
    middle_ref[...] = middle
    rho = lax.rsqrt(jnp.mean(middle * middle, axis=-1, keepdims=True) + EPS)
    routed = (middle * rho * small_ref[33:34, :].astype(F32)).astype(BF16)
    token_ref[:, :width] = routed
    logits = dot(routed, router_rows(small_ref), NT)
    logits = jnp.where(grad_ref[:, width:].astype(F32) > 0.5, logits, MASKED)
    raised = jnp.exp(logits - jnp.max(logits, axis=1, keepdims=True))
    gates = raised / jnp.sum(raised, axis=1, keepdims=True)
    gates_ref[...] = gates
    high = gates.astype(BF16).astype(F32)
    rest = gates - high
    middle_part = rest.astype(BF16).astype(F32)
    last = (rest - middle_part).astype(BF16).astype(F32)
    tail = high + pltpu.roll(middle_part, EXPERTS, 1) + pltpu.roll(last, 2 * EXPERTS, 1)
    token_ref[:, width:] = tail.astype(BF16)
    leaving = [pltpu.make_async_copy(token_ref, tokens_out.at[chip], left.at[chip]) for chip in range(8)]
    for move in leaving:
        move.start()
    for move in leaving:
        move.wait()


def unroute_kernel(
    member_ref, home_out, *refs,
):
    outside, (d_mixed_ref, mine_ref, others_ref, d_middle_ref) = refs[:8], refs[8:12]
    inside, arrived, home_ref, home_arrived, branch_ref = refs[12:20], *refs[20:24]
    middle_ref, gates_ref, grad_ref, token_ref, small_ref, own_ref, other_ref, mixed_ref = inside
    sources = [home_out.at[source] for source in range(8)]
    homes = [pltpu.make_async_copy(sources[n], home_ref.at[n], home_arrived.at[n]) for n in range(8)]
    moves = []
    for n in range(8):
        source = outside[n].at[0] if n == 3 else outside[n]
        moves.append(pltpu.make_async_copy(source, inside[n], arrived.at[n]))
    for move in homes + moves:
        move.start()
    width = middle_ref.shape[1]
    homes[0].wait()
    total = home_ref[0].astype(F32)
    for source in range(1, 8):
        homes[source].wait()
        total += home_ref[source].astype(F32)
    for move in moves[:5]:
        move.wait()
    tail = total[:, width:]
    lane = lax.broadcasted_iota(jnp.int32, tail.shape, 1)
    d_gates = jnp.where(lane < EXPERTS, tail + pltpu.roll(tail, 128 - EXPERTS, 1), 0.0)
    gates = gates_ref[...]
    d_logits = (gates * (d_gates - jnp.sum(gates * d_gates, axis=1, keepdims=True))).astype(BF16)
    d_routed = total[:, :width] + dot(d_logits, router_rows(small_ref))
    middle = middle_ref[...]
    rho = lax.rsqrt(jnp.mean(middle * middle, axis=-1, keepdims=True) + EPS)
    unit = middle * rho
    gain_part = jnp.sum(d_routed * unit, axis=0, keepdims=True)
    c = d_routed * small_ref[33:34, :].astype(F32)
    d_middle = grad_ref[:, :width].astype(F32) + rho * (c - unit * jnp.mean(c * unit, axis=-1, keepdims=True))
    d_middle_ref[...] = d_middle
    branch_ref[...] = d_middle.astype(BF16)
    for move in moves[5:]:
        move.wait()
    d_mixed = jnp.zeros((branch_ref.shape[0], width), F32)
    for place in range(8):
        columns = pl.ds(pl.multiple_of(member_ref[place] * 128, 128), 128)
        weight = (own_ref if place < 4 else other_ref)[place % 4].reshape(width, 128)
        d_mixed += dot(branch_ref[:, columns], weight, NT)
    d_mixed = d_mixed.astype(BF16)
    for block in range(8):
        d_mixed_ref[block] = d_mixed[:, block * 128 : (block + 1) * 128]
    router_part = dot(d_logits, token_ref[:, :width], TN)[:EXPERTS].astype(BF16)
    gain_rows = jnp.where(lax.broadcasted_iota(jnp.int32, (16, width), 0) == 0, gain_part, 0.0).astype(BF16)
    small_rows = jnp.concatenate([router_part, gain_rows], axis=0)
    row = lax.broadcasted_iota(jnp.int32, (128, 48), 0)
    column = lax.broadcasted_iota(jnp.int32, (128, 48), 1)
    for number, target in enumerate((mine_ref, others_ref)):
        member = (member_ref[0] + number) % 2
        half = pl.ds(pl.multiple_of(member * (width // 2), width // 2), width // 2)
        target[:, : width // 2] = dot(mixed_ref[...], branch_ref[:, half], TN).astype(BF16)
        place = row % 16
        wanted = jnp.where(place == 2, EXPERTS, jnp.where(place < 2, row // 16 * 4 + member * 2 + place, -1))
        choose = (wanted == column).astype(F32).astype(BF16)
        for block in range(8):
            rows = slice(block * 128, (block + 1) * 128)
            target[rows, width // 2 :] = dot(choose, small_rows[:, rows]).astype(BF16)


def add_kernel(mine_ref, passed_ref, sum_ref):
    sum_ref[...] = (mine_ref[...].astype(F32) + passed_ref[...].astype(F32)).astype(BF16)


def late_kernel(mine_ref, passed_ref, *refs):
    add_kernel(mine_ref, passed_ref, refs[-1])


def add_four_kernel(a_ref, b_ref, c_ref, part_out, sum_ref, other_ref, part_ref, arrived):
    move = pltpu.make_async_copy(part_out, part_ref, arrived)
    move.start()
    total = a_ref[...].astype(F32) + b_ref[...].astype(F32) + c_ref[...].astype(F32)
    move.wait()
    total = (total + part_ref[...].astype(F32)).astype(BF16)
    sum_ref[...] = total[0]
    other_ref[...] = total[1]


def hidden_grad_kernel(near_ref, passed_ref, d_middle_ref, hidden_ref, small_ref, grad_ref):
    x = hidden_ref[...].astype(F32)
    rho = lax.rsqrt(jnp.mean(x * x, axis=-1, keepdims=True) + EPS)
    unit = x * rho
    d_normed = near_ref[...].astype(F32) + passed_ref[...].astype(F32)
    c = d_normed * small_ref[32:33, :].astype(F32)
    grad_ref[...] = d_middle_ref[...] + rho * (c - unit * jnp.mean(c * unit, axis=-1, keepdims=True))


def output_kernel(near_ref, passed_ref, middle_ref, before_ref, output_ref):
    total = middle_ref[...] + near_ref[...].astype(F32) + passed_ref[...].astype(F32)
    output_ref[...] = total.astype(BF16)


def reduce_kernel(early_ref, late_ref, a_ref, b_ref, sums_ref, scratch):
    early = early_ref[0].astype(F32)
    for source in range(1, 64):
        early += early_ref[source].astype(F32)
    scratch[:, 1024:] = early.astype(BF16)
    for block in range(8):
        late = late_ref[block * 8].astype(F32)
        for source in range(1, 8):
            late += late_ref[block * 8 + source].astype(F32)
        scratch[:, block * 128 : (block + 1) * 128] = late.astype(BF16)
    for peer in range(16):
        sums_ref[peer] = scratch[...]


def finish_kernel(
    sums_ref, w_query_ref, w_key_ref, w_value_ref, gain_ref,
    query_ref, key_ref, value_ref, out_ref, gain_a_ref, gain_m_ref, router_ref,
):
    lane = lax.broadcasted_iota(jnp.int32, (8, 128), 1)
    low = lane < HEAD
    for peer in range(16):
        sums = sums_ref[peer].astype(F32)
        rows = slice(peer * 8, (peer + 1) * 8)
        query_ref[rows, :] = sums[:8, :1024]
        for pair in range(4):
            even = sums[8:, pair * 256 : pair * 256 + 128]
            odd = sums[8:, pair * 256 + 128 : (pair + 1) * 256]
            columns = slice(pair * 128, (pair + 1) * 128)
            key_ref[rows, columns] = jnp.where(low, even, pltpu.roll(odd, HEAD, 1))
            value_ref[rows, columns] = jnp.where(low, pltpu.roll(even, HEAD, 1), odd)
        columns = slice(peer % 2 * 512, (peer % 2 + 1) * 512)
        out_ref[peer // 2 * 16 : (peer // 2 + 1) * 16, columns] = sums[:, 1024:1536]
        router_ref[peer * 2 : peer * 2 + 2, :] = sums[0:2, 1536:]
        if peer == 0:
            gain_m_ref[...] = sums[2:3, 1536:]
    total = jnp.sum(w_query_ref[...].astype(F32) * query_ref[...], axis=1, keepdims=True)
    total += jnp.sum(w_key_ref[...].astype(F32) * key_ref[...], axis=1, keepdims=True)
    total += jnp.sum(w_value_ref[...].astype(F32) * value_ref[...], axis=1, keepdims=True)
    total = jnp.broadcast_to(total, (128, 128)).T
    gain_a_ref[...] = total[0:1, :] / gain_ref[...].astype(F32)


def pack_weights_kernel(gate_ref, up_ref, down_ref, before_ref, packed_ref):
    deep = gate_ref.shape[2]
    for e in range(2):
        base = e * 3 * deep
        packed_ref[:, base : base + deep] = gate_ref[e]
        packed_ref[:, base + deep : base + 2 * deep] = up_ref[e]
        packed_ref[:, base + 2 * deep : base + 3 * deep] = down_ref[e].T


def pair_kernel(mine_ref, beside_ref, before_ref, pair_ref):
    pair_ref[0] = mine_ref[...]
    pair_ref[1] = beside_ref[...]


def pick_kernel(expert_ref, place_ref, *refs):
    grads, pick_ref, flags_ref, arrived = refs[:2], *refs[2:]
    share = grads[0].shape[2]
    width = grads[0].shape[3] - 128
    fetches = []
    for piece in range(16):
        source = grads[piece // 8].at[place_ref[piece % 8] % 4, piece % 8 // 4, :, width:]
        fetches.append(pltpu.make_async_copy(source, flags_ref.at[piece], arrived.at[piece]))
        fetches[-1].start()
    row = lax.broadcasted_iota(jnp.int32, (16, 128), 0)
    lane = lax.broadcasted_iota(jnp.int32, (16, 128), 1)
    choose = ((lane == expert_ref[0] + row) & (row < 2)).astype(F32).astype(BF16)
    ahead = lax.broadcasted_iota(jnp.int32, (share, share), 0) < lax.broadcasted_iota(jnp.int32, (share, share), 1)
    ahead = ahead.astype(F32).astype(BF16)
    slot = lax.broadcasted_iota(jnp.int32, (SLOTS, share), 0).astype(F32)
    for fetch in fetches:
        fetch.wait()
    for piece in range(16):
        source = piece // 8 * 8 + place_ref[piece % 8]
        named = dot(choose, flags_ref[piece], NT)
        rank = dot(named.astype(BF16), ahead)
        for e in range(2):
            hit = (named[e : e + 1, :] > 0.5) & (rank[e : e + 1, :] == slot)
            pick_ref[source, e * SLOTS : (e + 1) * SLOTS, :] = hit.astype(F32).astype(BF16)


def experts_kernel(
    number, expert_ref, zl_ref, places_ref, pick_ref, tokens_out, grads_out, own_out, other_out,
    route_out, rows_out, d_result_out, inner_out, d_both_out, gated_out,
    route_ref, rows_ref, d_result_ref, inner_ref, d_both_ref, gated_ref,
    gate_ref, weight_ref, token_ref, grad_ref, back_ref, weight_here, token_here, grad_here, left, route_left,
):
    width = weight_ref.shape[1]
    part = width // 2
    deep = weight_ref.shape[2] // 3

    def token_move(source):
        token = tokens_out.at[places_ref[source]]
        return pltpu.make_async_copy(token, token_ref.at[source], token_here.at[source])

    def weight_move(e, place):
        block = (zl_ref[0] + place) % 2
        source = (own_out, other_out)[place].at[:, pl.ds(pl.multiple_of(e * 3 * deep, 3 * deep), 3 * deep)]
        target = weight_ref.at[e, pl.ds(pl.multiple_of(block * part, part), part), :]
        return pltpu.make_async_copy(source, target, weight_here.at[e, place])

    def leave(e, place):
        source, target = ((d_result_ref, d_result_out), (inner_ref, inner_out), (d_both_ref, d_both_out),
                          (gated_ref, gated_out), (rows_ref, rows_out))[place]
        return pltpu.make_async_copy(source.at[e], target.at[e], left.at[e, place])

    def route_leave(source):
        kept = route_ref if number == 1 else back_ref
        return pltpu.make_async_copy(kept.at[source], route_out.at[places_ref[source]], route_left.at[source])

    grads = []
    for source in range(8):
        grad = grads_out.at[places_ref[source] % 4, source // 4, :, :width]
        grads.append(pltpu.make_async_copy(grad, grad_ref.at[source], grad_here.at[source]))
    for source in range(8):
        token_move(source).start()
    for move in grads:
        move.start()
    for e in range(2):
        for place in range(2):
            weight_move(e, place).start()
    for move in grads:
        move.wait()
    lane = lax.broadcasted_iota(jnp.int32, (SLOTS, 128), 1)

    def gather(source, carry):
        token_move(source).wait()
        pick = pick_ref[number * 8 + places_ref[source]]
        rows = dot(pick, token_ref[source])
        cotangent = dot(pick, grad_ref[source])
        here = pl.ds(pl.multiple_of(source * SLOTS, SLOTS), SLOTS)
        for e in range(2):
            part = slice(e * SLOTS, (e + 1) * SLOTS)
            rows_ref[e, here, :] = rows[part, :width].astype(BF16)
            d_result_ref[e, here, :] = cotangent[part].astype(BF16)
            mine = (lane % EXPERTS == expert_ref[0] + e) & (lane < 3 * EXPERTS)
            gate = jnp.sum(jnp.where(mine, rows[part, width:], 0.0), axis=1, keepdims=True)
            gate_ref[e, here, :] = jnp.broadcast_to(gate, (SLOTS, 128))
        return carry

    lax.fori_loop(0, 8, gather, 0)
    lane = lax.broadcasted_iota(jnp.int32, (8 * SLOTS, 128), 1)

    def visit(e, carry):
        leave(e, 4).start()
        weight_move(e, 0).wait()
        weight_move(e, 1).wait()
        both = dot(rows_ref[e], weight_ref[e, :, : 2 * deep])
        a, b = both[:, :deep], both[:, deep:]
        sigma = 1.0 / (1.0 + jnp.exp(-a))
        inner = (a * sigma * b).astype(BF16)
        inner_ref[e] = inner
        down = weight_ref[e, :, 2 * deep :]
        result = dot(inner, down, NT).astype(BF16).astype(F32)
        gate = gate_ref[e, :, 0:1]
        cotangent = d_result_ref[e].astype(F32)
        gate_grad = jnp.sum(cotangent * result, axis=1, keepdims=True)
        gated_ref[e] = (gate * result).astype(BF16)
        d_result = (gate * cotangent).astype(BF16)
        d_result_ref[e] = d_result
        d_inner = dot(d_result, down)
        d_both_ref[e, :, :deep] = (d_inner * b * sigma * (1.0 + a * (1.0 - sigma))).astype(BF16)
        d_both_ref[e, :, deep:] = (d_inner * a * sigma).astype(BF16)
        for place in range(4):
            leave(e, place).start()
        d_rows = dot(d_both_ref[e], weight_ref[e, :, : 2 * deep], NT).astype(BF16)
        high = gate_grad.astype(BF16).astype(F32)
        low = gate_grad - high
        expert = expert_ref[0] + e
        tail = jnp.where(lane == expert, high, 0.0) + jnp.where(lane == expert + EXPERTS, low, 0.0)
        tail = tail.astype(BF16)
        here = pl.ds(pl.multiple_of(e * SLOTS, SLOTS), SLOTS)
        for source in range(8):
            part = slice(source * SLOTS, (source + 1) * SLOTS)
            back_ref[source, here, :width] = d_rows[part]
            back_ref[source, here, width:] = tail[part]
        return carry

    lax.fori_loop(0, 2, visit, 0)

    def scatter(source, carry):
        if number == 1:
            pick = pick_ref[8 + places_ref[source]]
            route_ref[source] = dot(pick, back_ref[source], TN).astype(BF16)
        route_leave(source).start()
        return carry

    lax.fori_loop(0, 8, scatter, 0)
    for e in range(2):
        for place in range(5):
            leave(e, place).wait()
    for source in range(8):
        route_leave(source).wait()


def join_kernel(pick_ref, back_out, passed_out, sum_out, back_ref, passed_ref, sum_ref, arrived, left):
    moves = []
    for source in range(8):
        moves.append(pltpu.make_async_copy(back_out.at[source], back_ref.at[source], arrived.at[0, source]))
        moves.append(pltpu.make_async_copy(passed_out.at[source], passed_ref.at[source], arrived.at[1, source]))
    for move in moves:
        move.start()
    leaving = []
    for source in range(8):
        moves[2 * source].wait()
        moves[2 * source + 1].wait()
        sums = dot(pick_ref[source], back_ref[source], TN)
        sum_ref[source] = (sums + passed_ref[source].astype(F32)).astype(BF16)
        leaving.append(pltpu.make_async_copy(sum_ref.at[source], sum_out.at[source], left.at[source]))
        leaving[-1].start()
    for move in leaving:
        move.wait()


def expert_grads_kernel(number, zl_ref, *refs):
    outside, grads_out, inside, grads_ref, arrived, left = refs[:8], refs[9], refs[10:18], *refs[18:21]
    deep = inside[2].shape[2]
    part = inside[0].shape[2]
    columns = pl.ds(pl.multiple_of((zl_ref[0] + number) % 2 * part, part), part)
    moves = []
    for e in range(2):
        for n in range(8):
            source = outside[n].at[e, :, columns] if n % 4 < 2 else outside[n].at[e]
            moves.append(pltpu.make_async_copy(source, inside[n].at[e], arrived.at[e, n]))
            moves[-1].start()
    halves = (inside[:4], inside[4:])
    leaving = []
    for e in range(2):
        base = e * 3 * deep
        for move in moves[8 * e : 8 * e + 8]:
            move.wait()
        both = sum(dot(rows[e], d_both[e], TN) for rows, d_result, inner, d_both in halves)
        grads_ref[:, base : base + 2 * deep] = both.astype(BF16)
        down = sum(dot(d_result[e], inner[e], TN) for rows, d_result, inner, d_both in halves)
        grads_ref[:, base + 2 * deep : base + 3 * deep] = down.astype(BF16)
        wide = slice(base, base + 3 * deep)
        leaving.append(pltpu.make_async_copy(grads_ref.at[:, wide], grads_out.at[:, wide], left.at[e]))
        leaving[-1].start()
    for move in leaving:
        move.wait()


def outputs_kernel(number, place_ref, pick_ref, *refs):
    gated_out, (gated_ref, sum_ref, arrived, left) = refs[0], refs[-4:]
    sums_out = refs[6:10] if number == 0 else refs[2:6]
    moves = [pltpu.make_async_copy(gated_out, gated_ref, arrived.at[8])]
    if number == 0:
        passed_out, passed_ref = refs[1:5], refs[10]
        for piece in range(8):
            source = passed_out[piece % 4].at[piece // 4]
            moves.append(pltpu.make_async_copy(source, passed_ref.at[piece], arrived.at[piece]))
    for move in moves:
        move.start()
    moves[0].wait()
    leaving = []
    for piece in range(8):
        here = slice(piece * SLOTS, (piece + 1) * SLOTS)
        both = jnp.concatenate([gated_ref[0, here, :], gated_ref[1, here, :]], axis=0)
        sums = dot(pick_ref[number * 8 + place_ref[piece]], both, TN)
        if number == 0:
            moves[1 + piece].wait()
            sums += passed_ref[piece].astype(F32)
        sum_ref[piece] = sums.astype(BF16)
        target = sums_out[piece % 4].at[piece // 4]
        leaving.append(pltpu.make_async_copy(sum_ref.at[piece], target, left.at[piece]))
        leaving[-1].start()
    for move in leaving:
        move.wait()


SMEM = pl.BlockSpec(memory_space=pltpu.SMEM)
VMEM = pl.BlockSpec(memory_space=pltpu.VMEM)
HBM = pl.BlockSpec(memory_space=pltpu.HBM)


def kernel_call(kernel, micros, scalars, arrays, outside, outs, outs_outside, scratch, limit=60):
    shapes = [jax.ShapeDtypeStruct(shape, kind) for shape, kind in (*outs, *outs_outside)]
    return pl.pallas_call(
        kernel,
        in_specs=[SMEM] * len(scalars) + [VMEM] * len(arrays) + [HBM] * len(outside),
        out_specs=[VMEM] * len(outs) + [HBM] * len(outs_outside),
        out_shape=shapes,
        scratch_shapes=scratch,
        compiler_params=pltpu.CompilerParams(vmem_limit_bytes=limit * 1024 * 1024),
        cost_estimate=pl.CostEstimate(flops=int(micros * 1.1e9) + 1, bytes_accessed=1, transcendentals=0),
    )(*scalars, *arrays, *outside)


def keep(*shape, kind=BF16):
    return pltpu.VMEM(shape, kind)


def arrivals(*shape):
    return pltpu.SemaphoreType.DMA(shape)


def experts_call(number, expert, zl_index, chip_places, pick, tokens, grads, weights_own, weights_other):
    chips, share, wide = tokens.shape
    width, total, deep = wide - SIDE, chips * SLOTS, weights_own.shape[1] // 6
    route = (chips, share, wide) if number == 1 else (chips, 2 * SLOTS, wide)
    shapes = [(2, total, width), (2, total, width), (2, total, deep), (2, total, 2 * deep), (2, total, width)]
    return kernel_call(
        functools.partial(experts_kernel, number), 0, [expert, zl_index, chip_places], [pick],
        [tokens, grads, weights_own, weights_other],
        [], [(shape, BF16) for shape in [route] + shapes],
        [keep(*shape) for shape in [route] + shapes]
        + [keep(2, total, 128, kind=F32), keep(2, width, 3 * deep), keep(chips, share, wide)]
        + [keep(chips, share, width), keep(chips, 2 * SLOTS, wide)]
        + [arrivals(2, 2), arrivals(8), arrivals(8), arrivals(2, 5), arrivals(8)],
    )


def grads_call(number, zl_index, near, far, before):
    two, total, width = near[0].shape
    half, deep = width // 2, near[2].shape[2]
    columns = [(2, total, half), (2, total, half), (2, total, deep), (2, total, 2 * deep)]
    return kernel_call(
        functools.partial(expert_grads_kernel, number), 0, [zl_index], [], [*near[:4], *far[:4], before],
        [], [((half, 6 * deep), BF16)],
        [keep(*shape) for shape in columns * 2] + [keep(half, 6 * deep), arrivals(2, 8), arrivals(2)],
    )[0]


def on_device(
    hidden, doc_lengths, expert_ids, attn_gain, w_query, key_projection, w_value, w_out,
    moe_gain, w_router, w_gate, w_up, w_down, out_grad,
):
    share, width = hidden.shape[1], hidden.shape[2]
    ctx, chips, peers = 8, 8, 16
    row = share * ctx
    wide, half = width + SIDE, width // 2
    local, deep = w_gate.shape[0], w_gate.shape[2]
    zl, y, zh, x, core = (lax.axis_index(name) for name in ("zl", "y", "zh", "x", "core"))
    expert = (((zh * 4 + x) * 2 + core) * local).astype(jnp.int32)[None]
    core_index = core.astype(jnp.int32)[None]
    zl_index = zl.astype(jnp.int32)[None]
    ctx_places = jnp.stack([(zl + d) % 2 * 4 + (y + s) % 4 for d in range(2) for s in STEPS]).astype(jnp.int32)
    chip_places = jnp.stack([(zh + d) % 2 * 4 + (x + s) % 4 for d in range(2) for s in STEPS]).astype(jnp.int32)
    members = [((x + s) % 4 * 2 + (core + d) % 2) for d in range(2) for s in STEPS]
    members = jnp.stack(members).astype(jnp.int32)

    lanes = jnp.arange(128, dtype=jnp.int32)
    chosen = jnp.any(expert_ids[0][:, :, None] == lanes[None, None, :], axis=1)
    grad_rows = jnp.concatenate([out_grad[0], chosen.astype(BF16)], axis=1)
    grad_beside = pass_on(grad_rows, "zh", 1)

    (sent,) = kernel_call(
        pack_kernel, 2, [members],
        [w_query, key_projection, w_value, w_router, attn_gain[None], moe_gain[None], hidden[0], w_out], [],
        [((ctx, 304 + 9 * share, 128), BF16)], [], [],
    )
    got = exchange(sent, CTX)
    (grad_pair,) = kernel_call(
        pair_kernel, 0, [], [grad_rows, grad_beside], [sent], [((2, share, wide), BF16)], [], [],
    )
    grads = lax.all_gather(grad_pair, "x", axis=0, tiled=False)

    (packed,) = kernel_call(
        pack_weights_kernel, 0, [], [w_gate, w_up, w_down], [sent], [((share, 6 * deep), BF16)], [], [],
    )
    weights_own = lax.all_gather(packed, "y", axis=0, tiled=True)
    packed_other = pass_on(packed, "zl", 1)
    out_blocks = ring_blocks(got[:, 304 + 8 * share :], "x")

    ends = jnp.cumsum(doc_lengths[0]).astype(jnp.int32)
    freq = THETA ** (-(np.arange(HEAD // 2, dtype=np.float32) * 2.0 / HEAD))
    angle = np.arange(row, dtype=np.float32)[:, None] * freq[None, :].astype(np.float32)
    cosine, sine = np.cos(angle), np.sin(angle)
    table = jnp.asarray(np.concatenate([cosine] * 4 + [-sine, sine, -sine, sine], axis=1).astype(np.float32))

    mixed, small, normed, query, key, value, weight = kernel_call(
        attend_kernel, 8, [ends], [got], [table],
        [((row, 128), BF16), ((48, width), BF16)],
        [((row, width), BF16)] + [((row, 128), BF16)] * 3 + [((width, 256), BF16)],
        [keep(row, width)] + [keep(row, 128)] * 3 + [keep(width, 256), arrivals(5)]
        + [keep(row, 256, kind=F32), arrivals()],
    )
    mixed_rows, packed_other = together(exchange(mixed.reshape(ctx, share, 128), CTX), packed_other)
    weights_other = lax.all_gather(packed_other, "y", axis=0, tiled=True)
    mixed, *out_blocks = together(mixed, *out_blocks)
    out_own = jnp.stack(out_blocks)
    out_other = pass_on(out_own, "core", 1)
    middle, gates, mixed_rows, tokens = kernel_call(
        route_kernel, 4, [members], [mixed_rows, out_own, out_other, hidden[0], small, grad_rows], [],
        [((share, width), F32), ((share, 128), F32), ((share, width), BF16)], [((chips, share, wide), BF16)],
        [keep(share, wide), keep(share, width, kind=F32), arrivals(8)],
    )
    tokens, grads = together(tokens, grads)
    grads_far = pass_on(grads, "core", 1)
    (pick,) = kernel_call(
        pick_kernel, 0, [expert, chip_places], [], [grads, grads_far], [((peers, 2 * SLOTS, share), BF16)], [],
        [keep(peers, share, SIDE), arrivals(16)],
    )
    tokens_near, pick = together(exchange(tokens, CHIP), pick)
    tokens_far = pass_on(tokens_near, "core", 1)

    total = chips * SLOTS

    common = (expert, zl_index, chip_places, pick)
    back_near, *near = experts_call(0, *common, tokens_near, grads, weights_own, weights_other)
    *near, tokens_far = together(*near, tokens_far)
    route_far, *far = experts_call(1, *common, tokens_far, grads_far, weights_own, weights_other)
    route_passed = pass_on(route_far, "core", 1)
    (route_sums,) = kernel_call(
        join_kernel, 0, [], [pick], [back_near, route_passed], [], [((chips, share, wide), BF16)],
        [keep(chips, 2 * SLOTS, wide), keep(chips, share, wide), keep(chips, share, wide), arrivals(2, 8), arrivals(8)],
        limit=16,
    )
    grads_other = grads_call(1, zl_index, near, far, route_sums)
    sums_other = lax.psum_scatter(grads_other, "y", scatter_dimension=0, tiled=True)
    out_far = kernel_call(
        functools.partial(outputs_kernel, 1), 0, [chip_places], [pick], [far[4], route_sums],
        [], [((2, share, width), BF16)] * 4,
        [keep(2, total, width), keep(chips, share, width), arrivals(9), arrivals(8)],
    )
    grads_own = grads_call(0, zl_index, near, far, route_sums)
    out_sums = kernel_call(
        functools.partial(outputs_kernel, 0), 0, [chip_places], [pick],
        [near[4], *[pass_on(block, "core", 1) for block in out_far], route_sums], [], [((2, share, width), BF16)] * 4,
        [keep(chips, share, width), keep(2, total, width), keep(chips, share, width), arrivals(9), arrivals(8)],
    )
    route_sums, grads_own, *out_sums = together(exchange(route_sums, CHIP), grads_own, *out_sums)
    sums_own = lax.psum_scatter(grads_own, "y", scatter_dimension=0, tiled=True)

    d_mixed, early_mine, early_others, d_middle = kernel_call(
        unroute_kernel, 4, [members], [],
        [route_sums, middle, gates, grad_rows, tokens, small, out_own, out_other, mixed_rows],
        [((ctx, share, 128), BF16)] + [((row, half + 128), BF16)] * 2 + [((share, width), F32)], [],
        [keep(share, width, kind=F32), keep(share, 128, kind=F32), keep(share, wide), keep(share, wide)]
        + [keep(48, width), keep(4, ctx, 128, 128), keep(4, ctx, 128, 128), keep(share, width), arrivals(8)]
        + [keep(chips, share, wide), arrivals(8), keep(share, width)],
    )
    early_passed = pass_on(early_others, "core", 1)
    out_blocks = ring_blocks_out(out_sums, "x")
    d_mixed, early_passed = together(exchange(d_mixed, CTX), early_passed)
    (early,) = kernel_call(
        add_kernel, 0, [], [early_mine, early_passed], [], [((row, 640), BF16)], [], [], limit=16,
    )
    early, d_mixed = together(early, d_mixed)
    d_mixed = d_mixed.reshape(row, 128)
    passed = pass_on(sums_other, "zl", 1)
    late_mine, late_others, *d_normed_part = kernel_call(
        attend_back_kernel, 11, [ends, ctx_places, core_index], [d_mixed],
        [query, key, value, table, normed, weight, early],
        [((row, 128), BF16)] * 2, [((2, share, width), BF16)] * 4,
        [keep(row, 128, kind=F32), keep(row, 128, kind=F32), keep(row, 256), keep(width, 256, kind=F32)]
        + [keep(4, 2, share, width), arrivals(4, 2)]
        + [keep(row, 128)] * 3 + [keep(row, 256, kind=F32), keep(row, width), keep(width, 256), arrivals(6)],
    )

    early = exchange(early.reshape(ctx * chips, 16, 640), CTX + CHIP)
    late_passed = pass_on(late_others, "core", 1)
    (late,) = kernel_call(
        late_kernel, 0, [], [late_mine, late_passed], [early, *out_blocks[1:]], [((row, 128), BF16)], [], [], limit=16,
    )
    late = exchange(late.reshape(ctx * chips, 16, 128), CTX + CHIP)
    out_sums, out_other = kernel_call(
        add_four_kernel, 0, [], out_blocks[1:], [out_blocks[0]], [((share, width), BF16)] * 2, [],
        [keep(2, share, width), arrivals()], limit=16,
    )
    gate_sum, up_sum, down_sum = kernel_call(
        expert_sums_kernel, 0, [], [sums_own, passed], [],
        [((local, 128, deep), F32)] * 2 + [((local, deep, 128), F32)], [], [], limit=16,
    )
    (output,) = kernel_call(
        output_kernel, 0, [], [out_sums, pass_on(out_other, "zh", 1), middle], [gate_sum],
        [((share, width), BF16)], [], [], limit=16,
    )
    d_normed_blocks = ring_blocks_out(d_normed_part, "y")
    d_normed_near, d_normed_other = kernel_call(
        add_four_kernel, 0, [], d_normed_blocks[1:], [d_normed_part[0]], [((share, width), BF16)] * 2, [],
        [keep(2, share, width), arrivals()], limit=16,
    )
    (sums,) = kernel_call(
        reduce_kernel, 0, [], [early, late], [d_normed_near, output], [((peers, 16, 1664), BF16)], [], [keep(16, 1664)], limit=16,
    )
    (hidden_grad,) = kernel_call(
        hidden_grad_kernel, 0, [],
        [d_normed_near, pass_on(d_normed_other, "zl", 1), d_middle, hidden[0], small], [],
        [((share, width), F32)], [], [], limit=16,
    )
    sums, gate_sum, up_sum, down_sum, hidden_grad, output = together(
        exchange(sums, EP), gate_sum, up_sum, down_sum, hidden_grad, output
    )
    query_grad, key_grad, value_grad, out_weight_grad, attn_gain_grad, moe_gain_grad, router_grad = kernel_call(
        finish_kernel, 3, [], [sums, w_query, key_projection, w_value, attn_gain[None]], [],
        [((128, width), F32), ((128, half), F32), ((128, half), F32), ((128, width), F32)]
        + [((1, 128), F32), ((1, 128), F32), ((EXPERTS, 128), F32)], [], [], limit=16,
    )
    return (
        output[None], hidden_grad[None], attn_gain_grad[0], query_grad, key_grad, value_grad,
        out_weight_grad, moe_gain_grad[0], router_grad, gate_sum, up_sum, down_sum,
    )


def solution(mesh):
    axes = ("zl", "y", "zh", "x", "core")
    inner = Mesh(mesh.devices.reshape(2, 4, 2, 4, 2), axes)
    in_specs = (
        P(EP, CTX, None), P(EP, None), P(EP, CTX, None), P(CTX), P(CTX, None), P(CTX, None),
        P(CTX, None), P(CTX, None), P(CTX), P(None, CTX), P(EP, CTX, None), P(EP, CTX, None),
        P(EP, None, CTX), P(EP, CTX, None),
    )
    out_specs = (
        P(EP, CTX, None), P(EP, CTX, None), P(CTX), P(CTX, None), P(CTX, None), P(CTX, None),
        P(CTX, None), P(CTX), P(None, CTX), P(EP, CTX, None), P(EP, CTX, None), P(EP, None, CTX),
    )
    return jax.shard_map(on_device, mesh=inner, in_specs=in_specs, out_specs=out_specs, check_vma=False)
```
